32 devices in a mesh: dp: 8 (over z, y), mp: 4 (over x, core).
Axes of the slice: x: 2, y: 2, z: 4, core: 2. Of those that a mesh axis runs over, the one named last changes fastest.
Arguments:
- clean_latent: float32 [16, 3, 1024], P('dp'), may hold values from -6 to 6
- noise_latent: float32 [16, 3, 1024], P('dp'), may hold values from -6 to 6
- timesteps: int32 [16], P('dp'), may hold values from 0 to 999
- labels: int32 [16], P('dp'), may hold values from 0 to 999
- image_sides: int32 [16], P('dp'), may hold values from 16 to 32, as said below
- w_square: float32 [5, 512, 512], P(None, 'dp', 'mp'), may hold values from -0.25 to 0.25
- mom_square: float32 [5, 512, 512], P(None, 'dp', 'mp'), may hold values from -0.0048828125 to 0.0048828125
- w_conv: float32 [9, 512, 512], P(None, 'dp', 'mp'), may hold values from -0.09375 to 0.09375
- mom_conv: float32 [9, 512, 512], P(None, 'dp', 'mp'), may hold values from -0.0048828125 to 0.0048828125
- w_qkv: float32 [512, 3, 512], P('dp', None, 'mp'), may hold values from -0.25 to 0.25
- mom_qkv: float32 [512, 3, 512], P('dp', None, 'mp'), may hold values from -0.0048828125 to 0.0048828125
- w_ffin: float32 [512, 2, 2048], P('dp', None, 'mp'), may hold values from -0.25 to 0.25
- mom_ffin: float32 [512, 2, 2048], P('dp', None, 'mp'), may hold values from -0.0048828125 to 0.0048828125
- w_ffout: float32 [2048, 512], P('dp', 'mp'), may hold values from -0.125 to 0.125
- mom_ffout: float32 [2048, 512], P('dp', 'mp'), may hold values from -0.0048828125 to 0.0048828125
- w_time_in: float32 [256, 1024], P('dp', 'mp'), may hold values from -0.5 to 0.5
- mom_time_in: float32 [256, 1024], P('dp', 'mp'), may hold values from -0.0048828125 to 0.0048828125
- w_time_out: float32 [1024, 512], P('dp', 'mp'), may hold values from -0.375 to 0.375
- mom_time_out: float32 [1024, 512], P('dp', 'mp'), may hold values from -0.0048828125 to 0.0048828125
- kron_stats: float32 [84, 128, 128], P('mp'), as said below
- class_table: float32 [1000, 512], P(None, 'mp'), may hold values from -6 to 6
- table_mean: float32 [1000, 512], P(None, 'mp'), may hold values from -0.0048828125 to 0.0048828125
- table_var: float32 [1000, 512], P(None, 'mp'), may hold values from 3.0517579e-06 to 1.2207031e-05
- conv_first: float32 [9, 3, 512], P(None, None, 'mp'), may hold values from -1.25 to 1.25
- first_mean: float32 [9, 3, 512], P(None, None, 'mp'), may hold values from -0.0048828125 to 0.0048828125
- first_var: float32 [9, 3, 512], P(None, None, 'mp'), may hold values from 3.0517579e-06 to 1.2207031e-05
- conv_last: float32 [9, 512, 3], P(None, 'mp'), may hold values from -0.25 to 0.25
- last_mean: float32 [9, 512, 3], P(None, 'mp'), may hold values from -0.046875 to 0.046875
- last_var: float32 [9, 512, 3], P(None, 'mp'), may hold values from 0.00030517578 to 0.0012207031
- norm_params: float32 [5, 2, 512], P(None, None, 'mp'), may hold values from 0.5 to 1.5
- norm_mean: float32 [5, 2, 512], P(None, None, 'mp'), may hold values from -0.0048828125 to 0.0048828125
- norm_var: float32 [5, 2, 512], P(None, None, 'mp'), may hold values from 0.0012207031 to 0.0048828125
Outputs:
- square_new: float32 [5, 512, 512], P(None, 'dp', 'mp')
- square_mom: float32 [5, 512, 512], P(None, 'dp', 'mp')
- conv_new: float32 [9, 512, 512], P(None, 'dp', 'mp')
- conv_mom: float32 [9, 512, 512], P(None, 'dp', 'mp')
- qkv_new: float32 [512, 3, 512], P('dp', None, 'mp')
- qkv_mom: float32 [512, 3, 512], P('dp', None, 'mp')
- ffin_new: float32 [512, 2, 2048], P('dp', None, 'mp')
- ffin_mom: float32 [512, 2, 2048], P('dp', None, 'mp')
- ffout_new: float32 [2048, 512], P('dp', 'mp')
- ffout_mom: float32 [2048, 512], P('dp', 'mp')
- time_in_new: float32 [256, 1024], P('dp', 'mp')
- time_in_mom: float32 [256, 1024], P('dp', 'mp')
- time_out_new: float32 [1024, 512], P('dp', 'mp')
- time_out_mom: float32 [1024, 512], P('dp', 'mp')
- stats_new: float32 [84, 128, 128], P('mp')
- table_new: float32 [1000, 512], P(None, 'mp')
- table_mean_new: float32 [1000, 512], P(None, 'mp')
- table_var_new: float32 [1000, 512], P(None, 'mp')
- first_new: float32 [9, 3, 512], P(None, None, 'mp')
- first_mean_new: float32 [9, 3, 512], P(None, None, 'mp')
- first_var_new: float32 [9, 3, 512], P(None, None, 'mp')
- last_new: float32 [9, 512, 3], P(None, 'mp')
- last_mean_new: float32 [9, 512, 3], P(None, 'mp')
- last_var_new: float32 [9, 512, 3], P(None, 'mp')
- norm_new: float32 [5, 2, 512], P(None, None, 'mp')
- norm_mean_new: float32 [5, 2, 512], P(None, None, 'mp')
- norm_var_new: float32 [5, 2, 512], P(None, None, 'mp')
- loss_terms: float32 [2, 4], replicated
The draws below stay inside these ranges and needn't reach their ends.
Inputs may be any that keep to these rules, and one draw needn't show every extreme that they name: `image_sides`: each image's side is 16, 24 or 32; the image fills the upper left square of that side in its slot. `kron_stats`: symmetric with a dominant positive diagonal.
All inputs are finite; a program needn't handle non-finite values.
Results may differ from the reference program's by a relative error of at most 0.004.
The reference program's roundings to bfloat16 on the way (of `noisy`, `res_input`, `queries`, `attended` and `last_in`) count: a program that leaves them out, or rounds other values in their place, can miss the bound.
Values may be sent and summed in bfloat16 or wider, within the bound.
A program may use at most 128 MiB of HBM per device.

```python
import math
import jax
import jax.numpy as jnp
from jax import lax

C = 512
GROUPS = 32
HEADS = 8
HD = 64
FFH = 2048
TE = 256
TD = 1024
NCLS = 1000
LAT = 3
SIDE = 32
IMG_DEV = 2
NBANDS = 4
NS_ITERS = 6
STEP = 5
NIMG = 16
GRP = 128
NBLK = 21
NSTAT = 84
N_MP = 4


def draw_image_sides(key, part):
    key = jax.random.fold_in(key, 11)
    positions = jnp.arange(NIMG)
    base_level = positions * 3 // NIMG
    offsets = jax.random.randint(key, (NIMG,), -1, 2)
    level = jnp.clip(base_level + offsets, 0, 2)
    level = level.at[0].set(0).at[NIMG - 1].set(2)
    return (SIDE // 2 + level * (SIDE // 4)).astype(jnp.int32)


def draw_kron_stats(key, part):
    key = jax.random.fold_in(key, 23)
    key_diag, key_off = jax.random.split(key)
    unit_size = 0.5 * C / (NIMG * SIDE * SIDE)
    diagonal = unit_size * jnp.exp(jax.random.uniform(key_diag, (NSTAT, GRP), jnp.float32, 0.0, 1.3862944))
    offdiag = jax.random.uniform(key_off, (NSTAT, GRP, GRP), jnp.float32, -0.4, 0.4) * unit_size / GRP
    offdiag = 0.5 * (offdiag + jnp.swapaxes(offdiag, 1, 2))
    identity = jnp.eye(GRP, dtype=jnp.float32)
    return offdiag * (1.0 - identity) + diagonal[:, :, None] * identity


def plant(values, key, smallest, high):
    place = [jax.random.randint(jax.random.fold_in(key, axis), (), 0, length) for axis, length in enumerate(values.shape)]
    longest = values.shape.index(max(values.shape))
    next_to = place[:longest] + [(place[longest] + 1) % values.shape[longest]] + place[longest + 1:]
    return values.at[tuple(place)].set(smallest).at[tuple(next_to)].set(high)


def level_of(key, shape, pieces, low, largest):
    def one(dim, shards_of):
        heights = jax.random.uniform(jax.random.fold_in(jax.random.fold_in(key, 6), dim), (shards_of,), jnp.float32, low / len(pieces), largest / len(pieces))
        return jnp.repeat(jnp.exp(heights), shape[dim] // shards_of).reshape((-1,) + (1,) * (len(shape) - dim - 1))

    level = one(*pieces[0])
    for cut in pieces[1:]:
        level = level * one(*cut)
    return level


def bell_draw(stream_key, dims, scale, bound, pieces=(), kind=jnp.bfloat16):
    values = jax.random.normal(stream_key, dims, jnp.float32) * scale
    if len(pieces) > 0:
        values = level_of(stream_key, dims, pieces, -0.22, 0.18) * values
    return jnp.clip(values, min=-bound, max=bound).astype(kind)


def setup_inputs(seed: int = 0) -> dict:
    keys = jax.random.split(jax.random.key(seed), 33)
    clean_latent = bell_draw(keys[0], (NIMG, LAT, SIDE * SIDE), 1.0, 6.0, ((0, 8),), jnp.float32)
    noise_latent = bell_draw(keys[1], (NIMG, LAT, SIDE * SIDE), 1.0, 6.0, ((0, 8),), jnp.float32)
    timesteps = plant(jax.random.randint(keys[2], (NIMG,), 0, 1000), jax.random.fold_in(keys[2], 1), 0, 999).astype(jnp.int32)
    labels = plant(jax.random.randint(keys[3], (NIMG,), 0, NCLS), jax.random.fold_in(keys[3], 1), 0, NCLS - 1).astype(jnp.int32)
    image_sides = draw_image_sides(jax.random.fold_in(keys[32], 71), 0)
    w_square = bell_draw(keys[5], (5, C, C), C ** -0.5, 0.25, ((1, 8), (2, 4)), jnp.float32)
    mom_square = bell_draw(keys[6], (5, C, C), ((100 * NIMG * SIDE * SIDE) ** -0.5), 0.0048828125, ((1, 8), (2, 4)), jnp.float32)
    w_conv = bell_draw(keys[7], (9, C, C), (9 * C) ** -0.5, 0.09375, ((1, 8), (2, 4)), jnp.float32)
    mom_conv = bell_draw(keys[8], (9, C, C), ((100 * NIMG * SIDE * SIDE) ** -0.5), 0.0048828125, ((1, 8), (2, 4)), jnp.float32)
    w_qkv = bell_draw(keys[9], (C, 3, C), C ** -0.5, 0.25, ((0, 8), (2, 4)), jnp.float32)
    mom_qkv = bell_draw(keys[10], (C, 3, C), ((100 * NIMG * SIDE * SIDE) ** -0.5), 0.0048828125, ((0, 8), (2, 4)), jnp.float32)
    w_ffin = bell_draw(keys[11], (C, 2, FFH), C ** -0.5, 0.25, ((0, 8), (2, 4)), jnp.float32)
    mom_ffin = bell_draw(keys[12], (C, 2, FFH), ((100 * NIMG * SIDE * SIDE) ** -0.5), 0.0048828125, ((0, 8), (2, 4)), jnp.float32)
    w_ffout = bell_draw(keys[13], (FFH, C), FFH ** -0.5, 0.125, ((0, 8), (1, 4)), jnp.float32)
    mom_ffout = bell_draw(keys[14], (FFH, C), ((100 * NIMG * SIDE * SIDE) ** -0.5), 0.0048828125, ((0, 8), (1, 4)), jnp.float32)
    w_time_in = bell_draw(keys[15], (TE, TD), (TE // 2) ** -0.5, 0.5, ((0, 8), (1, 4)), jnp.float32)
    mom_time_in = bell_draw(keys[16], (TE, TD), ((100 * NIMG * SIDE * SIDE) ** -0.5), 0.0048828125, ((0, 8), (1, 4)), jnp.float32)
    w_time_out = bell_draw(keys[17], (TD, C), (TD // 4) ** -0.5, 0.375, ((0, 8), (1, 4)), jnp.float32)
    mom_time_out = bell_draw(keys[18], (TD, C), ((100 * NIMG * SIDE * SIDE) ** -0.5), 0.0048828125, ((0, 8), (1, 4)), jnp.float32)
    kron_stats = draw_kron_stats(jax.random.fold_in(keys[32], 71), 0)
    class_table = bell_draw(keys[20], (NCLS, C), 1.0, 6.0, ((1, 4),), jnp.float32)
    table_mean = bell_draw(keys[21], (NCLS, C), (0.1 * (NIMG * SIDE * SIDE) ** -0.5), 0.0048828125, ((1, 4),), jnp.float32)
    table_var = jnp.clip(jnp.exp(math.log(1.220703143189894e-05) - 1.3862944 * jax.random.uniform(keys[22], (NCLS, C), jnp.float32) ** level_of(keys[22], (NCLS, C), ((1, 4),), -0.2, 0.2)), 3.051757857974735e-06, 1.220703143189894e-05)
    conv_first = bell_draw(keys[23], (9, LAT, C), (9 * LAT) ** -0.5, 1.25, ((2, 4),), jnp.float32)
    first_mean = bell_draw(keys[24], (9, LAT, C), (0.1 * (NIMG * SIDE * SIDE) ** -0.5), 0.0048828125, ((2, 4),), jnp.float32)
    first_var = jnp.clip(jnp.exp(math.log(1.220703143189894e-05) - 1.3862944 * jax.random.uniform(keys[25], (9, LAT, C), jnp.float32) ** level_of(keys[25], (9, LAT, C), ((2, 4),), -0.2, 0.2)), 3.051757857974735e-06, 1.220703143189894e-05)
    conv_last = bell_draw(keys[26], (9, C, LAT), (9 * C // 8) ** -0.5, 0.25, ((1, 4),), jnp.float32)
    last_mean = bell_draw(keys[27], (9, C, LAT), ((NIMG * SIDE * SIDE) ** -0.5), 0.046875, ((1, 4),), jnp.float32)
    last_var = jnp.clip(jnp.exp(math.log(0.0012207031) - 1.3862944 * jax.random.uniform(keys[28], (9, C, LAT), jnp.float32) ** level_of(keys[28], (9, C, LAT), ((1, 4),), -0.2, 0.2)), 0.00030517578, 0.0012207031)
    norm_params = jnp.clip(0.5 + 1.0 * jax.random.uniform(keys[29], (5, 2, C), jnp.float32) ** level_of(keys[29], (5, 2, C), ((2, 4),), -0.2, 0.2), 0.5, 1.5)
    norm_mean = bell_draw(keys[30], (5, 2, C), (0.1 * (NIMG * SIDE * SIDE) ** -0.5), 0.0048828125, ((2, 4),), jnp.float32)
    norm_var = jnp.clip(jnp.exp(math.log(0.0048828125) - 1.3862944 * jax.random.uniform(keys[31], (5, 2, C), jnp.float32) ** level_of(keys[31], (5, 2, C), ((2, 4),), -0.2, 0.2)), 0.0012207031, 0.0048828125)
    return {"clean_latent": clean_latent, "noise_latent": noise_latent, "timesteps": timesteps, "labels": labels, "image_sides": image_sides, "w_square": w_square, "mom_square": mom_square, "w_conv": w_conv, "mom_conv": mom_conv, "w_qkv": w_qkv, "mom_qkv": mom_qkv, "w_ffin": w_ffin, "mom_ffin": mom_ffin, "w_ffout": w_ffout, "mom_ffout": mom_ffout, "w_time_in": w_time_in, "mom_time_in": mom_time_in, "w_time_out": w_time_out, "mom_time_out": mom_time_out, "kron_stats": kron_stats, "class_table": class_table, "table_mean": table_mean, "table_var": table_var, "conv_first": conv_first, "first_mean": first_mean, "first_var": first_var, "conv_last": conv_last, "last_mean": last_mean, "last_var": last_var, "norm_params": norm_params, "norm_mean": norm_mean, "norm_var": norm_var}


@jax.custom_vjp
def low(v):
    return lax.optimization_barrier(v.astype(jnp.bfloat16)).astype(jnp.float32)

@jax.custom_vjp
def low_back(v):
    return v

def low_keep(v):
    return (low(v), None)

def low_pass(kept, grad):
    return (grad,)

def back_keep(v):
    return (v, None)

def back_low(kept, grad):
    return (low(grad),)
low.defvjp(low_keep, low_pass)
low_back.defvjp(back_keep, back_low)
highest = lax.Precision.HIGHEST
norm_eps = 1e-05
steps_total = 1000
beta_one = 0.9
beta_two = 0.95
adam_eps = 1e-08
decay = 0.01
shampoo_momentum = 0.9
shampoo_beta = 0.95
shampoo_rate = 0.5
rate_table = 0.5
rate_first = 0.2
rate_last = 0.015
rate_gain = 0.1
score_scale = 0.125
masked_score = -1000000000.0

def square_mask(image_sides, extent):
    positions = jnp.arange(extent)
    inside = positions[None, :] < image_sides[:, None]
    return (inside[:, :, None] & inside[:, None, :]).astype(jnp.float32)

def conv_three(images, kernel):
    rows_px, cols_px = (images.shape[1], images.shape[2])
    padded = jnp.pad(images, ((0, 0), (1, 1), (1, 1), (0, 0)))
    result = 0.0
    for tap_index in range(9):
        i, j = divmod(tap_index, 3)
        result = result + jnp.einsum('bhwc,co->bhwo', padded[:, i:i + rows_px, j:j + cols_px], kernel[tap_index], precision=highest)
    return result

def group_norm(values, valid, gain_vec, bias_vec, groups):
    count_img, rows_px, cols_px, channels = values.shape
    grouped = values.reshape(count_img, rows_px, cols_px, groups, channels // groups)
    weight = valid[:, :, :, None, None]
    members = lax.optimization_barrier(jnp.sum(valid, axis=(1, 2)))[:, None, None, None, None] * (channels // groups)
    centre = lax.optimization_barrier(jnp.sum(grouped * weight, axis=(1, 2, 4), keepdims=True)) / members
    spread = lax.optimization_barrier(jnp.sum(((grouped - centre) * weight) ** 2, axis=(1, 2, 4), keepdims=True)) / members
    normed = (grouped - centre) * lax.rsqrt(spread + norm_eps)
    return normed.reshape(values.shape) * gain_vec + bias_vec

def layer_norm(values, gain_vec, bias_vec):
    centre = lax.optimization_barrier(jnp.mean(values, axis=-1, keepdims=True))
    spread = lax.optimization_barrier(jnp.mean(values * values, axis=-1, keepdims=True)) - centre * centre
    return (values - centre) * lax.rsqrt(spread + norm_eps) * gain_vec + bias_vec

def sinusoid(timesteps, embed_dims):
    half_dims = embed_dims // 2
    frequency = jnp.exp(-math.log(10000.0) * jnp.arange(half_dims).astype(jnp.float32) / half_dims)
    angles = timesteps.astype(jnp.float32)[:, None] * frequency[None, :]
    return jnp.concatenate([jnp.cos(angles), jnp.sin(angles)], axis=1)

def attend(inputs):
    queries, keys_in, values_in, key_keep = inputs
    scores = low_back(jnp.einsum('qhd,khd->hqk', queries, keys_in, precision=highest) * score_scale)
    scores = jnp.where(key_keep[None, None, :] > 0, scores, masked_score)
    peak = lax.optimization_barrier(jnp.max(scores, axis=-1, keepdims=True))
    expo = jnp.exp(scores - peak)
    weights = low(expo / lax.optimization_barrier(jnp.sum(expo, axis=-1, keepdims=True)))
    return jnp.einsum('hqk,khd->qhd', weights, values_in, precision=highest)

def layout(layout_kind, shape, groups, group_width):
    if layout_kind == 'stack':
        return ((shape[0], shape[1], groups, group_width), (1, 2, 0, 3), shape[1], shape[0])
    if layout_kind == 'conv':
        return ((shape[0] * shape[1], groups, 1, group_width), (0, 1, 2, 3), shape[0] * shape[1], 1)
    if layout_kind == 'trio':
        return ((shape[0], shape[1], groups, group_width), (0, 2, 1, 3), shape[0], shape[1])
    if layout_kind == 'pair':
        inner_count = shape[2] // (groups * group_width)
        return ((shape[0], shape[1], groups, inner_count, group_width), (0, 2, 1, 3, 4), shape[0], shape[1] * inner_count)
    inner_count = shape[1] // (groups * group_width)
    return ((shape[0], groups, inner_count, group_width), (0, 1, 2, 3), shape[0], inner_count)

def to_blocks(array, sectioned, axes_order, row_count, groups, block_count, group_width):
    return array.reshape(sectioned).transpose(axes_order).reshape(row_count, groups, block_count, group_width)

def from_blocks(blocked, sectioned, axes_order, shape):
    arranged = tuple((sectioned[position] for position in axes_order))
    undo = tuple((axes_order.index(position) for position in range(len(axes_order))))
    return blocked.reshape(arranged).transpose(undo).reshape(shape)

def inverse_root(matrices):
    size_n = matrices.shape[-1]
    identity = jnp.eye(size_n, dtype=jnp.float32)
    trace_val = jnp.trace(matrices, axis1=-2, axis2=-1)[..., None, None]
    current = matrices / trace_val
    inverse = jnp.broadcast_to(identity, matrices.shape)
    for sweep in range(NS_ITERS):
        middle = 1.5 * identity - 0.5 * jnp.matmul(inverse, current, precision=highest)
        current = jnp.matmul(current, middle, precision=highest)
        inverse = jnp.matmul(middle, inverse, precision=highest)
    return inverse * lax.rsqrt(trace_val)

def adam_step(weight, moment_one, moment_two, gradient, step_rate):
    moment_one_new = beta_one * moment_one + (1 - beta_one) * gradient
    moment_two_new = beta_two * moment_two + (1 - beta_two) * gradient * gradient
    corrected = moment_one_new / (1 - beta_one ** STEP) / (jnp.sqrt(moment_two_new / (1 - beta_two ** STEP)) + adam_eps)
    return (weight - step_rate * (corrected + decay * weight), moment_one_new, moment_two_new)

def group_loss(params, clean_latent, noise_latent, timesteps, labels, image_sides, band_weight):
    w_square, w_conv, w_qkv, w_ffin, w_ffout, w_time_in, w_time_out, class_table, conv_first, conv_last = tuple((low(member) for member in params[:10]))
    gains = params[10]
    count_img = clean_latent.shape[0]
    mid_side = SIDE // 2
    token_count = mid_side * mid_side
    full_mask = square_mask(image_sides, SIDE)
    half_mask = square_mask(image_sides // 2, mid_side)
    full_keep = full_mask[..., None]
    half_keep = half_mask[..., None]
    fraction = (timesteps.astype(jnp.float32) + 0.5) / steps_total
    signal = jnp.cos(0.5 * math.pi * fraction)[:, None, None, None]
    noise_level = jnp.sin(0.5 * math.pi * fraction)[:, None, None, None]
    latent = clean_latent.reshape(count_img, LAT, SIDE, SIDE).transpose(0, 2, 3, 1)
    noise_img = noise_latent.reshape(count_img, LAT, SIDE, SIDE).transpose(0, 2, 3, 1)
    noisy = low((signal * latent + noise_level * noise_img) * full_keep)
    first = low_back(conv_three(noisy, conv_first)) * full_keep
    pooled = first.reshape(count_img, mid_side, 2, mid_side, 2, C).mean(axis=(2, 4))
    embedded = low(sinusoid(timesteps, TE))
    hidden_time = low_back(jnp.dot(embedded, w_time_in, precision=highest))
    time_vec = low_back(jnp.dot(low(jax.nn.silu(hidden_time)), w_time_out, precision=highest))
    res_input = low(jax.nn.silu(group_norm(pooled, half_mask, gains[0, 0], gains[0, 1], GROUPS)) * half_keep)
    res_out = low_back(conv_three(res_input, w_conv))
    after_res = pooled + (res_out + time_vec[:, None, None, :]) * half_keep
    normed_in = low(group_norm(after_res, half_mask, gains[1, 0], gains[1, 1], GROUPS) * half_keep).reshape(count_img, token_count, C)
    stream = low_back(jnp.einsum('btc,cd->btd', normed_in, w_square[0], precision=highest))
    attn_in = low(layer_norm(stream, gains[2, 0], gains[2, 1]))
    projected = low_back(jnp.einsum('btc,cjd->btjd', attn_in, w_qkv, precision=highest))
    queries = low(projected[:, :, 0]).reshape(count_img, token_count, HEADS, HD)
    keys_all = low(projected[:, :, 1]).reshape(count_img, token_count, HEADS, HD)
    values_all = low(projected[:, :, 2]).reshape(count_img, token_count, HEADS, HD)
    key_keep = half_mask.reshape(count_img, token_count)
    attended = lax.map(jax.checkpoint(attend), (queries, keys_all, values_all, key_keep))
    attended = low_back(low(attended.reshape(count_img, token_count, C)))
    stream = stream + low_back(jnp.einsum('btc,cd->btd', attended, w_square[1], precision=highest))
    context = class_table[labels]
    cross_val = low_back(low(jnp.dot(context, w_square[2], precision=highest)))
    cross_out = low_back(jnp.dot(cross_val, w_square[3], precision=highest))
    stream = stream + cross_out[:, None, :]
    ff_in = low(layer_norm(stream, gains[3, 0], gains[3, 1]))
    ff_proj = low_back(jnp.einsum('btc,cjf->btjf', ff_in, w_ffin, precision=highest))
    ff_hidden = low(ff_proj[:, :, 0] * jax.nn.gelu(ff_proj[:, :, 1], approximate=False))
    stream = stream + low_back(jnp.einsum('btf,fc->btc', ff_hidden, w_ffout, precision=highest))
    proj_out = low_back(jnp.einsum('btc,cd->btd', low(stream), w_square[4], precision=highest))
    after_attn = after_res + proj_out.reshape(count_img, mid_side, mid_side, C) * half_keep
    merged = jnp.repeat(jnp.repeat(after_attn, 2, axis=1), 2, axis=2) + first
    last_in = low(jax.nn.silu(group_norm(merged, full_mask, gains[4, 0], gains[4, 1], GROUPS)) * full_keep)
    predicted = low_back(conv_three(last_in, conv_last))
    target = signal * noise_img - noise_level * latent
    error = (predicted - target) * full_keep
    per_image = lax.optimization_barrier(jnp.sum(error * error, axis=(1, 2, 3)))
    return (jnp.sum(per_image * band_weight), per_image)

def reference(clean_latent, noise_latent, timesteps, labels, image_sides, w_square, mom_square, w_conv, mom_conv, w_qkv, mom_qkv, w_ffin, mom_ffin, w_ffout, mom_ffout, w_time_in, mom_time_in, w_time_out, mom_time_out, kron_stats, class_table, table_mean, table_var, conv_first, first_mean, first_var, conv_last, last_mean, last_var, norm_params, norm_mean, norm_var):
    band_ids = timesteps * NBANDS // steps_total
    band_hot = (band_ids[:, None] == jnp.arange(NBANDS)[None, :]).astype(jnp.float32)
    pixel_count = (LAT * image_sides * image_sides).astype(jnp.float32)
    counts = jnp.dot(pixel_count, band_hot, precision=highest)
    band_weight = jnp.dot(band_hot, 1.0 / (counts + 1.0), precision=highest) / NBANDS
    params = (w_square, w_conv, w_qkv, w_ffin, w_ffout, w_time_in, w_time_out, class_table, conv_first, conv_last, norm_params)
    groups_count = NIMG // IMG_DEV
    portions = tuple((member.reshape((groups_count, IMG_DEV) + member.shape[1:]) for member in (clean_latent, noise_latent, timesteps, labels, image_sides, band_weight)))

    def one_group(totals, portion):
        loss_value, pullback, per_image = jax.vjp(lambda inner: group_loss(inner, *portion), params, has_aux=True)
        gradients = pullback(jnp.ones_like(loss_value))[0]
        return (jax.tree.map(jnp.add, totals, gradients), per_image)
    gradients, per_image = lax.scan(one_group, jax.tree.map(jnp.zeros_like, params), portions)
    band_sums = jnp.dot(per_image.reshape(-1), band_hot, precision=highest)
    layout_kinds = ('stack', 'conv', 'trio', 'pair', 'plain', 'plain', 'plain')
    matrices = (w_square, w_conv, w_qkv, w_ffin, w_ffout, w_time_in, w_time_out)
    momenta = (mom_square, mom_conv, mom_qkv, mom_ffin, mom_ffout, mom_time_in, mom_time_out)
    stats_view = kron_stats.reshape(N_MP, NBLK, GRP, GRP)
    results = []
    renewed_all = []
    offset = 0
    for position in range(7):
        sectioned, axes_order, row_count, block_count = layout(layout_kinds[position], matrices[position].shape, N_MP, GRP)
        blocks = to_blocks(gradients[position], sectioned, axes_order, row_count, N_MP, block_count, GRP)
        renewed = shampoo_beta * stats_view[:, offset:offset + block_count] + jnp.einsum('rmbi,rmbj->mbij', blocks, blocks, precision=highest)
        precond = inverse_root(renewed)
        moment = shampoo_momentum * momenta[position] + gradients[position]
        rotated = jnp.einsum('rmbi,mbij->rmbj', to_blocks(moment, sectioned, axes_order, row_count, N_MP, block_count, GRP), precond, precision=highest)
        direction = from_blocks(rotated, sectioned, axes_order, moment.shape)
        results += [matrices[position] - shampoo_rate * (direction + decay * matrices[position]), moment]
        renewed_all.append(renewed)
        offset += block_count
    stats_new = jnp.concatenate(renewed_all, axis=1).reshape(N_MP * NBLK, GRP, GRP)
    table_out = adam_step(class_table, table_mean, table_var, gradients[7], rate_table)
    first_out = adam_step(conv_first, first_mean, first_var, gradients[8], rate_first)
    last_out = adam_step(conv_last, last_mean, last_var, gradients[9], rate_last)
    norm_out = adam_step(norm_params, norm_mean, norm_var, gradients[10], rate_gain)
    loss_terms = jnp.stack([band_sums, counts])
    return (results[0], results[1], results[2], results[3], results[4], results[5], results[6], results[7], results[8], results[9], results[10], results[11], results[12], results[13], stats_new, table_out[0], table_out[1], table_out[2], first_out[0], first_out[1], first_out[2], last_out[0], last_out[1], last_out[2], norm_out[0], norm_out[1], norm_out[2], loss_terms)
```

```python
import functools
import math

import jax
import jax.numpy as jnp
from jax import lax
from jax.experimental import pallas as pl
from jax.experimental.pallas import tpu as pltpu
from jax.sharding import PartitionSpec as P

C = 512
GROUPS = 32
HD = 64
TE = 256
NCLS = 1000
LAT = 3
SIDE = 32
NBANDS = 4
NS_ITERS = 6
STEP = 5


highest = lax.Precision.HIGHEST
norm_eps = 1e-05
steps_total = 1000
beta_one = 0.9
beta_two = 0.95
adam_eps = 1e-08
decay = 0.01
shampoo_momentum = 0.9
shampoo_beta = 0.95
shampoo_rate = 0.5
rate_table = 0.5
rate_first = 0.2
rate_last = 0.015
rate_gain = 0.1
score_scale = 0.125
masked_score = -1000000000.0


DP, MP = "dp", "mp"
MESH_ID = pl.DeviceIdType.MESH
VMEM_LIMIT = 60 * 1024 * 1024


def remote(src, dst, send_sem, recv_sem, device):
    return pltpu.make_async_remote_copy(
        src_ref=src, dst_ref=dst, send_sem=send_sem, recv_sem=recv_sem, device_id=device, device_id_type=MESH_ID
    )


def steps(low, high, body):
    if high - low <= 8:
        for index in range(low, high):
            body(index)
    else:
        lax.fori_loop(low, high, lambda index, carry: (body(index), carry)[1], 0)


class Place:
    def __init__(self, dp_size, mp_size):
        self.dp_size = dp_size
        self.mp_size = mp_size
        self.outer_size = dp_size // 2
        self.dp = lax.axis_index(DP)
        self.mp = lax.axis_index(MP)
        self.outer = self.dp // 2
        self.inner = lax.rem(self.dp, 2)

    def at(self, outer, inner):
        return outer * 2 + inner

    def ahead(self, step):
        return lax.rem(self.outer + step, self.outer_size)

    def behind(self, step):
        return lax.rem(self.outer + self.outer_size - step, self.outer_size)

    def partner(self):
        return (self.at(self.outer, 1 - self.inner), self.mp)

    def across(self, step):
        return (self.at(self.ahead(step), self.inner), self.mp)

    def greet_dp(self, barrier):
        pl.semaphore_signal(barrier, inc=1, device_id=self.partner(), device_id_type=MESH_ID)

        def one(step):
            pl.semaphore_signal(barrier, inc=1, device_id=self.across(step), device_id_type=MESH_ID)

        steps(1, self.outer_size, one)
        return self.outer_size


class Gather:
    def __init__(self, place, shard, full, sems, pieces):
        self.place = place
        self.shard = shard
        self.full = full
        self.out_send, self.out_recv, self.in_send, self.in_recv = sems
        self.pieces = pieces

    @staticmethod
    def sems(place_outer, count):
        return [pltpu.SemaphoreType.DMA((count, place_outer))] * 4

    def part(self, ref, piece):
        low, count = self.pieces[piece]
        return ref.at[pl.ds(low, count)]

    def slot(self, source, piece):
        low, count = self.pieces[piece]
        return self.full.at[source, pl.ds(low, count)]

    def out_copy(self, piece, step, source):
        return remote(
            self.part(self.shard, piece),
            self.slot(source, piece),
            self.out_send.at[piece, step],
            self.out_recv.at[piece, step],
            self.place.across(step),
        )

    def in_copy(self, piece, step, source, src=None):
        return remote(
            self.slot(source, piece) if src is None else src,
            self.slot(source, piece),
            self.in_send.at[piece, step],
            self.in_recv.at[piece, step],
            self.place.partner(),
        )

    def start(self, piece):
        place = self.place
        steps(1, place.outer_size, lambda step: self.out_copy(piece, step, place.dp).start())
        self.in_copy(piece, 0, place.dp, self.part(self.shard, piece)).start()

    def pump(self, piece):
        place = self.place

        def one(step):
            source = place.at(place.behind(step), place.inner)
            self.out_copy(piece, step, source).wait_recv()
            self.in_copy(piece, step, source).start()

        steps(1, place.outer_size, one)

    def ready(self, piece):
        place = self.place

        def one(step):
            source = place.at(place.behind(step), 1 - place.inner)
            self.in_copy(piece, step, source).wait_recv()

        steps(0, place.outer_size, one)

    def drain(self, piece):
        place = self.place
        steps(1, place.outer_size, lambda step: self.out_copy(piece, step, place.dp).wait_send())
        self.in_copy(piece, 0, place.dp, self.part(self.shard, piece)).wait_send()

        def one(step):
            source = place.at(place.behind(step), place.inner)
            self.in_copy(piece, step, source).wait_send()

        steps(1, place.outer_size, one)


class Scatter:
    def __init__(self, place, partials, total, near, sums, far, sems, pieces):
        self.place = place
        self.partials = partials
        self.total = total
        self.near = near
        self.sums = sums
        self.far = far
        self.in_send, self.in_recv, self.out_send, self.out_recv = sems
        self.pieces = pieces

    def cut(self, ref, index, piece):
        low, count = self.pieces[piece]
        return ref.at[index, pl.ds(low, count)]

    def in_copy(self, piece, step):
        place = self.place
        return remote(
            self.cut(self.partials, place.at(place.ahead(step), 1 - place.inner), piece),
            self.cut(self.near, step, piece),
            self.in_send.at[piece, step],
            self.in_recv.at[piece, step],
            place.partner(),
        )

    def out_copy(self, piece, step):
        return remote(
            self.cut(self.sums, step, piece),
            self.cut(self.far, step, piece),
            self.out_send.at[piece, step],
            self.out_recv.at[piece, step],
            self.place.across(step),
        )

    def start(self, piece):
        last = self.place.outer_size
        steps(1, last, lambda step: self.in_copy(piece, step).start())
        self.in_copy(piece, 0).start()

    def pump(self, piece):
        place = self.place
        low, count = self.pieces[piece]

        def one(step):
            self.in_copy(piece, step).wait_recv()
            mine = self.partials[place.at(place.ahead(step), place.inner), pl.ds(low, count)]
            theirs = self.near[step, pl.ds(low, count)]
            self.sums[step, pl.ds(low, count)] = (
                mine.astype(jnp.float32) + theirs.astype(jnp.float32)
            ).astype(jnp.bfloat16)
            self.out_copy(piece, step).start()

        steps(1, place.outer_size, one)
        self.in_copy(piece, 0).wait_recv()
        self.total[pl.ds(low, count)] = self.partials[
            place.dp, pl.ds(low, count)
        ].astype(jnp.float32) + self.near[0, pl.ds(low, count)].astype(jnp.float32)

    def finish(self, piece):
        low, count = self.pieces[piece]

        def one(step):
            self.out_copy(piece, step).wait_recv()
            self.total[pl.ds(low, count)] += self.far[step, pl.ds(low, count)].astype(jnp.float32)

        steps(1, self.place.outer_size, one)

    def drain(self, piece):
        last = self.place.outer_size
        steps(0, last, lambda step: self.in_copy(piece, step).wait_send())
        steps(1, last, lambda step: self.out_copy(piece, step).wait_send())


def split(values):
    high = values.astype(jnp.bfloat16)
    return high, (values - high.astype(jnp.float32)).astype(jnp.bfloat16)


def dot_nn(left, right):
    return lax.dot_general(left, right, (((1,), (0,)), ((), ())), preferred_element_type=jnp.float32)


def dot_tn(left, right):
    return lax.dot_general(left, right, (((0,), (0,)), ((), ())), preferred_element_type=jnp.float32)


def dot_nt(left, right):
    return lax.dot_general(left, right, (((1,), (1,)), ((), ())), preferred_element_type=jnp.float32)


def exact(left, right):
    left_high, left_low = split(left)
    right_high, right_low = split(right)
    return dot_nn(left_high, right_high) + (dot_nn(left_high, right_low) + dot_nn(left_low, right_high))


def gram_of(values):
    high, low = split(values)
    cross = dot_tn(high, low)
    return dot_tn(high, high) + (cross + cross.T)


TIN, TOUT, CONV, SQ0, QKV, SQ1, SQ2, SQ3, FFIN, FFOUT, SQ4 = range(11)
SQUARES = (SQ0, SQ1, SQ2, SQ3, SQ4)
SECTIONS = ((TIN, 1), (TOUT, 2), (CONV, 9), (SQ0, 1), (QKV, 3), (SQ1, 1), (SQ2, 1), (SQ3, 1), (FFIN, 8), (FFOUT, 4), (SQ4, 1))
STARTS = {}
for _name, _count in SECTIONS:
    STARTS[_name] = sum(count for name, count in SECTIONS[: len(STARTS)])
SECTION_COUNT = sum(count for name, count in SECTIONS)
BLOCKS = (
    tuple((STARTS[SQUARES[k]], 1) for k in range(5))
    + ((STARTS[CONV], 9),)
    + tuple((STARTS[QKV] + k, 1) for k in range(3))
    + tuple((STARTS[FFIN] + k, 1) for k in range(8))
    + ((STARTS[FFOUT], 4), (STARTS[TIN], 1), (STARTS[TIN], 1), (STARTS[TOUT], 2))
)
GATHER_PIECES = ((0, 3), (3, 3), (6, 3), (9, 3), (12, 4), (16, 3), (19, 4), (23, 4), (27, 5))
SCATTER_PIECES = ((27, 5), (23, 4), (19, 4), (16, 3), (12, 4), (9, 3), (6, 3), (3, 3), (0, 3))


def pack(square, conv, qkv, ffin, ffout, time_in, time_out):
    rows = square.shape[1]
    width = square.shape[2]
    parts = {
        TIN: time_in.reshape(1, rows, width),
        TOUT: time_out.reshape(2, rows, width),
        CONV: conv,
        QKV: qkv.transpose(1, 0, 2),
        FFIN: ffin.reshape(rows, 8, width).transpose(1, 0, 2),
        FFOUT: ffout.reshape(4, rows, width),
    }
    for k in range(5):
        parts[SQUARES[k]] = square[k : k + 1]
    return jnp.concatenate([parts[name] for name, count in SECTIONS], axis=0)


def unpack(packed, square, conv, qkv, ffin, ffout, time_in, time_out):
    def part(name):
        low = STARTS[name]
        return packed[low : low + dict(SECTIONS)[name]]

    return (
        jnp.concatenate([part(SQUARES[k]) for k in range(5)], axis=0),
        part(CONV),
        part(QKV).transpose(1, 0, 2),
        part(FFIN).transpose(1, 0, 2).reshape(ffin.shape),
        part(FFOUT).reshape(ffout.shape),
        part(TIN).reshape(time_in.shape),
        part(TOUT).reshape(time_out.shape),
    )


def gather_kernel(dp_size, mp_size, shard, counts, full, counts_full, *sems):
    place = Place(dp_size, mp_size)
    barrier = pltpu.get_barrier_semaphore()
    pl.semaphore_wait(barrier, place.greet_dp(barrier))
    weights = Gather(place, shard, full, sems[:4], GATHER_PIECES)
    small = Gather(place, counts, counts_full, sems[4:8], ((0, 1),))
    pieces = range(len(GATHER_PIECES))
    small.start(0)
    for piece in pieces:
        weights.start(piece)
    full[place.dp] = shard[...]
    counts_full[place.dp] = counts[...]
    small.pump(0)
    for piece in pieces:
        weights.pump(piece)
    small.ready(0)
    for piece in pieces:
        weights.ready(piece)
    small.drain(0)
    for piece in pieces:
        weights.drain(piece)


def gather_weights(dp_size, mp_size, shard, counts):
    vmem = pl.BlockSpec(memory_space=pltpu.VMEM)
    outer = dp_size // 2
    return pl.pallas_call(
        functools.partial(gather_kernel, dp_size, mp_size),
        out_shape=(
            jax.ShapeDtypeStruct((dp_size,) + shard.shape, shard.dtype),
            jax.ShapeDtypeStruct((dp_size,) + counts.shape, counts.dtype),
        ),
        in_specs=[vmem] * 2,
        out_specs=(vmem, vmem),
        scratch_shapes=Gather.sems(outer, len(GATHER_PIECES)) + Gather.sems(outer, 1),
        compiler_params=pltpu.CompilerParams(
            collective_id=1, has_side_effects=True, vmem_limit_bytes=VMEM_LIMIT
        ),
        name="gather_weights",
    )(shard, counts)


def inverse_roots(matrices):
    size = matrices[0].shape[-1]
    rows = lax.broadcasted_iota(jnp.int32, (size, size), 0)
    columns = lax.broadcasted_iota(jnp.int32, (size, size), 1)
    identity = (rows == columns).astype(jnp.float32)
    traces = [jnp.sum(matrix * identity) for matrix in matrices]
    current = [matrix * (1.0 / trace) for matrix, trace in zip(matrices, traces)]
    inverse = [identity for _ in matrices]
    for sweep in range(NS_ITERS):
        if sweep == 0:
            middle = [1.5 * identity - 0.5 * c for c in current]
            inverse = middle
        else:
            middle = [1.5 * identity - 0.5 * exact(z, c) for z, c in zip(inverse, current)]
            inverse = [exact(m, z) for m, z in zip(middle, inverse)]
        if sweep < NS_ITERS - 1:
            current = [exact(c, m) for c, m in zip(current, middle)]
    return [z * lax.rsqrt(jnp.full((1, size), trace, jnp.float32)) for z, trace in zip(inverse, traces)]


def reduce_kernel(dp_size, mp_size, partials, small_in, table_rows, weights, momenta, stats_in,
                  weights_out, momenta_out, stats_out, small_out, rows_out,
                  near, sums, far, total, gram_send, gram_land, root_own, root_all, stat_own, stat_all,
                  small_near, small_far, *sems):
    place = Place(dp_size, mp_size)
    barrier = pltpu.get_barrier_semaphore()

    def hello(step):
        pl.semaphore_signal(barrier, inc=1, device_id=(lax.rem(place.dp + step, dp_size), place.mp), device_id_type=MESH_ID)

    steps(1, dp_size, hello)
    pl.semaphore_wait(barrier, dp_size - 1)
    count = len(SCATTER_PIECES)
    scatter = Scatter(place, partials, total, near, sums, far, sems[:4], SCATTER_PIECES)
    roots = Gather(place, root_own, root_all, sems[4:8], ((0, root_own.shape[0]),))
    stats = Gather(place, stat_own, stat_all, sems[8:12], ((0, stat_own.shape[0]),))
    table = Gather(place, table_rows, rows_out, sems[12:16], ((0, 1),))
    gram_ss, gram_rs, small_ss, small_rs = sems[16:20]
    for piece in range(count):
        scatter.start(piece)

    table.start(0)
    near_copy = remote(small_in, small_near, small_ss.at[0], small_rs.at[0], place.partner())
    near_copy.start()
    rows_out[place.dp] = table_rows[...]

    def gram_copy(block, source):
        owner = block % dp_size
        return remote(
            gram_send.at[block],
            gram_land.at[block // dp_size, source],
            gram_ss.at[block],
            gram_rs.at[block // dp_size, source],
            (owner, place.mp),
        )

    parity = lax.rem(lax.broadcasted_iota(jnp.int32, total.shape[1:], 0), 2)

    def block_grams(blocks):
        for block in blocks:
            low, sections = BLOCKS[block]
            values = total[low : low + sections].reshape(-1, total.shape[2])
            if low == STARTS[TIN]:
                values = jnp.where(parity == block - 18, values, 0.0)
            gram_send[block] = gram_of(values)
            owner = block % dp_size

            @pl.when(place.dp != owner)
            def _():
                gram_copy(block, place.dp).start()

            @pl.when(place.dp == owner)
            def _():
                gram_land[block // dp_size, place.dp] = gram_send[block]

    done = set()
    for piece in range(count):
        scatter.pump(piece)
        if piece >= 2:
            scatter.finish(piece - 2)
            low = SCATTER_PIECES[piece - 2][0]
            now = [b for b in range(21) if BLOCKS[b][0] >= low and b not in done]
            done.update(now)
            block_grams(now)
        if piece == 1:
            near_copy.wait_recv()
            small_far[0] = small_in[...] + small_near[...]
            table.pump(0)

            def spread(step):
                remote(small_far.at[0], small_far.at[step], small_ss.at[step], small_rs.at[step], place.across(step)).start()

            steps(1, place.outer_size, spread)
    for piece in range(count - 2, count):
        scatter.finish(piece)
        low = SCATTER_PIECES[piece][0]
        now = [b for b in range(21) if BLOCKS[b][0] >= low and b not in done]
        done.update(now)
        block_grams(now)

    slots = root_own.shape[0]
    for slot in range(slots):
        full_slot = dp_size * (slot + 1) <= 21

        def receive(slot=slot):
            def one(step):
                source = lax.rem(place.dp + step, dp_size)
                block = slot * dp_size
                remote(
                    gram_send.at[block],
                    gram_land.at[slot, source],
                    gram_ss.at[block],
                    gram_rs.at[slot, source],
                    (source, place.mp),
                ).wait_recv()

            steps(1, dp_size, one)

        if full_slot:
            receive()
        else:
            pl.when(place.dp < 21 - dp_size * slot)(receive)
    renewed = []
    for slot in range(slots):
        block = lax.min(place.dp + slot * dp_size, 20)
        gram = gram_land[slot, 0]
        for source in range(1, dp_size):
            gram = gram + gram_land[slot, source]
        renewed.append(shampoo_beta * stats_in[block] + gram)
        stat_own[slot] = renewed[-1]
    stats.start(0)
    for slot, root in enumerate(inverse_roots(renewed)):
        root_own[slot] = root.astype(root_own.dtype)
    roots.start(0)
    roots.pump(0)
    stats.pump(0)
    root_all[place.dp] = root_own[...]
    stat_all[place.dp] = stat_own[...]
    small_total = small_far[0]

    def collect(step):
        remote(small_far.at[0], small_far.at[step], small_ss.at[step], small_rs.at[step], place.across(step)).wait_recv()

    steps(1, place.outer_size, collect)
    small_out[...] = jnp.sum(small_far[...], axis=0)
    table.ready(0)
    roots.ready(0)
    section_block = {}
    for block in range(21):
        low, sections = BLOCKS[block]
        for k in range(low, low + sections):
            section_block.setdefault(k, []).append(block)
    for k in range(SECTION_COUNT):
        moment = shampoo_momentum * momenta[k] + total[k]
        momenta_out[k] = moment
        high, low = split(moment)
        turned = []
        for block in section_block[k]:
            root = root_all[block % dp_size, block // dp_size]
            turned.append(dot_nn(high, root) + dot_nn(low, root))
        direction = turned[0]
        if len(turned) == 2:
            direction = jnp.where(parity == 0, turned[0], turned[1])
        weight = weights[k]
        weights_out[k] = weight - shampoo_rate * (direction + decay * weight)
    stats.ready(0)
    for block in range(21):
        stats_out[block] = stat_all[block % dp_size, block // dp_size].astype(jnp.float32)
    for piece in range(count):
        scatter.drain(piece)
    for gathered in (roots, stats, table):
        gathered.drain(0)
    near_copy.wait_send()

    def sent(step):
        remote(small_far.at[0], small_far.at[step], small_ss.at[step], small_rs.at[step], place.across(step)).wait_send()

    steps(1, place.outer_size, sent)
    for block in range(21):
        @pl.when(place.dp != block % dp_size)
        def _():
            gram_copy(block, place.dp).wait_send()


def reduce_and_update(dp_size, mp_size, partials, small, table_rows, weights, momenta, stats):
    vmem = pl.BlockSpec(memory_space=pltpu.VMEM)
    outer = dp_size // 2
    bf16, f32 = jnp.bfloat16, jnp.float32
    sections, rows, width = weights.shape
    pieces = len(SCATTER_PIECES)
    slots = -(-21 // dp_size)
    dma = pltpu.SemaphoreType.DMA
    return pl.pallas_call(
        functools.partial(reduce_kernel, dp_size, mp_size),
        out_shape=(
            jax.ShapeDtypeStruct(weights.shape, f32),
            jax.ShapeDtypeStruct(weights.shape, f32),
            jax.ShapeDtypeStruct(stats.shape, f32),
            jax.ShapeDtypeStruct(small.shape, f32),
            jax.ShapeDtypeStruct((dp_size,) + table_rows.shape, f32),
        ),
        in_specs=[vmem] * 6,
        out_specs=(vmem,) * 5,
        scratch_shapes=[
            pltpu.VMEM((outer, sections, rows, width), bf16),
            pltpu.VMEM((outer, sections, rows, width), bf16),
            pltpu.VMEM((outer, sections, rows, width), bf16),
            pltpu.VMEM((sections, rows, width), f32),
            pltpu.VMEM((21, width, width), f32),
            pltpu.VMEM((slots, dp_size, width, width), f32),
            pltpu.VMEM((slots, width, width), bf16),
            pltpu.VMEM((dp_size, slots, width, width), bf16),
            pltpu.VMEM((slots, width, width), f32),
            pltpu.VMEM((dp_size, slots, width, width), f32),
            pltpu.VMEM(small.shape, f32),
            pltpu.VMEM((outer,) + small.shape, f32),
        ]
        + [dma((pieces, outer))] * 4
        + Gather.sems(outer, 1) * 3
        + [dma((21,)), dma((slots, dp_size)), dma((outer,)), dma((outer,))],
        compiler_params=pltpu.CompilerParams(
            collective_id=2, has_side_effects=True, vmem_limit_bytes=VMEM_LIMIT
        ),
        name="reduce_and_update",
    )(partials, small, table_rows, weights, momenta, stats)


MID = SIDE // 2
TOKENS = MID * MID
PIXELS = SIDE * SIDE
LANES = 128


def sigmoid(values):
    return 1.0 / (1.0 + jnp.exp(-values))


ERF_TOP = (-2.72614225801306e-10, 2.77068142495902e-08, -2.10102402082508e-06, -5.69250639462346e-05, -7.34990630326855e-04, -2.95459980854025e-03, -1.60960333262415e-02)
ERF_LOW = (-1.45660718464996e-05, -2.13374055278905e-04, -1.68282697438203e-03, -7.37332916720468e-03, -1.42647390514189e-02)


def erf(values):
    values = jnp.clip(values, -4.0, 4.0)
    square = values * values
    top = jnp.full_like(square, ERF_TOP[0])
    for factor in ERF_TOP[1:]:
        top = top * square + factor
    low = jnp.full_like(square, ERF_LOW[0])
    for factor in ERF_LOW[1:]:
        low = low * square + factor
    return values * top / low


def group_sums(rows, spread):
    parts = []
    for row in rows:
        for _ in range(3):
            high = row.astype(jnp.bfloat16)
            parts.append(high)
            row = row - high.astype(jnp.float32)
    parts.append(jnp.zeros((16 - len(parts), LANES), jnp.bfloat16))
    summed = dot_nn(jnp.concatenate([part.astype(jnp.float32) for part in parts], axis=0).astype(jnp.bfloat16), spread)
    return [jnp.sum(summed[3 * k : 3 * k + 3], axis=0, keepdims=True) for k in range(len(rows))]


def column_sum(values):
    return jnp.sum(values, axis=0, keepdims=True)


def norm_stats(values, mask, share, spread):
    centre = group_sums([column_sum(values * mask)], spread)[0] * share
    off = (values - centre) * mask
    variance = group_sums([column_sum(off * off)], spread)[0] * share
    return centre, lax.rsqrt(variance + norm_eps)


def norm_backward(grads, normal, inv_std, mask, gain, share, spread):
    bias_grad = column_sum(grads)
    gain_grad = column_sum(grads * normal)
    first, second = group_sums([bias_grad * gain, gain_grad * gain], spread)
    return (
        inv_std * (grads * gain - mask * (first * share + normal * (second * share))),
        gain_grad,
        bias_grad,
    )


def token_norm(values, gain, bias):
    centre = jnp.mean(values, axis=-1, keepdims=True)
    variance = jnp.mean(values * values, axis=-1, keepdims=True) - centre * centre
    inv_std = lax.rsqrt(variance + norm_eps)
    normal = (values - centre) * inv_std
    return normal * gain + bias, normal, inv_std


def token_norm_backward(grads, normal, inv_std, gain):
    scaled = grads * gain
    width = grads.shape[-1]
    first = jnp.sum(scaled, axis=-1, keepdims=True) * (1.0 / width)
    second = jnp.sum(scaled * normal, axis=-1, keepdims=True) * (1.0 / width)
    return (scaled - first - normal * second) * inv_std, column_sum(grads * normal), column_sum(grads)


def shift_rows(values, rows):
    if rows == 0:
        return values
    count = abs(rows) * MID
    zeros = jnp.zeros((count, values.shape[1]), values.dtype)
    if rows > 0:
        return jnp.concatenate([values[count:], zeros], axis=0)
    return jnp.concatenate([zeros, values[:-count]], axis=0)


(X_NORMS, X_CONTEXT, X_TIME, X_RES, X_NORM, X_FFOUT_W, X_CROSS_VAL, X_CROSS_OUT, X_ATTN, X_FF, X_LAST, X_PREDICTED, X_G_PROJ, X_G_FF, X_GC, X_GV, X_GX, X_G_ATTN, X_G_AT, X_G_IN, X_G_RES, X_GT, X_NORM_SUMS, X_DW_FFOUT) = range(100, 124)


class Model:
    def __init__(self, place, refs, images, dp_size, mp_size):
        self.place = place
        self.r = refs
        self.images = images
        self.dp_size = dp_size
        self.mp_size = mp_size
        self.rows = refs.full.shape[2]
        self.me = place.mp
        self.exchange_ids = {}
        self.pending = []

    def peer(self, step):
        return (self.place.dp, lax.rem(self.me + step, self.mp_size))

    def source(self, step):
        return lax.rem(self.me + self.mp_size - step, self.mp_size)

    def index_of(self, name, part):
        key = (name, part)
        if key not in self.exchange_ids:
            self.exchange_ids[key] = len(self.exchange_ids)
        return self.exchange_ids[key]

    def spread(self, name, part, ref, cut):
        index = self.index_of(name, part)
        for step in range(1, self.mp_size):
            copy = remote(
                cut(ref, self.me), cut(ref, self.me), self.r.ex_send.at[index, step], self.r.ex_recv.at[index, step], self.peer(step)
            )
            copy.start()
            self.pending.append(copy)

    def spread_wait(self, name, part, ref, cut):
        index = self.index_of(name, part)
        for step in range(1, self.mp_size):
            region = cut(ref, self.source(step))
            remote(region, region, self.r.ex_send.at[index, step], self.r.ex_recv.at[index, step], self.peer(step)).wait_recv()

    def deal(self, name, part, out, land):
        index = self.index_of(name, part)
        for step in range(1, self.mp_size):
            target = lax.rem(self.me + step, self.mp_size)
            copy = remote(
                out(target), land(self.me), self.r.ex_send.at[index, step], self.r.ex_recv.at[index, step], self.peer(step)
            )
            copy.start()
            self.pending.append(copy)

    def deal_wait(self, name, part, land):
        index = self.index_of(name, part)
        for step in range(1, self.mp_size):
            region = land(self.source(step))
            remote(region, region, self.r.ex_send.at[index, step], self.r.ex_recv.at[index, step], self.peer(step)).wait_recv()

    def drain(self):
        for copy in self.pending:
            copy.wait_send()

    def greet(self, barrier):
        for step in range(1, self.mp_size):
            pl.semaphore_signal(barrier, inc=1, device_id=self.peer(step), device_id_type=MESH_ID)
        return self.mp_size - 1

    def flat(self, values):
        width = values.shape[-1]
        count = math.prod(values.shape[:-1])
        if values.shape[-2] % 16 == 0:
            return values.reshape(count, width)
        return values.astype(jnp.float32).reshape(count, width).astype(jnp.bfloat16)

    def weight(self, name, k=0):
        return self.flat(self.r.full[:, STARTS[name] + k])

    def weight_rows(self, name, count):
        return self.flat(self.r.full[:, STARTS[name] : STARTS[name] + count])

    def emit(self, name, values, k=0):
        self.r.partials[:, STARTS[name] + k] = values.reshape(self.dp_size, self.rows, LANES).astype(jnp.bfloat16)

    def emit_rows(self, name, values, count):
        low = STARTS[name]
        self.r.partials[:, low : low + count] = values.reshape(self.dp_size, count, self.rows, LANES).astype(jnp.bfloat16)

    def wide(self, ref, m):
        return self.flat(ref[m])

    def wide_mine(self, ref, m):
        share = self.dp_size // self.mp_size
        return self.flat(ref[m, pl.ds(self.me * share, share)])

    def columns(self, image):
        return lambda ref, m: ref.at[pl.ds(image * TOKENS, TOKENS), pl.ds(pl.multiple_of(m * LANES, LANES), LANES)]

    def token_rows(self, image):
        share = TOKENS // self.mp_size
        return lambda ref, m: ref.at[pl.ds(pl.multiple_of(image * TOKENS + m * share, share), share)]

    def mine(self):
        return pl.ds(pl.multiple_of(self.me * LANES, LANES), LANES)

    def my_tokens(self):
        share = TOKENS // self.mp_size
        return pl.ds(pl.multiple_of(self.me * share, share), share)

    def image_rows(self, image):
        return pl.ds(image * TOKENS, TOKENS)

    @staticmethod
    def whole_slot(ref, m):
        return ref.at[m]

    def across_lanes(self, image):
        key = lax.broadcasted_iota(jnp.int32, (1, TOKENS), 1)
        side = self.r.sides[image] // 2
        return (key // MID < side) & (lax.rem(key, MID) < side)

    def full_lane(self, norm, which):
        return jnp.concatenate([self.r.norms_all[m, norm, which : which + 1] for m in range(self.mp_size)], axis=1)

    def gain(self, norm):
        return self.r.norms[norm, 0:1]

    def bias(self, norm):
        return self.r.norms[norm, 1:2]

    def tap_lanes(self, values, tap):
        i, j = divmod(tap, 3)
        offset = (i - 1) * SIDE + (j - 1)
        moved = values if offset == 0 else pltpu.roll(values, (-offset) % PIXELS, 1)
        pixel = lax.broadcasted_iota(jnp.int32, values.shape, 1)
        row, column = pixel // SIDE + (i - 1), lax.rem(pixel, SIDE) + (j - 1)
        inside = (row >= 0) & (row < SIDE) & (column >= 0) & (column < SIDE)
        return jnp.where(inside, moved, 0.0)

    def setup(self):
        r = self.r
        lane = lax.broadcasted_iota(jnp.int32, (LANES, LANES), 1) // (C // GROUPS)
        row = lax.broadcasted_iota(jnp.int32, (LANES, LANES), 0) // (C // GROUPS)
        r.group_spread[...] = (lane == row).astype(jnp.bfloat16)
        r.norms_all[self.me] = r.norms[...]
        self.spread(X_NORMS, 0, r.norms_all, self.whole_slot)
        r.context_all[self.me] = r.context[...]
        self.spread(X_CONTEXT, 0, r.context_all, self.whole_slot)
        for image in range(self.images):
            side = r.sides[image]
            pixel = lax.broadcasted_iota(jnp.int32, (PIXELS, LANES), 0)
            r.full_mask[image] = ((pixel // SIDE < side) & (lax.rem(pixel, SIDE) < side)).astype(jnp.float32)
            half = side // 2
            token = lax.broadcasted_iota(jnp.int32, (TOKENS, LANES), 0)
            r.half_mask[image] = ((token // MID < half) & (lax.rem(token, MID) < half)).astype(jnp.float32)
        for image in range(self.images):
            r.latent8[LAT * image : LAT * image + LAT] = r.latent[image]
            r.noise8[LAT * image : LAT * image + LAT] = r.noise[image]
        rest = LAT * self.images
        r.latent8[rest:] = jnp.zeros((8 - rest, PIXELS), jnp.float32)
        r.noise8[rest:] = jnp.zeros((8 - rest, PIXELS), jnp.float32)
        lane_row = lax.broadcasted_iota(jnp.int32, (8, PIXELS), 0)
        pixel = lax.broadcasted_iota(jnp.int32, (8, PIXELS), 1)
        side = jnp.zeros((8, PIXELS), jnp.int32)
        for image in range(self.images):
            side = jnp.where(lane_row // LAT == image, r.sides[image], side)
        r.lane_mask[...] = ((pixel // SIDE < side) & (lax.rem(pixel, SIDE) < side)).astype(jnp.float32)
        signal, level = r.signal8[:, 0:1], r.level8[:, 0:1]
        noisy = (signal * r.latent8[...] + level * r.noise8[...]) * r.lane_mask[...]
        noisy = noisy.astype(jnp.bfloat16).astype(jnp.float32)
        for tap in range(9):
            r.taps[8 * tap : 8 * tap + 8] = self.tap_lanes(noisy, tap)

    def entry(self, image):
        r = self.r
        first = dot_tn(r.taps[...].astype(jnp.bfloat16), r.first_w[image]) * r.full_mask[image]
        r.first[image] = first
        paired = r.first[image, pl.ds(0, PIXELS // 2, stride=2)] + r.first[image, pl.ds(1, PIXELS // 2, stride=2)]
        pooled = jnp.sum(paired.reshape(MID, 2, MID, LANES), axis=1).reshape(TOKENS, LANES) * 0.25
        r.pooled[image] = pooled
        mask = r.half_mask[image]
        centre, inv_std = norm_stats(pooled, mask, r.share_half[image], r.group_spread[...])
        values = (pooled - centre) * inv_std * self.gain(0) + self.bias(0)
        r.x_res[self.image_rows(image), self.mine()] = (values * sigmoid(values) * mask).astype(jnp.bfloat16)
        self.spread(X_RES, image, r.x_res, self.columns(image))

    def time_in(self):
        r = self.r
        table = self.weight(TIN)
        hidden = jnp.concatenate([dot_nn(r.embedded[h], table) for h in range(r.embedded.shape[0])], axis=1)
        r.hidden_time[...] = hidden
        r.time_act[self.me] = (hidden * sigmoid(hidden)).astype(jnp.bfloat16).astype(jnp.float32)
        self.spread(X_TIME, 0, r.time_act, self.whole_slot)

    def time_out(self):
        r = self.r
        self.spread_wait(X_TIME, 0, r.time_act, self.whole_slot)
        table = self.weight_rows(TOUT, 2)
        width = r.time_act.shape[2]
        total = 0.0
        for m in range(self.mp_size):
            total = total + dot_nn(r.time_act[m].astype(jnp.bfloat16), table[m * width : (m + 1) * width])
        r.time_vec[...] = total

    def convolve(self, image):
        r = self.r
        self.spread_wait(X_RES, image, r.x_res, self.columns(image))
        values = r.x_res[self.image_rows(image), :]
        column = lax.rem(lax.broadcasted_iota(jnp.int32, (TOKENS, LANES), 0), MID)
        total = 0.0
        for j in range(3):
            moved = 0.0
            for i in range(3):
                moved = moved + shift_rows(dot_nn(values, self.weight(CONV, 3 * i + j)), i - 1)
            if j == 0:
                moved = jnp.where(column > 0, pltpu.roll(moved, 1, 0), 0.0)
            elif j == 2:
                moved = jnp.where(column < MID - 1, pltpu.roll(moved, TOKENS - 1, 0), 0.0)
            total = total + moved
        mask = r.half_mask[image]
        after = r.pooled[image] + (total + r.time_vec[image : image + 1]) * mask
        r.after_res[image] = after
        centre, inv_std = norm_stats(after, mask, r.share_half[image], r.group_spread[...])
        values = (after - centre) * inv_std * self.gain(1) + self.bias(1)
        r.x_norm[self.image_rows(image), self.mine()] = (values * mask).astype(jnp.bfloat16)
        self.spread(X_NORM, image, r.x_norm, self.columns(image))

    def share_square(self, name, ref):
        low = STARTS[name]
        ref[self.me] = self.r.full[:, low]
        index = self.index_of(name, 0)
        for step in range(1, self.mp_size):
            copy = remote(
                self.r.full.at[:, low], ref.at[self.me], self.r.ex_send.at[index, step], self.r.ex_recv.at[index, step], self.peer(step)
            )
            copy.start()
            self.pending.append(copy)

    def share_square_wait(self, name, ref):
        self.spread_wait(name, 0, ref, self.whole_slot)

    def hidden_rows(self, ref, m):
        share = self.dp_size // self.mp_size
        low = STARTS[FFOUT]
        return ref.at[pl.ds(m * share, share), pl.ds(low, 4)]

    def share_ffout(self):
        r = self.r
        share = self.dp_size // self.mp_size
        low = STARTS[FFOUT]
        r.w_ffout[self.me] = r.full[pl.ds(self.me * share, share), low : low + 4]
        self.deal(X_FFOUT_W, 0, lambda m: self.hidden_rows(r.full, m), lambda m: r.w_ffout.at[m])

    def share_ffout_wait(self):
        self.deal_wait(X_FFOUT_W, 0, lambda m: self.r.w_ffout.at[m])

    def cross_first(self):
        r = self.r
        self.spread_wait(X_CONTEXT, 0, r.context_all, self.whole_slot)
        table = self.weight(SQ2)
        total = 0.0
        for m in range(self.mp_size):
            total = total + dot_nn(r.context_all[m].astype(jnp.bfloat16), table[m * LANES : (m + 1) * LANES])
        r.cross_val[self.me] = total.astype(jnp.bfloat16).astype(jnp.float32)
        self.spread(X_CROSS_VAL, 0, r.cross_val, self.whole_slot)

    def cross_second(self):
        r = self.r
        self.spread_wait(X_CROSS_VAL, 0, r.cross_val, self.whole_slot)
        table = self.weight(SQ3)
        total = 0.0
        for m in range(self.mp_size):
            total = total + dot_nn(r.cross_val[m].astype(jnp.bfloat16), table[m * LANES : (m + 1) * LANES])
        r.cross_out[self.me] = total
        self.spread(X_CROSS_OUT, 0, r.cross_out, self.whole_slot)

    def cross_last(self):
        self.spread_wait(X_CROSS_OUT, 0, self.r.cross_out, self.whole_slot)

    def attention(self, image):
        r = self.r
        self.spread_wait(X_NORM, image, r.x_norm, self.columns(image))
        values = r.x_norm[self.image_rows(image), :]
        for m in range(self.mp_size):
            r.stream_in[image, :, m * LANES : (m + 1) * LANES] = dot_nn(values, self.wide(r.w_in, m))
        attn_in = token_norm(r.stream_in[image], self.full_lane(2, 0), self.full_lane(2, 1))[0].astype(jnp.bfloat16)
        r.attn_in[self.image_rows(image), :] = attn_in
        for j in range(3):
            r.qkv[j, self.image_rows(image)] = dot_nn(attn_in, self.weight(QKV, j)).astype(jnp.bfloat16)
        keep = self.across_lanes(image)
        lane_head = lax.broadcasted_iota(jnp.int32, (TOKENS, LANES), 1) // HD
        queries, keys, vals = (r.qkv[j, self.image_rows(image)] for j in range(3))
        zero = jnp.zeros((), jnp.bfloat16)
        attended = jnp.zeros((TOKENS, LANES), jnp.float32)
        for head in range(LANES // HD):
            own = lane_head == head
            scores = dot_nt(jnp.where(own, queries, zero), keys) * score_scale
            scores = jnp.where(keep, scores, masked_score)
            peak = jnp.max(scores, axis=-1, keepdims=True)
            expo = jnp.exp(scores - peak)
            probs = expo / jnp.sum(expo, axis=-1, keepdims=True)
            r.probs[image, head] = probs
            attended = jnp.where(own, dot_nn(probs.astype(jnp.bfloat16), vals), attended)
        r.x_attn[self.image_rows(image), self.mine()] = attended.astype(jnp.bfloat16)
        self.spread(X_ATTN, image, r.x_attn, self.columns(image))

    def feed(self, image):
        r = self.r
        self.spread_wait(X_ATTN, image, r.x_attn, self.columns(image))
        values = r.x_attn[self.image_rows(image), :]
        for m in range(self.mp_size):
            cut = slice(m * LANES, (m + 1) * LANES)
            r.stream_cross[image, :, cut] = (
                r.stream_in[image, :, cut] + dot_nn(values, self.wide(r.w_attn, m)) + r.cross_out[m, image : image + 1]
            )
        ff_in = token_norm(r.stream_cross[image], self.full_lane(3, 0), self.full_lane(3, 1))[0].astype(jnp.bfloat16)
        r.ff_in[self.image_rows(image), :] = ff_in
        for k in range(4):
            cut = slice(k * LANES, (k + 1) * LANES)
            value = dot_nn(ff_in, self.weight(FFIN, k))
            gate = dot_nn(ff_in, self.weight(FFIN, 4 + k))
            r.ff_value[image, :, cut] = value
            r.ff_gate[image, :, cut] = gate
            half = 0.5 * (1.0 + erf(gate * math.sqrt(0.5)))
            r.ff_hidden[self.image_rows(image), cut] = (value * (gate * half)).astype(jnp.bfloat16)
        hidden = r.ff_hidden[self.image_rows(image), :]
        for m in range(self.mp_size):
            total = dot_nn(hidden, self.wide_hidden(m))
            self.token_out(X_FF, image, r.ff_send, m, total)
        self.token_deal(X_FF, image, r.ff_send, r.ff_land)

    def wide_hidden(self, m):
        return self.flat(self.r.w_ffout[m])

    def token_out(self, name, image, send, m, total):
        share = TOKENS // self.mp_size
        send[image, :, :, m * LANES : (m + 1) * LANES] = total.reshape(self.mp_size, share, LANES).astype(send.dtype)

    def token_deal(self, name, image, send, land):
        land[image, self.me] = send[image, self.me]
        self.deal(name, image, lambda m: send.at[image, m], lambda m: land.at[image, m])

    def token_sum(self, name, image, land):
        self.deal_wait(name, image, lambda m: land.at[image, m])
        return jnp.sum(land[image].astype(jnp.float32), axis=0)

    def leave(self, image):
        r = self.r
        total = self.token_sum(X_FF, image, r.ff_land)
        stream = (r.stream_cross[image, self.my_tokens(), :] + total).astype(jnp.bfloat16)
        self.token_rows(image)(r.x_last, self.me)[...] = stream
        self.spread(X_LAST, image, r.x_last, self.token_rows(image))

    def upsample(self, ref, image, values):
        twice = jnp.broadcast_to(values.reshape(MID, 1, MID, LANES), (MID, 2, MID, LANES)).reshape(PIXELS // 2, LANES)
        ref[image, pl.ds(0, PIXELS // 2, stride=2)] = twice
        ref[image, pl.ds(1, PIXELS // 2, stride=2)] = twice

    def finish(self, image):
        r = self.r
        self.spread_wait(X_LAST, image, r.x_last, self.token_rows(image))
        values = r.x_last[self.image_rows(image), :]
        after = r.after_res[image] + dot_nn(values, self.weight(SQ4)) * r.half_mask[image]
        self.upsample(r.merged, image, after)
        merged = r.merged[image] + r.first[image]
        r.merged[image] = merged
        mask = r.full_mask[image]
        centre, inv_std = norm_stats(merged, mask, r.share_full[image], r.group_spread[...])
        r.final_stats[image, 0:1] = centre
        r.final_stats[image, 1:2] = inv_std
        values = (merged - centre) * inv_std * self.gain(4) + self.bias(4)
        last_in = (values * sigmoid(values) * mask).astype(jnp.bfloat16)
        r.last_in[image] = last_in
        part = dot_nt(r.last_w[image], last_in)
        if image == 0:
            r.out_taps[...] = part
        else:
            r.out_taps[...] += part

    def predict(self):
        r = self.r
        total = 0.0
        for tap in range(9):
            total = total + self.tap_lanes(r.out_taps[8 * tap : 8 * tap + 8], tap)
        r.predicted[self.me] = total
        self.spread(X_PREDICTED, 0, r.predicted, self.whole_slot)

    def loss(self):
        r = self.r
        self.spread_wait(X_PREDICTED, 0, r.predicted, self.whole_slot)
        predicted = jnp.sum(r.predicted[...], axis=0)
        signal, level = r.signal8[:, 0:1], r.level8[:, 0:1]
        error = (predicted - (signal * r.noise8[...] - level * r.latent8[...])) * r.lane_mask[...]
        per_row = jnp.sum(error * error, axis=1, keepdims=True)
        r.small[8 * 20 : 8 * 20 + 8] = jnp.broadcast_to(column_sum(per_row * r.hot8[...]), (8, LANES))
        counts = jnp.sum(r.counts_all[...].reshape(-1, 8, LANES), axis=0)[0:1]
        weight = jnp.sum(r.hot8[...] * ((1.0 / NBANDS) / (counts + 1.0)), axis=1, keepdims=True)
        grads = (2.0 * error * weight).astype(jnp.bfloat16).astype(jnp.float32)
        for tap in range(9):
            r.out_taps[8 * tap : 8 * tap + 8] = self.tap_lanes(grads, 8 - tap)

    def pool_sum(self, ref, image):
        paired = ref[image, pl.ds(0, PIXELS // 2, stride=2)] + ref[image, pl.ds(1, PIXELS // 2, stride=2)]
        return jnp.sum(paired.reshape(MID, 2, MID, LANES), axis=1).reshape(TOKENS, LANES)

    def add_small(self, row, image, values):
        if image == 0:
            self.r.small[row : row + values.shape[0]] = values
        else:
            self.r.small[row : row + values.shape[0]] += values

    def tap_rows(self, values, image):
        row = lax.rem(lax.broadcasted_iota(jnp.int32, values.shape, 0), 8)
        return jnp.where(row // LAT == image, values, 0.0)

    def back_last(self, image):
        r = self.r
        grads_taps = r.out_taps[...].astype(jnp.bfloat16)
        mask = r.full_mask[image]
        grads = dot_tn(grads_taps, r.last_w[image]) * mask
        self.add_small(72, image, self.tap_rows(dot_nn(grads_taps, r.last_in[image]), image))
        inv_std = r.final_stats[image, 1:2]
        normal = (r.merged[image] - r.final_stats[image, 0:1]) * inv_std
        values = normal * self.gain(4) + self.bias(4)
        gate = sigmoid(values)
        grads = grads * (gate * (1.0 + values * (1.0 - gate)))
        grads, gain_grad, bias_grad = norm_backward(
            grads, normal, inv_std, mask, self.gain(4), r.share_full[image], r.group_spread[...]
        )
        self.add_small(144 + 8, image, gain_grad)
        self.add_small(144 + 9, image, bias_grad)
        r.merged[image] = grads
        after = self.pool_sum(r.merged, image)
        r.grad_after[image] = after
        r.g_proj[self.image_rows(image), self.mine()] = (after * r.half_mask[image]).astype(jnp.bfloat16)
        self.spread(X_G_PROJ, image, r.g_proj, self.columns(image))

    def back_feed(self, image):
        r = self.r
        self.spread_wait(X_G_PROJ, image, r.g_proj, self.columns(image))
        total = 0.0
        for m in range(self.mp_size):
            total = total + dot_nt(r.g_proj[self.image_rows(image), m * LANES : (m + 1) * LANES], self.wide(r.w_out, m))
        r.grad_stream[image] = total
        grads_low = total.astype(jnp.bfloat16)
        r.g_ffout[self.image_rows(image), :] = grads_low
        hidden = 0.0
        for m in range(self.mp_size):
            hidden = hidden + dot_nt(grads_low[:, m * LANES : (m + 1) * LANES], self.wide_hidden(m))
        r.g_hidden[...] = hidden
        for k in range(4):
            cut = slice(k * LANES, (k + 1) * LANES)
            value, gate, grads = r.ff_value[image, :, cut], r.ff_gate[image, :, cut], r.g_hidden[:, cut]
            half = 0.5 * (1.0 + erf(gate * math.sqrt(0.5)))
            slope = half + gate * (jnp.exp(-0.5 * gate * gate) * (1.0 / math.sqrt(2.0 * math.pi)))
            r.g_ffin[k, self.image_rows(image)] = (grads * (gate * half)).astype(jnp.bfloat16)
            r.g_ffin[4 + k, self.image_rows(image)] = (grads * value * slope).astype(jnp.bfloat16)
        total = 0.0
        for k in range(8):
            total = total + dot_nt(r.g_ffin[k, self.image_rows(image)], self.weight(FFIN, k))
        share = TOKENS // self.mp_size
        r.gff_send[image] = total.reshape(self.mp_size, share, C).astype(r.gff_send.dtype)
        self.token_deal(X_G_FF, image, r.gff_send, r.gff_land)

    def token_back(self, name, image, land, stream, norm, row):
        r = self.r
        grads = self.token_sum(name, image, land)
        values = stream[image, self.my_tokens(), :]
        gain = self.full_lane(norm, 0)
        _, normal, inv_std = token_norm(values, gain, 0.0)
        grads, gain_grad, bias_grad = token_norm_backward(grads, normal, inv_std, gain)
        for which, values in ((0, gain_grad), (1, bias_grad)):
            for m in range(self.mp_size):
                place = r.norm_send.at[m, row + which : row + which + 1]
                cut = values[:, m * LANES : (m + 1) * LANES]
                place[...] = cut if image == 0 else place[...] + cut
        total = r.grad_stream[image, self.my_tokens(), :] + grads
        r.grad_stream[image, self.my_tokens(), :] = total
        return total

    def back_cross(self, image):
        r = self.r
        total = self.token_back(X_G_FF, image, r.gff_land, r.stream_cross, 3, 2)
        r.gc_part[self.me, image : image + 1] = column_sum(total)
        self.token_rows(image)(r.g_attn, self.me)[...] = total.astype(jnp.bfloat16)
        self.spread(X_G_ATTN, image, r.g_attn, self.token_rows(image))

    def cross_one(self):
        r = self.r
        r.gc_part[self.me, self.images :] = jnp.zeros((8 - self.images, C), jnp.float32)
        self.spread(X_GC, 0, r.gc_part, self.whole_slot)

    def cross_two(self):
        r = self.r
        self.spread_wait(X_GC, 0, r.gc_part, self.whole_slot)
        r.gc_full[...] = jnp.sum(r.gc_part[...], axis=0)
        mine = r.gc_full[:, self.mine()].astype(jnp.bfloat16)
        for m in range(self.mp_size):
            r.dw[m * LANES : (m + 1) * LANES] = dot_tn(r.cross_val[m].astype(jnp.bfloat16), mine)
        self.emit(SQ3, r.dw[...])
        r.gv_part[self.me] = dot_nt(mine, self.weight(SQ3))
        self.spread(X_GV, 0, r.gv_part, self.whole_slot)

    def cross_three(self):
        r = self.r
        self.spread_wait(X_GV, 0, r.gv_part, self.whole_slot)
        r.gc_full[...] = jnp.sum(r.gv_part[...], axis=0)
        mine = r.gc_full[:, self.mine()].astype(jnp.bfloat16)
        for m in range(self.mp_size):
            r.dw[m * LANES : (m + 1) * LANES] = dot_tn(r.context_all[m].astype(jnp.bfloat16), mine)
        self.emit(SQ2, r.dw[...])
        r.gx_part[self.me] = dot_nt(mine, self.weight(SQ2))
        self.spread(X_GX, 0, r.gx_part, self.whole_slot)

    def cross_four(self):
        r = self.r
        self.spread_wait(X_GX, 0, r.gx_part, self.whole_slot)
        r.gc_full[...] = jnp.sum(r.gx_part[...], axis=0)
        row = lax.broadcasted_iota(jnp.int32, (8, LANES), 0)
        r.table_rows[0] = jnp.where(row < self.images, r.gc_full[:, self.mine()], r.labels8[...])

    def back_attention(self, image):
        r = self.r
        self.spread_wait(X_G_ATTN, image, r.g_attn, self.token_rows(image))
        total = 0.0
        for m in range(self.mp_size):
            total = total + dot_nt(r.g_attn[self.image_rows(image), m * LANES : (m + 1) * LANES], self.wide_mine(r.w_attn, m))
        grads = total.astype(jnp.bfloat16)
        queries, keys, vals = (r.qkv[j, self.image_rows(image)] for j in range(3))
        lane_head = lax.broadcasted_iota(jnp.int32, (TOKENS, LANES), 1) // HD
        zero = jnp.zeros((), jnp.bfloat16)
        results = [jnp.zeros((TOKENS, LANES), jnp.float32) for _ in range(3)]
        for head in range(LANES // HD):
            own = lane_head == head
            probs = r.probs[image, head]
            results[2] = jnp.where(own, dot_tn(probs.astype(jnp.bfloat16), grads), results[2])
            grad_probs = dot_nt(jnp.where(own, grads, zero), vals)
            grad_scores = (probs * (grad_probs - jnp.sum(probs * grad_probs, axis=-1, keepdims=True))).astype(jnp.bfloat16)
            results[0] = jnp.where(own, dot_nn(grad_scores, keys) * score_scale, results[0])
            results[1] = jnp.where(own, dot_tn(grad_scores, queries) * score_scale, results[1])
        total = 0.0
        for j in range(3):
            low = results[j].astype(jnp.bfloat16)
            r.g_qkv[j, self.image_rows(image)] = low
            total = total + dot_nt(low, self.weight(QKV, j))
        share = TOKENS // self.mp_size
        r.gat_send[image] = total.reshape(self.mp_size, share, C).astype(r.gat_send.dtype)
        self.token_deal(X_G_AT, image, r.gat_send, r.gat_land)

    def back_in(self, image):
        r = self.r
        total = self.token_back(X_G_AT, image, r.gat_land, r.stream_in, 2, 0)
        self.token_rows(image)(r.g_in, self.me)[...] = total.astype(jnp.bfloat16)
        self.spread(X_G_IN, image, r.g_in, self.token_rows(image))

    def back_conv(self, image):
        r = self.r
        self.spread_wait(X_G_IN, image, r.g_in, self.token_rows(image))
        mask = r.half_mask[image]
        grads = 0.0
        for m in range(self.mp_size):
            grads = grads + dot_nt(r.g_in[self.image_rows(image), m * LANES : (m + 1) * LANES], self.wide_mine(r.w_in, m))
        after = r.after_res[image]
        centre, inv_std = norm_stats(after, mask, r.share_half[image], r.group_spread[...])
        normal = (after - centre) * inv_std
        grads, gain_grad, bias_grad = norm_backward(
            grads * mask, normal, inv_std, mask, self.gain(1), r.share_half[image], r.group_spread[...]
        )
        self.add_small(144 + 2, image, gain_grad)
        self.add_small(144 + 3, image, bias_grad)
        grads = r.grad_after[image] + grads
        r.grad_after[image] = grads
        masked = grads * mask
        r.grad_time[image : image + 1] = column_sum(masked).astype(jnp.bfloat16).astype(jnp.float32)
        low = masked.astype(jnp.bfloat16).astype(jnp.float32)
        column = lax.rem(lax.broadcasted_iota(jnp.int32, (TOKENS, LANES), 0), MID)
        total = 0.0
        for tap in range(9):
            i, j = divmod(tap, 3)
            moved = shift_rows(low, 1 - i)
            if j == 0:
                moved = jnp.where(column < MID - 1, pltpu.roll(moved, TOKENS - 1, 0), 0.0)
            elif j == 2:
                moved = jnp.where(column > 0, pltpu.roll(moved, 1, 0), 0.0)
            moved = moved.astype(jnp.bfloat16)
            r.g_taps[self.image_rows(image), tap * LANES : (tap + 1) * LANES] = moved
            total = total + dot_nt(moved, self.weight(CONV, tap))
        for m in range(self.mp_size):
            r.gres_send[image, m] = total[:, m * LANES : (m + 1) * LANES].astype(r.gres_send.dtype)
        self.token_deal(X_G_RES, image, r.gres_send, r.gres_land)

    def back_first(self, image):
        r = self.r
        grads = self.token_sum(X_G_RES, image, r.gres_land)
        mask = r.half_mask[image]
        pooled = r.pooled[image]
        centre, inv_std = norm_stats(pooled, mask, r.share_half[image], r.group_spread[...])
        normal = (pooled - centre) * inv_std
        values = normal * self.gain(0) + self.bias(0)
        gate = sigmoid(values)
        grads = grads * mask * (gate * (1.0 + values * (1.0 - gate)))
        grads, gain_grad, bias_grad = norm_backward(
            grads, normal, inv_std, mask, self.gain(0), r.share_half[image], r.group_spread[...]
        )
        self.add_small(144, image, gain_grad)
        self.add_small(144 + 1, image, bias_grad)
        self.upsample(r.first, image, 0.25 * (r.grad_after[image] + grads))
        low = ((r.merged[image] + r.first[image]) * r.full_mask[image]).astype(jnp.bfloat16)
        self.add_small(0, image, self.tap_rows(dot_nn(r.taps[...].astype(jnp.bfloat16), low), image))

    def back_time(self):
        r = self.r
        r.grad_time[self.images :] = jnp.zeros((8 - self.images, LANES), jnp.float32)
        grads = r.grad_time[...].astype(jnp.bfloat16)
        width = r.time_act.shape[2]
        for m in range(self.mp_size):
            r.dw_time[m * width : (m + 1) * width] = dot_tn(r.time_act[m].astype(jnp.bfloat16), grads)
        self.emit_rows(TOUT, r.dw_time[...], 2)
        total = dot_nt(grads, self.weight_rows(TOUT, 2))
        for m in range(self.mp_size):
            r.gt_send[m] = total[:, m * width : (m + 1) * width]
        r.gt_land[self.me] = r.gt_send[self.me]
        self.deal(X_GT, 0, lambda m: r.gt_send.at[m], lambda m: r.gt_land.at[m])
        r.norm_land[self.me] = r.norm_send[self.me]
        self.deal(X_NORM_SUMS, 0, lambda m: r.norm_send.at[m], lambda m: r.norm_land.at[m])

    def back_time_in(self):
        r = self.r
        self.deal_wait(X_GT, 0, lambda m: r.gt_land.at[m])
        grads = jnp.sum(r.gt_land[...], axis=0)
        hidden = r.hidden_time[...]
        gate = sigmoid(hidden)
        grads = (grads * (gate * (1.0 + hidden * (1.0 - gate)))).astype(jnp.bfloat16)
        total = 0.0
        for h in range(r.embedded.shape[0]):
            total = total + dot_tn(r.embedded[h], grads[:, h * LANES : (h + 1) * LANES])
        self.emit(TIN, total)
        self.deal_wait(X_NORM_SUMS, 0, lambda m: r.norm_land.at[m])
        r.small[144 + 4 : 144 + 8] = jnp.sum(r.norm_land[...], axis=0)[0:4]
        r.small[144 + 10 : 160] = jnp.zeros((6, LANES), jnp.float32)

    def grads_out(self):
        r = self.r
        self.emit(SQ4, dot_tn(r.x_last[...], r.g_proj[:, self.mine()]))

    def grads_ffout(self):
        r = self.r
        share = self.dp_size // self.mp_size
        for m in range(self.mp_size):
            part = dot_tn(r.ff_hidden[...], r.g_ffout[:, m * LANES : (m + 1) * LANES])
            r.dw_ffout[m] = part.reshape(share, 4, self.rows, LANES).astype(jnp.bfloat16)
        low = STARTS[FFOUT]
        r.partials[pl.ds(self.me * share, share), low : low + 4] = r.dw_ffout[self.me]
        self.deal(X_DW_FFOUT, 0, lambda m: r.dw_ffout.at[m], lambda m: self.hidden_rows(r.partials, m))

    def grads_ffout_wait(self):
        self.deal_wait(X_DW_FFOUT, 0, lambda m: self.hidden_rows(self.r.partials, m))

    def grads_ffin(self):
        for k in range(8):
            self.emit(FFIN, dot_tn(self.r.ff_in[...], self.r.g_ffin[k]), k)

    def grads_attn(self):
        r = self.r
        self.emit(SQ1, dot_tn(r.x_attn[...], r.g_attn[:, self.mine()]))

    def grads_qkv(self):
        for j in range(3):
            self.emit(QKV, dot_tn(self.r.attn_in[...], self.r.g_qkv[j]), j)

    def grads_in(self):
        r = self.r
        self.emit(SQ0, dot_tn(r.x_norm[...], r.g_in[:, self.mine()]))

    def grads_conv(self):
        r = self.r
        for tap in range(9):
            self.emit(CONV, dot_tn(r.x_res[...], r.g_taps[:, tap * LANES : (tap + 1) * LANES]), tap)


SMALL_ROWS = 168
EXCHANGES = 64


def model_scratch(images, dp_size, mp_size, rows, time_local, hidden_local):
    bf16, f32 = jnp.bfloat16, jnp.float32
    tokens = images * TOKENS
    share = TOKENS // mp_size
    wide = lambda kind: pltpu.VMEM((tokens, C), kind)
    per_image = lambda width, kind=f32: pltpu.VMEM((images, TOKENS, width), kind)
    send = lambda kind: pltpu.VMEM((images, mp_size, share, C), kind)
    tiny = lambda width: pltpu.VMEM((mp_size, 8, width), f32)
    square = lambda: pltpu.VMEM((mp_size, dp_size, rows, LANES), bf16)
    dma = pltpu.SemaphoreType.DMA((EXCHANGES, mp_size))
    link = LINK
    return dict(
        ex_send=dma, ex_recv=dma,
        group_spread=pltpu.VMEM((LANES, LANES), bf16),
        norms_all=pltpu.VMEM((mp_size, 5, 2, LANES), f32),
        context_all=tiny(LANES), time_act=tiny(time_local), cross_val=tiny(LANES), cross_out=tiny(LANES),
        full_mask=pltpu.VMEM((images, PIXELS, LANES), f32), half_mask=per_image(LANES),
        latent8=pltpu.VMEM((8, PIXELS), f32), noise8=pltpu.VMEM((8, PIXELS), f32), lane_mask=pltpu.VMEM((8, PIXELS), f32),
        taps=pltpu.VMEM((72, PIXELS), f32), out_taps=pltpu.VMEM((72, PIXELS), f32),
        first=pltpu.VMEM((images, PIXELS, LANES), f32), merged=pltpu.VMEM((images, PIXELS, LANES), f32),
        last_in=pltpu.VMEM((images, PIXELS, LANES), bf16),
        pooled=per_image(LANES), after_res=per_image(LANES), grad_after=per_image(LANES),
        final_stats=pltpu.VMEM((images, 8, LANES), f32),
        hidden_time=pltpu.VMEM((8, time_local), f32), time_vec=pltpu.VMEM((8, LANES), f32), grad_time=pltpu.VMEM((8, LANES), f32),
        x_res=wide(bf16), x_norm=wide(bf16), x_attn=wide(bf16), x_last=wide(bf16),
        g_proj=wide(bf16), g_ffout=wide(bf16), g_attn=wide(bf16), g_in=wide(bf16),
        attn_in=wide(bf16), ff_in=wide(bf16), ff_hidden=pltpu.VMEM((tokens, hidden_local), bf16),
        stream_in=per_image(C), stream_cross=per_image(C), grad_stream=per_image(C),
        ff_value=per_image(hidden_local), ff_gate=per_image(hidden_local),
        g_hidden=pltpu.VMEM((TOKENS, hidden_local), f32), g_ffin=pltpu.VMEM((8, tokens, LANES), bf16),
        qkv=pltpu.VMEM((3, tokens, LANES), bf16), g_qkv=pltpu.VMEM((3, tokens, LANES), bf16),
        probs=pltpu.VMEM((images, LANES // HD, TOKENS, TOKENS), f32),
        w_in=square(), w_attn=square(), w_out=square(),
        w_ffout=pltpu.VMEM((mp_size, dp_size // mp_size, 4, rows, LANES), bf16),
        dw_ffout=pltpu.VMEM((mp_size, dp_size // mp_size, 4, rows, LANES), bf16),
        ff_send=send(link), ff_land=send(link), gff_send=send(link), gff_land=send(link),
        gat_send=send(link), gat_land=send(link),
        gres_send=pltpu.VMEM((images, mp_size, TOKENS, LANES), link), gres_land=pltpu.VMEM((images, mp_size, TOKENS, LANES), link),
        predicted=pltpu.VMEM((mp_size, 8, PIXELS), f32),
        norm_send=tiny(LANES), norm_land=tiny(LANES),
        gc_part=tiny(C), gv_part=tiny(C), gx_part=tiny(C), gc_full=pltpu.VMEM((8, C), f32),
        dw=pltpu.VMEM((C, LANES), f32), dw_time=pltpu.VMEM((mp_size * time_local, LANES), f32),
        gt_send=tiny(time_local), gt_land=tiny(time_local),
        g_taps=pltpu.VMEM((tokens, 9 * LANES), bf16),
    )


def run_model(model, need, emitted):
    r = model.r
    images = range(model.images)
    model.setup()
    for image in images:
        model.entry(image)
    need(TIN)
    model.time_in()
    need(CONV)
    model.time_out()
    for image in images:
        model.convolve(image)
    need(SQ0)
    model.share_square(SQ0, r.w_in)
    need(SQ1)
    model.share_square(SQ1, r.w_attn)
    need(SQ3)
    model.cross_first()
    model.spread_wait(X_NORMS, 0, r.norms_all, model.whole_slot)
    model.share_square_wait(SQ0, r.w_in)
    for image in images:
        model.attention(image)
    model.cross_second()
    need(FFOUT)
    model.share_ffout()
    model.share_square(SQ4, r.w_out)
    model.share_square_wait(SQ1, r.w_attn)
    model.cross_last()
    model.share_ffout_wait()
    for image in images:
        model.feed(image)
    for image in images:
        model.leave(image)
    for image in images:
        model.finish(image)
    model.predict()
    model.share_square_wait(SQ4, r.w_out)
    model.loss()
    for image in images:
        model.back_last(image)
    model.grads_out()
    for image in images:
        model.back_feed(image)
    model.grads_ffout()
    for image in images:
        model.back_cross(image)
    model.cross_one()
    model.grads_ffin()
    model.grads_ffout_wait()
    emitted(0)
    for image in images:
        model.back_attention(image)
    model.cross_two()
    model.grads_attn()
    model.grads_qkv()
    for image in images:
        model.back_in(image)
    model.cross_three()
    emitted(1)
    for image in images:
        model.back_conv(image)
    model.grads_in()
    model.back_time()
    model.grads_conv()
    emitted(2)
    for image in images:
        model.back_first(image)
    model.cross_four()
    model.back_time_in()
    emitted(3)
    model.drain()


class Refs:
    pass


LINK = jnp.float32
MODEL_INPUTS = ["sides", "share_full", "share_half", "full", "counts_all", "latent", "noise", "embedded", "signal8", "level8", "hot8", "labels8", "context", "norms", "first_w", "last_w"]
MODEL_OUTPUTS = ["partials", "small", "table_rows"]


def model_kernel(images, dp_size, mp_size, names, *refs):
    r = Refs()
    for name, ref in zip(names, refs):
        setattr(r, name, ref)
    place = Place(dp_size, mp_size)
    model = Model(place, r, images, dp_size, mp_size)
    barrier = pltpu.get_barrier_semaphore()
    pl.semaphore_wait(barrier, model.greet(barrier))
    run_model(model, lambda name: None, lambda names: None)


def model_step(images, dp_size, mp_size, inputs):
    vmem = pl.BlockSpec(memory_space=pltpu.VMEM)
    smem = pl.BlockSpec(memory_space=pltpu.SMEM)
    full = inputs[3]
    rows = full.shape[2]
    scratch = model_scratch(images, dp_size, mp_size, rows, 256, 512)
    names = MODEL_INPUTS + MODEL_OUTPUTS + list(scratch)
    return pl.pallas_call(
        functools.partial(model_kernel, images, dp_size, mp_size, names),
        out_shape=(
            jax.ShapeDtypeStruct(full.shape, jnp.bfloat16),
            jax.ShapeDtypeStruct((SMALL_ROWS, LANES), jnp.float32),
            jax.ShapeDtypeStruct((1, 8, LANES), jnp.float32),
        ),
        in_specs=[smem] * 3 + [vmem] * (len(inputs) - 3),
        out_specs=(vmem,) * 3,
        scratch_shapes=list(scratch.values()),
        compiler_params=pltpu.CompilerParams(
            collective_id=3, has_side_effects=True, vmem_limit_bytes=VMEM_LIMIT
        ),
        name="model_step",
    )(*inputs)


def sinusoid(timesteps, embed_dims):
    half_dims = embed_dims // 2
    frequency = jnp.exp(-math.log(10000.0) * jnp.arange(half_dims).astype(jnp.float32) / half_dims)
    angles = timesteps.astype(jnp.float32)[:, None] * frequency[None, :]
    return jnp.concatenate([jnp.cos(angles), jnp.sin(angles)], axis=1)


def adam_step(weight, moment_one, moment_two, gradient, step_rate):
    moment_one_new = beta_one * moment_one + (1 - beta_one) * gradient
    moment_two_new = beta_two * moment_two + (1 - beta_two) * gradient * gradient
    corrected = (
        moment_one_new
        / (1 - beta_one**STEP)
        / (jnp.sqrt(moment_two_new / (1 - beta_two**STEP)) + adam_eps)
    )
    return (weight - step_rate * (corrected + decay * weight), moment_one_new, moment_two_new)


def local(
    clean_latent,
    noise_latent,
    timesteps,
    labels,
    image_sides,
    w_square,
    mom_square,
    w_conv,
    mom_conv,
    w_qkv,
    mom_qkv,
    w_ffin,
    mom_ffin,
    w_ffout,
    mom_ffout,
    w_time_in,
    mom_time_in,
    w_time_out,
    mom_time_out,
    kron_stats,
    class_table,
    table_mean,
    table_var,
    conv_first,
    first_mean,
    first_var,
    conv_last,
    last_mean,
    last_var,
    norm_params,
    norm_mean,
    norm_var,
):
    bf16 = jnp.bfloat16
    dp_size = lax.axis_size(DP)
    mp_size = lax.axis_size(MP)
    count_img = clean_latent.shape[0]
    chans_local = w_square.shape[2]
    rows_of = LAT * count_img
    sides = image_sides.astype(jnp.float32)
    half_sides = (image_sides // 2).astype(jnp.float32)
    share = GROUPS / C
    band_ids = timesteps * NBANDS // steps_total
    band_hot = (band_ids[:, None] == jnp.arange(LANES)[None, :]).astype(jnp.float32)
    pixel_count = LAT * sides * sides
    counts_local = jnp.sum(pixel_count[:, None] * band_hot, axis=0)
    fraction = (timesteps.astype(jnp.float32) + 0.5) / steps_total

    def by_row(values):
        spread = jnp.repeat(jnp.broadcast_to(values, (count_img, LANES)), LAT, axis=0)
        return jnp.pad(spread, ((0, 8 - rows_of), (0, 0)))

    signal8 = by_row(jnp.cos(0.5 * math.pi * fraction)[:, None])
    level8 = by_row(jnp.sin(0.5 * math.pi * fraction)[:, None])
    embedded = sinusoid(timesteps, TE)
    halves = w_time_in.shape[1] // LANES
    embedded = embedded[None, :, :, None] * jnp.eye(halves)[:, None, None, :]
    embedded = jnp.pad(embedded.reshape(halves, count_img, -1), ((0, 0), (0, 8 - count_img), (0, 0))).astype(bf16)
    context = jnp.take(class_table, labels, axis=0).astype(bf16).astype(jnp.float32)
    context = jnp.pad(context, ((0, 8 - count_img), (0, 0)))
    labels8 = jnp.broadcast_to(labels.astype(jnp.float32)[:, None], (count_img, LANES))
    labels8 = jnp.pad(labels8, ((count_img, 8 - 2 * count_img), (0, 0)))

    def by_tap(kernel):
        kernel = kernel.astype(bf16)
        return jnp.stack(
            [
                jnp.pad(kernel, ((0, 0), (LAT * k, 8 - LAT * k - LAT), (0, 0))).reshape(72, LANES)
                for k in range(count_img)
            ]
        )

    packed = pack(w_square, w_conv, w_qkv, w_ffin, w_ffout, w_time_in, w_time_out)
    full, counts_all = gather_weights(
        dp_size, mp_size, packed.astype(bf16), jnp.pad(counts_local[None, None], ((0, 0), (0, 7), (0, 0)))
    )
    partials, small, table_rows = model_step(
        count_img,
        dp_size,
        mp_size,
        [
            image_sides,
            share / (sides * sides),
            share / (half_sides * half_sides),
            full,
            counts_all,
            clean_latent,
            noise_latent,
            embedded,
            signal8,
            level8,
            by_row(band_hot),
            labels8,
            context,
            norm_params,
            by_tap(conv_first),
            by_tap(conv_last.transpose(0, 2, 1)),
        ],
    )
    momenta = pack(mom_square, mom_conv, mom_qkv, mom_ffin, mom_ffout, mom_time_in, mom_time_out)
    packed_new, packed_mom, renewed, small_all, rows_all = reduce_and_update(
        dp_size, mp_size, partials, small, table_rows, packed, momenta, kron_stats
    )
    shapes = (w_square, w_conv, w_qkv, w_ffin, w_ffout, w_time_in, w_time_out)
    results = []
    for new, moment in zip(unpack(packed_new, *shapes), unpack(packed_mom, *shapes)):
        results += [new, moment]

    def taps_of(rows):
        rows = rows.reshape(9, 8, chans_local)
        return sum(rows[:, LAT * k : LAT * k + LAT] for k in range(count_img))

    grad_first_all = taps_of(small_all[:72])
    grad_last_all = taps_of(small_all[72:144]).transpose(0, 2, 1)
    grad_norm_all = small_all[144:154].reshape(5, 2, chans_local)
    band_all = small_all[160, :NBANDS]
    counts = jnp.sum(counts_all[:, 0, 0, :NBANDS], axis=0)
    label_all = rows_all[:, 0, count_img : 2 * count_img, 0].reshape(1, -1)
    hot = (jnp.arange(NCLS).astype(jnp.float32)[:, None] == label_all).astype(jnp.float32)
    grad_table_all = jnp.dot(hot, rows_all[:, 0, :count_img].reshape(-1, chans_local), precision=highest)
    table_out = adam_step(class_table, table_mean, table_var, grad_table_all, rate_table)
    first_out = adam_step(conv_first, first_mean, first_var, grad_first_all, rate_first)
    last_out = adam_step(conv_last, last_mean, last_var, grad_last_all, rate_last)
    norm_out = adam_step(norm_params, norm_mean, norm_var, grad_norm_all, rate_gain)
    loss_terms = jnp.stack([band_all, counts])
    return (
        results[0],
        results[1],
        results[2],
        results[3],
        results[4],
        results[5],
        results[6],
        results[7],
        results[8],
        results[9],
        results[10],
        results[11],
        results[12],
        results[13],
        renewed,
        table_out[0],
        table_out[1],
        table_out[2],
        first_out[0],
        first_out[1],
        first_out[2],
        last_out[0],
        last_out[1],
        last_out[2],
        norm_out[0],
        norm_out[1],
        norm_out[2],
        loss_terms,
    )


def solution(mesh):
    return jax.shard_map(
        local,
        mesh=mesh,
        in_specs=(
            P(DP, None, None),
            P(DP, None, None),
            P(DP),
            P(DP),
            P(DP),
            P(None, DP, MP),
            P(None, DP, MP),
            P(None, DP, MP),
            P(None, DP, MP),
            P(DP, None, MP),
            P(DP, None, MP),
            P(DP, None, MP),
            P(DP, None, MP),
            P(DP, MP),
            P(DP, MP),
            P(DP, MP),
            P(DP, MP),
            P(DP, MP),
            P(DP, MP),
            P(MP, None, None),
            P(None, MP),
            P(None, MP),
            P(None, MP),
            P(None, None, MP),
            P(None, None, MP),
            P(None, None, MP),
            P(None, MP, None),
            P(None, MP, None),
            P(None, MP, None),
            P(None, None, MP),
            P(None, None, MP),
            P(None, None, MP),
        ),
        out_specs=(
            P(None, DP, MP),
            P(None, DP, MP),
            P(None, DP, MP),
            P(None, DP, MP),
            P(DP, None, MP),
            P(DP, None, MP),
            P(DP, None, MP),
            P(DP, None, MP),
            P(DP, MP),
            P(DP, MP),
            P(DP, MP),
            P(DP, MP),
            P(DP, MP),
            P(DP, MP),
            P(MP, None, None),
            P(None, MP),
            P(None, MP),
            P(None, MP),
            P(None, None, MP),
            P(None, None, MP),
            P(None, None, MP),
            P(None, MP, None),
            P(None, MP, None),
            P(None, MP, None),
            P(None, None, MP),
            P(None, None, MP),
            P(None, None, MP),
            P(),
        ),
        check_vma=False,
    )
```

```python
import functools
import math

import jax
import jax.numpy as jnp
from jax import lax
from jax.experimental import pallas as pl
from jax.experimental.pallas import tpu as pltpu
from jax.sharding import PartitionSpec as P

C = 512
GROUPS = 32
HD = 64
TE = 256
NCLS = 1000
LAT = 3
SIDE = 32
NBANDS = 4
NS_ITERS = 6
STEP = 5


LINK = jnp.float32
norm_eps = 1e-05
steps_total = 1000
beta_one = 0.9
beta_two = 0.95
adam_eps = 1e-08
decay = 0.01
shampoo_momentum = 0.9
shampoo_beta = 0.95
shampoo_rate = 0.5
rate_table = 0.5
rate_first = 0.2
rate_last = 0.015
rate_gain = 0.1
score_scale = 0.125
masked_score = -1000000000.0


DP, MP = "dp", "mp"
MESH_ID = pl.DeviceIdType.MESH
VMEM_LIMIT = 60 * 1024 * 1024


def remote(src, dst, send_sem, recv_sem, device):
    return pltpu.make_async_remote_copy(
        src_ref=src, dst_ref=dst, send_sem=send_sem, recv_sem=recv_sem, device_id=device, device_id_type=MESH_ID
    )


def steps(low, high, body):
    if high - low <= 8:
        for index in range(low, high):
            body(index)
    else:
        lax.fori_loop(low, high, lambda index, carry: (body(index), carry)[1], 0)


class Place:
    def __init__(self, dp_size, mp_size):
        self.dp_size = dp_size
        self.mp_size = mp_size
        self.outer_size = dp_size // 2
        self.dp = lax.axis_index(DP)
        self.mp = lax.axis_index(MP)
        self.outer = self.dp // 2
        self.inner = lax.rem(self.dp, 2)

    def at(self, outer, inner):
        return outer * 2 + inner

    def ahead(self, step):
        return lax.rem(self.outer + step, self.outer_size)

    def behind(self, step):
        return lax.rem(self.outer + self.outer_size - step, self.outer_size)

    def partner(self):
        return (self.at(self.outer, 1 - self.inner), self.mp)

    def across(self, step):
        return (self.at(self.ahead(step), self.inner), self.mp)

    def greet_dp(self, barrier):
        pl.semaphore_signal(barrier, inc=1, device_id=self.partner(), device_id_type=MESH_ID)

        def one(step):
            pl.semaphore_signal(barrier, inc=1, device_id=self.across(step), device_id_type=MESH_ID)

        steps(1, self.outer_size, one)
        return self.outer_size


class Gather:
    def __init__(self, place, shard, full, sems, pieces):
        self.place = place
        self.shard = shard
        self.full = full
        self.out_send, self.out_recv, self.in_send, self.in_recv = sems
        self.pieces = pieces

    @staticmethod
    def sems(place_outer, count):
        return [pltpu.SemaphoreType.DMA((count, place_outer))] * 4

    def part(self, ref, piece):
        low, count = self.pieces[piece]
        return ref.at[pl.ds(low, count)]

    def slot(self, source, piece):
        low, count = self.pieces[piece]
        return self.full.at[source, pl.ds(low, count)]

    def out_copy(self, piece, step, source):
        return remote(
            self.part(self.shard, piece),
            self.slot(source, piece),
            self.out_send.at[piece, step],
            self.out_recv.at[piece, step],
            self.place.across(step),
        )

    def in_copy(self, piece, step, source, src=None):
        return remote(
            self.slot(source, piece) if src is None else src,
            self.slot(source, piece),
            self.in_send.at[piece, step],
            self.in_recv.at[piece, step],
            self.place.partner(),
        )

    def start(self, piece):
        place = self.place
        steps(1, place.outer_size, lambda step: self.out_copy(piece, step, place.dp).start())
        self.in_copy(piece, 0, place.dp, self.part(self.shard, piece)).start()

    def pump(self, piece):
        place = self.place

        def one(step):
            source = place.at(place.behind(step), place.inner)
            self.out_copy(piece, step, source).wait_recv()
            self.in_copy(piece, step, source).start()

        steps(1, place.outer_size, one)

    def ready(self, piece):
        place = self.place

        def one(step):
            source = place.at(place.behind(step), 1 - place.inner)
            self.in_copy(piece, step, source).wait_recv()

        steps(0, place.outer_size, one)

    def drain(self, piece):
        place = self.place
        steps(1, place.outer_size, lambda step: self.out_copy(piece, step, place.dp).wait_send())
        self.in_copy(piece, 0, place.dp, self.part(self.shard, piece)).wait_send()

        def one(step):
            source = place.at(place.behind(step), place.inner)
            self.in_copy(piece, step, source).wait_send()

        steps(1, place.outer_size, one)


class Scatter:
    def __init__(self, place, partials, total, near, sums, far, sems, pieces):
        self.place = place
        self.partials = partials
        self.total = total
        self.near = near
        self.sums = sums
        self.far = far
        self.in_send, self.in_recv, self.out_send, self.out_recv = sems
        self.pieces = pieces

    def cut(self, ref, index, piece):
        low, count = self.pieces[piece]
        return ref.at[index, pl.ds(low, count)]

    def in_copy(self, piece, step):
        place = self.place
        return remote(
            self.cut(self.partials, place.at(place.ahead(step), 1 - place.inner), piece),
            self.cut(self.near, step, piece),
            self.in_send.at[piece, step],
            self.in_recv.at[piece, step],
            place.partner(),
        )

    def out_copy(self, piece, step):
        return remote(
            self.cut(self.sums, step, piece),
            self.cut(self.far, step, piece),
            self.out_send.at[piece, step],
            self.out_recv.at[piece, step],
            self.place.across(step),
        )

    def start(self, piece):
        last = self.place.outer_size
        steps(1, last, lambda step: self.in_copy(piece, step).start())
        self.in_copy(piece, 0).start()

    def pump(self, piece):
        place = self.place
        low, count = self.pieces[piece]

        def one(step):
            self.in_copy(piece, step).wait_recv()
            mine = self.partials[place.at(place.ahead(step), place.inner), pl.ds(low, count)]
            theirs = self.near[step, pl.ds(low, count)]
            self.sums[step, pl.ds(low, count)] = (
                mine.astype(jnp.float32) + theirs.astype(jnp.float32)
            ).astype(jnp.bfloat16)
            self.out_copy(piece, step).start()

        steps(1, place.outer_size, one)
        self.in_copy(piece, 0).wait_recv()
        self.total[pl.ds(low, count)] = self.partials[
            place.dp, pl.ds(low, count)
        ].astype(jnp.float32) + self.near[0, pl.ds(low, count)].astype(jnp.float32)

    def finish(self, piece):
        low, count = self.pieces[piece]

        def one(step):
            self.out_copy(piece, step).wait_recv()
            self.total[pl.ds(low, count)] += self.far[step, pl.ds(low, count)].astype(jnp.float32)

        steps(1, self.place.outer_size, one)

    def drain(self, piece):
        last = self.place.outer_size
        steps(0, last, lambda step: self.in_copy(piece, step).wait_send())
        steps(1, last, lambda step: self.out_copy(piece, step).wait_send())


def split(values):
    high = values.astype(jnp.bfloat16)
    return high, (values - high.astype(jnp.float32)).astype(jnp.bfloat16)


def dot_nn(left, right):
    return lax.dot_general(left, right, (((1,), (0,)), ((), ())), preferred_element_type=jnp.float32)


def dot_tn(left, right):
    return lax.dot_general(left, right, (((0,), (0,)), ((), ())), preferred_element_type=jnp.float32)


def dot_nt(left, right):
    return lax.dot_general(left, right, (((1,), (1,)), ((), ())), preferred_element_type=jnp.float32)


def exact(left, right):
    left_high, left_low = split(left)
    right_high, right_low = split(right)
    return dot_nn(left_high, right_high) + (dot_nn(left_high, right_low) + dot_nn(left_low, right_high))


def gram_of(values):
    high, low = split(values)
    cross = dot_tn(high, low)
    return dot_tn(high, high) + (cross + cross.T)


TIN, TOUT, SQ0, CONV, QKV, SQ1, SQ2, SQ3, FFOUT, FFIN, SQ4 = range(11)
SQUARES = (SQ0, SQ1, SQ2, SQ3, SQ4)
COUNTS = {TIN: 1, TOUT: 2, SQ0: 1, CONV: 9, QKV: 3, SQ1: 1, SQ2: 1, SQ3: 1, FFOUT: 4, FFIN: 8, SQ4: 1}
STARTS = {name: sum(COUNTS[other] for other in range(name)) for name in COUNTS}
SECTION_COUNT = sum(COUNTS.values())
GATHER_PIECES = ((0, 4), (4, 3), (7, 3), (10, 3), (13, 6), (19, 4), (23, 4), (27, 5))
SCATTER_PIECES = ((31, 1), (27, 4), (23, 4), (19, 4), (13, 4), (17, 2), (3, 1), (4, 3), (7, 3), (10, 3), (0, 3))
BLOCKS = (
    tuple((STARTS[name], 1) for name in SQUARES)
    + ((STARTS[CONV], 9),)
    + tuple((STARTS[QKV] + k, 1) for k in range(3))
    + tuple((STARTS[FFIN] + k, 1) for k in range(8))
    + ((STARTS[FFOUT], 4), (STARTS[TIN], 1), (STARTS[TIN], 1), (STARTS[TOUT], 2))
)
ORDER = (4, 9, 10, 11, 12, 13, 14, 15, 16, 17, 3, 2, 1, 6, 7, 8, 0, 20, 5, 18, 19)
TIN_BLOCKS = (18, 19)
BY_GRAM = (5, 17, 20)


def inverse_roots(matrices):
    size = matrices[0].shape[-1]
    rows = lax.broadcasted_iota(jnp.int32, (size, size), 0)
    columns = lax.broadcasted_iota(jnp.int32, (size, size), 1)
    identity = (rows == columns).astype(jnp.float32)
    traces = [jnp.sum(matrix * identity) for matrix in matrices]
    current = [matrix * (1.0 / trace) for matrix, trace in zip(matrices, traces)]
    inverse = [identity for _ in matrices]
    for sweep in range(NS_ITERS):
        if sweep == 0:
            middle = [1.5 * identity - 0.5 * c for c in current]
            inverse = middle
        else:
            middle = [1.5 * identity - 0.5 * exact(z, c) for z, c in zip(inverse, current)]
            inverse = [exact(m, z) for m, z in zip(middle, inverse)]
        if sweep < NS_ITERS - 1:
            current = [exact(c, m) for c, m in zip(current, middle)]
    return [z * lax.rsqrt(jnp.full((1, size), trace, jnp.float32)) for z, trace in zip(inverse, traces)]


MID = SIDE // 2
TOKENS = MID * MID
PIXELS = SIDE * SIDE
LANES = 128


def sigmoid(values):
    return 1.0 / (1.0 + jnp.exp(-values))


ERF_TOP = (-2.72614225801306e-10, 2.77068142495902e-08, -2.10102402082508e-06, -5.69250639462346e-05, -7.34990630326855e-04, -2.95459980854025e-03, -1.60960333262415e-02)
ERF_LOW = (-1.45660718464996e-05, -2.13374055278905e-04, -1.68282697438203e-03, -7.37332916720468e-03, -1.42647390514189e-02)


def erf(values):
    values = jnp.clip(values, -4.0, 4.0)
    square = values * values
    top = jnp.full_like(square, ERF_TOP[0])
    for factor in ERF_TOP[1:]:
        top = top * square + factor
    low = jnp.full_like(square, ERF_LOW[0])
    for factor in ERF_LOW[1:]:
        low = low * square + factor
    return values * top / low


def group_sums(rows, spread):
    parts = []
    for row in rows:
        for _ in range(3):
            high = row.astype(jnp.bfloat16)
            parts.append(high)
            row = row - high.astype(jnp.float32)
    parts.append(jnp.zeros((16 - len(parts), LANES), jnp.bfloat16))
    summed = dot_nn(jnp.concatenate([part.astype(jnp.float32) for part in parts], axis=0).astype(jnp.bfloat16), spread)
    return [jnp.sum(summed[3 * k : 3 * k + 3], axis=0, keepdims=True) for k in range(len(rows))]


def column_sum(values):
    return jnp.sum(values, axis=0, keepdims=True)


def norm_stats(values, mask, share, spread):
    centre = group_sums([column_sum(values * mask)], spread)[0] * share
    off = (values - centre) * mask
    variance = group_sums([column_sum(off * off)], spread)[0] * share
    return centre, lax.rsqrt(variance + norm_eps)


def norm_backward(grads, normal, inv_std, mask, gain, share, spread):
    bias_grad = column_sum(grads)
    gain_grad = column_sum(grads * normal)
    first, second = group_sums([bias_grad * gain, gain_grad * gain], spread)
    return (
        inv_std * (grads * gain - mask * (first * share + normal * (second * share))),
        gain_grad,
        bias_grad,
    )


def token_norm(values, gain, bias):
    centre = jnp.mean(values, axis=-1, keepdims=True)
    variance = jnp.mean(values * values, axis=-1, keepdims=True) - centre * centre
    inv_std = lax.rsqrt(variance + norm_eps)
    normal = (values - centre) * inv_std
    return normal * gain + bias, normal, inv_std


def token_norm_backward(grads, normal, inv_std, gain):
    scaled = grads * gain
    width = grads.shape[-1]
    first = jnp.sum(scaled, axis=-1, keepdims=True) * (1.0 / width)
    second = jnp.sum(scaled * normal, axis=-1, keepdims=True) * (1.0 / width)
    return (scaled - first - normal * second) * inv_std, column_sum(grads * normal), column_sum(grads)


def shift_rows(values, rows):
    if rows == 0:
        return values
    count = abs(rows) * MID
    zeros = jnp.zeros((count, values.shape[1]), values.dtype)
    if rows > 0:
        return jnp.concatenate([values[count:], zeros], axis=0)
    return jnp.concatenate([zeros, values[:-count]], axis=0)


(X_NORMS, X_CONTEXT, X_TIME, X_RES, X_NORM, X_FFOUT_W, X_CROSS_VAL, X_CROSS_OUT, X_ATTN, X_FF, X_LAST, X_PREDICTED, X_G_PROJ, X_G_FF, X_GC, X_GV, X_GX, X_G_ATTN, X_G_AT, X_G_IN, X_G_RES, X_GT, X_NORM_SUMS, X_DW_FFOUT) = range(100, 124)


def turn(angle):
    quarter = jnp.floor(angle * (2.0 / math.pi) + 0.5)
    rest = angle - quarter * 1.5703125
    rest = rest - quarter * 4.837512969970703e-04
    rest = rest - quarter * 7.549789948768648e-08
    square = rest * rest
    sine = ((-1.9515295891e-04 * square + 8.3321608736e-03) * square - 1.6666654611e-01) * square * rest + rest
    cosine = ((2.443315711809948e-05 * square - 1.388731625493765e-03) * square + 4.166664568298827e-02) * square
    cosine = cosine * square - 0.5 * square + 1.0
    turns = quarter - 4.0 * jnp.floor(quarter * 0.25)
    odd = (turns == 1.0) | (turns == 3.0)
    first, second = jnp.where(odd, sine, cosine), jnp.where(odd, cosine, sine)
    return (
        jnp.where((turns == 1.0) | (turns == 2.0), -first, first),
        jnp.where(turns >= 2.0, -second, second),
    )


class Model:
    def __init__(self, place, refs, images, dp_size, mp_size):
        self.place = place
        self.r = refs
        self.images = images
        self.dp_size = dp_size
        self.mp_size = mp_size
        self.rows = refs.full.shape[2]
        self.me = place.mp
        self.exchange_ids = {}
        self.pending = []

    def peer(self, step):
        return (self.place.dp, lax.rem(self.me + step, self.mp_size))

    def source(self, step):
        return lax.rem(self.me + self.mp_size - step, self.mp_size)

    def index_of(self, name, part):
        key = (name, part)
        if key not in self.exchange_ids:
            self.exchange_ids[key] = len(self.exchange_ids)
        return self.exchange_ids[key]

    def spread(self, name, part, ref, cut):
        index = self.index_of(name, part)
        for step in range(1, self.mp_size):
            copy = remote(
                cut(ref, self.me), cut(ref, self.me), self.r.ex_send.at[index, step], self.r.ex_recv.at[index, step], self.peer(step)
            )
            copy.start()
            self.pending.append(copy)

    def spread_wait(self, name, part, ref, cut):
        index = self.index_of(name, part)
        for step in range(1, self.mp_size):
            region = cut(ref, self.source(step))
            remote(region, region, self.r.ex_send.at[index, step], self.r.ex_recv.at[index, step], self.peer(step)).wait_recv()

    def deal(self, name, part, out, land):
        index = self.index_of(name, part)
        for step in range(1, self.mp_size):
            target = lax.rem(self.me + step, self.mp_size)
            copy = remote(
                out(target), land(self.me), self.r.ex_send.at[index, step], self.r.ex_recv.at[index, step], self.peer(step)
            )
            copy.start()
            self.pending.append(copy)

    def deal_wait(self, name, part, land):
        index = self.index_of(name, part)
        for step in range(1, self.mp_size):
            region = land(self.source(step))
            remote(region, region, self.r.ex_send.at[index, step], self.r.ex_recv.at[index, step], self.peer(step)).wait_recv()

    def drain(self):
        for copy in self.pending:
            copy.wait_send()

    def greet(self, barrier):
        for step in range(1, self.mp_size):
            pl.semaphore_signal(barrier, inc=1, device_id=self.peer(step), device_id_type=MESH_ID)
        return self.mp_size - 1

    def flat(self, values):
        width = values.shape[-1]
        count = math.prod(values.shape[:-1])
        if values.shape[-2] % 16 == 0:
            return values.reshape(count, width)
        return values.astype(jnp.float32).reshape(count, width).astype(jnp.bfloat16)

    def weight(self, name, k=0):
        return self.flat(self.r.full[:, STARTS[name] + k])

    def weight_rows(self, name, count):
        return self.flat(self.r.full[:, STARTS[name] : STARTS[name] + count])

    def emit(self, name, values, k=0):
        self.r.partials[:, STARTS[name] + k] = values.reshape(self.dp_size, self.rows, LANES).astype(jnp.bfloat16)

    def emit_rows(self, name, values, count):
        low = STARTS[name]
        self.r.partials[:, low : low + count] = values.reshape(self.dp_size, count, self.rows, LANES).astype(jnp.bfloat16)

    def wide(self, ref, m):
        return self.flat(ref[m])

    def wide_mine(self, ref, m):
        share = self.dp_size // self.mp_size
        return self.flat(ref[m, pl.ds(self.me * share, share)])

    def columns(self, image):
        return lambda ref, m: ref.at[pl.ds(image * TOKENS, TOKENS), pl.ds(pl.multiple_of(m * LANES, LANES), LANES)]

    def token_rows(self, image):
        share = TOKENS // self.mp_size
        return lambda ref, m: ref.at[pl.ds(pl.multiple_of(image * TOKENS + m * share, share), share)]

    def mine(self):
        return pl.ds(pl.multiple_of(self.me * LANES, LANES), LANES)

    def my_tokens(self):
        share = TOKENS // self.mp_size
        return pl.ds(pl.multiple_of(self.me * share, share), share)

    def image_rows(self, image):
        return pl.ds(image * TOKENS, TOKENS)

    @staticmethod
    def whole_slot(ref, m):
        return ref.at[m]

    def across_lanes(self, image):
        key = lax.broadcasted_iota(jnp.int32, (1, TOKENS), 1)
        side = self.r.sides[image] // 2
        return (key // MID < side) & (lax.rem(key, MID) < side)

    def full_lane(self, norm, which):
        return jnp.concatenate([self.r.norms_all[m, norm, which : which + 1] for m in range(self.mp_size)], axis=1)

    def gain(self, norm):
        return self.r.norms[norm, 0:1]

    def bias(self, norm):
        return self.r.norms[norm, 1:2]

    def tap_lanes(self, values, tap):
        i, j = divmod(tap, 3)
        offset = (i - 1) * SIDE + (j - 1)
        moved = values if offset == 0 else pltpu.roll(values, (-offset) % PIXELS, 1)
        pixel = lax.broadcasted_iota(jnp.int32, values.shape, 1)
        row, column = pixel // SIDE + (i - 1), lax.rem(pixel, SIDE) + (j - 1)
        inside = (row >= 0) & (row < SIDE) & (column >= 0) & (column < SIDE)
        return jnp.where(inside, moved, 0.0)

    def greet_all(self, barrier):
        for step in range(1, self.mp_size):
            pl.semaphore_signal(barrier, inc=1, device_id=self.peer(step), device_id_type=MESH_ID)

        def hello(step):
            other = lax.rem(self.place.dp + step, self.dp_size)
            pl.semaphore_signal(barrier, inc=1, device_id=(other, self.me), device_id_type=MESH_ID)

        steps(1, self.dp_size, hello)
        pl.semaphore_wait(barrier, self.mp_size + self.dp_size - 2)

    def pack(self):
        r = self.r
        bf16 = jnp.bfloat16
        rows = self.rows
        for h in range(r.w_tin.shape[1] // LANES):
            stride = r.w_tin.shape[1] // LANES
            r.tin_rows[pl.ds(h, rows // stride, stride=stride)] = r.w_tin[:, h * LANES : (h + 1) * LANES]
        r.shard[STARTS[TIN]] = r.tin_rows[...].astype(bf16)
        r.shard[STARTS[TOUT] : STARTS[TOUT] + 2] = r.w_tout[...].reshape(2, rows, LANES).astype(bf16)
        for k, name in enumerate(SQUARES):
            r.shard[STARTS[name]] = r.w_square[k].astype(bf16)
        r.shard[STARTS[CONV] : STARTS[CONV] + 9] = r.w_conv[...].astype(bf16)
        for j in range(3):
            r.shard[STARTS[QKV] + j] = r.w_qkv[:, j, :].astype(bf16)
        r.shard[STARTS[FFOUT] : STARTS[FFOUT] + 4] = r.w_fo[...].reshape(4, rows, LANES).astype(bf16)
        for j in range(2):
            for k in range(4):
                r.shard[STARTS[FFIN] + 4 * j + k] = r.w_fi[:, j, k * LANES : (k + 1) * LANES].astype(bf16)

    def by_row(self, values):
        row = lax.broadcasted_iota(jnp.int32, (8, LANES), 0) // LAT
        total = jnp.zeros((8, LANES), jnp.float32)
        for image in range(self.images):
            total = jnp.where(row == image, values[image], total)
        return total

    def share(self, image, halves):
        side = self.r.sides[image] // halves
        return (GROUPS / C) / jnp.full((1, LANES), side * side, jnp.int32).astype(jnp.float32)

    def prepare(self):
        r = self.r
        images = range(self.images)
        lane = lax.broadcasted_iota(jnp.int32, (8, LANES), 1)
        row = lax.broadcasted_iota(jnp.int32, (8, LANES), 0)
        hot = [(lane[0:1] == r.timesteps[k] * NBANDS // steps_total).astype(jnp.float32) for k in images]
        r.hot8[...] = self.by_row(hot)
        counts = jnp.zeros((1, LANES), jnp.float32)
        for k in images:
            side = r.sides[k]
            counts = counts + hot[k] * jnp.full((1, LANES), LAT * side * side, jnp.int32).astype(jnp.float32)
        r.counts[0] = jnp.where(row == 0, counts, 0.0)
        times = [jnp.full((1, LANES), r.timesteps[k], jnp.int32).astype(jnp.float32) for k in images]
        angle = (0.5 * math.pi / steps_total) * (self.by_row(times) + 0.5)
        cosine, sine = turn(angle)
        r.signal8[...] = cosine
        r.level8[...] = sine
        labels = jnp.zeros((8, LANES), jnp.float32)
        for k in images:
            label = jnp.full((8, LANES), r.labels[k], jnp.int32).astype(jnp.float32)
            labels = jnp.where(row == self.images + k, label, labels)
        r.labels8[...] = labels
        r.context[...] = jnp.zeros((8, LANES), jnp.float32)
        for k in images:
            chosen = r.class_table[pl.ds(r.labels[k], 1), :]
            r.context[k : k + 1] = chosen.astype(jnp.bfloat16).astype(jnp.float32)
        halves = r.embedded.shape[0]
        width = TE * halves
        place = lax.broadcasted_iota(jnp.int32, (8, width), 1)
        channel = place // halves
        half = TE // 2
        frequency = jnp.exp((-math.log(10000.0) / half) * lax.rem(channel, half).astype(jnp.float32))
        row = lax.broadcasted_iota(jnp.int32, (8, width), 0)
        time = jnp.zeros((8, width), jnp.float32)
        for k in images:
            time = jnp.where(row == k, jnp.full((8, width), r.timesteps[k], jnp.int32).astype(jnp.float32), time)
        cosine, sine = turn(time * frequency)
        values = jnp.where(channel < half, cosine, sine)
        for h in range(halves):
            r.embedded[h] = jnp.where((row < self.images) & (lax.rem(place, halves) == h), values, 0.0).astype(jnp.bfloat16)
        r.first_f[...] = jnp.zeros(r.first_f.shape, jnp.float32)
        r.last_f[...] = jnp.zeros(r.last_f.shape, jnp.float32)
        for image in images:
            for tap in range(9):
                low = 8 * tap + LAT * image
                r.first_f[image, low : low + LAT] = r.conv_first[tap]
                r.last_f[image, low : low + LAT] = r.conv_last[tap]
            r.first_w[image] = r.first_f[image].astype(jnp.bfloat16)
            r.last_w[image] = r.last_f[image].astype(jnp.bfloat16)

    def setup(self):
        r = self.r
        lane = lax.broadcasted_iota(jnp.int32, (LANES, LANES), 1) // (C // GROUPS)
        row = lax.broadcasted_iota(jnp.int32, (LANES, LANES), 0) // (C // GROUPS)
        r.group_spread[...] = (lane == row).astype(jnp.bfloat16)
        r.norms_all[self.me] = r.norms[...]
        self.spread(X_NORMS, 0, r.norms_all, self.whole_slot)
        r.context_all[self.me] = r.context[...]
        self.spread(X_CONTEXT, 0, r.context_all, self.whole_slot)
        for image in range(self.images):
            side = r.sides[image]
            pixel = lax.broadcasted_iota(jnp.int32, (PIXELS, LANES), 0)
            r.full_mask[image] = ((pixel // SIDE < side) & (lax.rem(pixel, SIDE) < side)).astype(jnp.float32)
            half = side // 2
            token = lax.broadcasted_iota(jnp.int32, (TOKENS, LANES), 0)
            r.half_mask[image] = ((token // MID < half) & (lax.rem(token, MID) < half)).astype(jnp.float32)
        for image in range(self.images):
            r.latent8[LAT * image : LAT * image + LAT] = r.latent[image]
            r.noise8[LAT * image : LAT * image + LAT] = r.noise[image]
        rest = LAT * self.images
        r.latent8[rest:] = jnp.zeros((8 - rest, PIXELS), jnp.float32)
        r.noise8[rest:] = jnp.zeros((8 - rest, PIXELS), jnp.float32)
        lane_row = lax.broadcasted_iota(jnp.int32, (8, PIXELS), 0)
        pixel = lax.broadcasted_iota(jnp.int32, (8, PIXELS), 1)
        side = jnp.zeros((8, PIXELS), jnp.int32)
        for image in range(self.images):
            side = jnp.where(lane_row // LAT == image, r.sides[image], side)
        r.lane_mask[...] = ((pixel // SIDE < side) & (lax.rem(pixel, SIDE) < side)).astype(jnp.float32)
        signal, level = r.signal8[:, 0:1], r.level8[:, 0:1]
        noisy = (signal * r.latent8[...] + level * r.noise8[...]) * r.lane_mask[...]
        noisy = noisy.astype(jnp.bfloat16).astype(jnp.float32)
        for tap in range(9):
            r.taps[8 * tap : 8 * tap + 8] = self.tap_lanes(noisy, tap)

    def entry(self, image):
        r = self.r
        first = dot_tn(r.taps[...].astype(jnp.bfloat16), r.first_w[image]) * r.full_mask[image]
        r.first[image] = first
        paired = r.first[image, pl.ds(0, PIXELS // 2, stride=2)] + r.first[image, pl.ds(1, PIXELS // 2, stride=2)]
        pooled = jnp.sum(paired.reshape(MID, 2, MID, LANES), axis=1).reshape(TOKENS, LANES) * 0.25
        r.pooled[image] = pooled
        mask = r.half_mask[image]
        centre, inv_std = norm_stats(pooled, mask, self.share(image, 2), r.group_spread[...])
        values = (pooled - centre) * inv_std * self.gain(0) + self.bias(0)
        r.x_res[self.image_rows(image), self.mine()] = (values * sigmoid(values) * mask).astype(jnp.bfloat16)
        self.spread(X_RES, image, r.x_res, self.columns(image))

    def time_in(self):
        r = self.r
        table = self.weight(TIN)
        hidden = jnp.concatenate([dot_nn(r.embedded[h], table) for h in range(r.embedded.shape[0])], axis=1)
        r.hidden_time[...] = hidden
        r.time_act[self.me] = (hidden * sigmoid(hidden)).astype(jnp.bfloat16).astype(jnp.float32)
        self.spread(X_TIME, 0, r.time_act, self.whole_slot)

    def time_out(self):
        r = self.r
        self.spread_wait(X_TIME, 0, r.time_act, self.whole_slot)
        table = self.weight_rows(TOUT, 2)
        width = r.time_act.shape[2]
        total = 0.0
        for m in range(self.mp_size):
            total = total + dot_nn(r.time_act[m].astype(jnp.bfloat16), table[m * width : (m + 1) * width])
        r.time_vec[...] = total

    def res_wait(self, image):
        self.spread_wait(X_RES, image, self.r.x_res, self.columns(image))

    def convolve(self, image, i):
        r = self.r
        values = r.x_res[self.image_rows(image), :]
        for j in range(3):
            moved = shift_rows(dot_nn(values, self.weight(CONV, 3 * i + j)), i - 1)
            if i > 0:
                moved = r.conv_sum[image, j] + moved
            r.conv_sum[image, j] = moved

    def convolved(self, image):
        r = self.r
        column = lax.rem(lax.broadcasted_iota(jnp.int32, (TOKENS, LANES), 0), MID)
        total = r.conv_sum[image, 1]
        total = total + jnp.where(column > 0, pltpu.roll(r.conv_sum[image, 0], 1, 0), 0.0)
        total = total + jnp.where(column < MID - 1, pltpu.roll(r.conv_sum[image, 2], TOKENS - 1, 0), 0.0)
        mask = r.half_mask[image]
        after = r.pooled[image] + (total + r.time_vec[image : image + 1]) * mask
        r.after_res[image] = after
        centre, inv_std = norm_stats(after, mask, self.share(image, 2), r.group_spread[...])
        values = (after - centre) * inv_std * self.gain(1) + self.bias(1)
        r.x_norm[self.image_rows(image), self.mine()] = (values * mask).astype(jnp.bfloat16)
        self.spread(X_NORM, image, r.x_norm, self.columns(image))

    def share_square(self, name, ref):
        low = STARTS[name]
        ref[self.me] = self.r.full[:, low]
        index = self.index_of(name, 0)
        for step in range(1, self.mp_size):
            copy = remote(
                self.r.full.at[:, low], ref.at[self.me], self.r.ex_send.at[index, step], self.r.ex_recv.at[index, step], self.peer(step)
            )
            copy.start()
            self.pending.append(copy)

    def share_square_wait(self, name, ref):
        self.spread_wait(name, 0, ref, self.whole_slot)

    def hidden_rows(self, ref, m):
        share = self.dp_size // self.mp_size
        low = STARTS[FFOUT]
        return ref.at[pl.ds(m * share, share), pl.ds(low, 4)]

    def share_ffout(self):
        r = self.r
        share = self.dp_size // self.mp_size
        low = STARTS[FFOUT]
        r.w_ffout[self.me] = r.full[pl.ds(self.me * share, share), low : low + 4]
        self.deal(X_FFOUT_W, 0, lambda m: self.hidden_rows(r.full, m), lambda m: r.w_ffout.at[m])

    def share_ffout_wait(self):
        self.deal_wait(X_FFOUT_W, 0, lambda m: self.r.w_ffout.at[m])

    def cross_first(self):
        r = self.r
        self.spread_wait(X_CONTEXT, 0, r.context_all, self.whole_slot)
        table = self.weight(SQ2)
        total = 0.0
        for m in range(self.mp_size):
            total = total + dot_nn(r.context_all[m].astype(jnp.bfloat16), table[m * LANES : (m + 1) * LANES])
        r.cross_val[self.me] = total.astype(jnp.bfloat16).astype(jnp.float32)
        self.spread(X_CROSS_VAL, 0, r.cross_val, self.whole_slot)

    def cross_second(self):
        r = self.r
        self.spread_wait(X_CROSS_VAL, 0, r.cross_val, self.whole_slot)
        table = self.weight(SQ3)
        total = 0.0
        for m in range(self.mp_size):
            total = total + dot_nn(r.cross_val[m].astype(jnp.bfloat16), table[m * LANES : (m + 1) * LANES])
        r.cross_out[self.me] = total
        self.spread(X_CROSS_OUT, 0, r.cross_out, self.whole_slot)

    def cross_last(self):
        self.spread_wait(X_CROSS_OUT, 0, self.r.cross_out, self.whole_slot)

    def attention(self, image):
        r = self.r
        self.spread_wait(X_NORM, image, r.x_norm, self.columns(image))
        values = r.x_norm[self.image_rows(image), :]
        for m in range(self.mp_size):
            r.stream_in[image, :, m * LANES : (m + 1) * LANES] = dot_nn(values, self.wide(r.w_in, m))
        attn_in = token_norm(r.stream_in[image], self.full_lane(2, 0), self.full_lane(2, 1))[0].astype(jnp.bfloat16)
        r.attn_in[self.image_rows(image), :] = attn_in
        for j in range(3):
            r.qkv[j, self.image_rows(image)] = dot_nn(attn_in, self.weight(QKV, j)).astype(jnp.bfloat16)
        keep = self.across_lanes(image)
        lane_head = lax.broadcasted_iota(jnp.int32, (TOKENS, LANES), 1) // HD
        queries, keys, vals = (r.qkv[j, self.image_rows(image)] for j in range(3))
        zero = jnp.zeros((), jnp.bfloat16)
        attended = jnp.zeros((TOKENS, LANES), jnp.float32)
        for head in range(LANES // HD):
            own = lane_head == head
            scores = dot_nt(jnp.where(own, queries, zero), keys) * score_scale
            scores = jnp.where(keep, scores, masked_score)
            peak = jnp.max(scores, axis=-1, keepdims=True)
            expo = jnp.exp(scores - peak)
            probs = expo / jnp.sum(expo, axis=-1, keepdims=True)
            r.probs[image, head] = probs
            attended = jnp.where(own, dot_nn(probs.astype(jnp.bfloat16), vals), attended)
        r.x_attn[self.image_rows(image), self.mine()] = attended.astype(jnp.bfloat16)
        self.spread(X_ATTN, image, r.x_attn, self.columns(image))

    def feed(self, image):
        r = self.r
        self.spread_wait(X_ATTN, image, r.x_attn, self.columns(image))
        values = r.x_attn[self.image_rows(image), :]
        for m in range(self.mp_size):
            cut = slice(m * LANES, (m + 1) * LANES)
            r.stream_cross[image, :, cut] = (
                r.stream_in[image, :, cut] + dot_nn(values, self.wide(r.w_attn, m)) + r.cross_out[m, image : image + 1]
            )
        ff_in = token_norm(r.stream_cross[image], self.full_lane(3, 0), self.full_lane(3, 1))[0].astype(jnp.bfloat16)
        r.ff_in[self.image_rows(image), :] = ff_in
        for k in range(4):
            cut = slice(k * LANES, (k + 1) * LANES)
            value = dot_nn(ff_in, self.weight(FFIN, k))
            gate = dot_nn(ff_in, self.weight(FFIN, 4 + k))
            r.ff_value[image, :, cut] = value
            r.ff_gate[image, :, cut] = gate
            half = 0.5 * (1.0 + erf(gate * math.sqrt(0.5)))
            r.ff_hidden[self.image_rows(image), cut] = (value * (gate * half)).astype(jnp.bfloat16)
        hidden = r.ff_hidden[self.image_rows(image), :]
        for m in range(self.mp_size):
            total = dot_nn(hidden, self.wide_hidden(m))
            self.token_out(X_FF, image, r.ff_send, m, total)
        self.token_deal(X_FF, image, r.ff_send, r.ff_land)

    def wide_hidden(self, m):
        return self.flat(self.r.w_ffout[m])

    def token_out(self, name, image, send, m, total):
        share = TOKENS // self.mp_size
        send[image, :, :, m * LANES : (m + 1) * LANES] = total.reshape(self.mp_size, share, LANES).astype(send.dtype)

    def token_deal(self, name, image, send, land):
        land[image, self.me] = send[image, self.me]
        self.deal(name, image, lambda m: send.at[image, m], lambda m: land.at[image, m])

    def token_sum(self, name, image, land):
        self.deal_wait(name, image, lambda m: land.at[image, m])
        return jnp.sum(land[image].astype(jnp.float32), axis=0)

    def leave(self, image):
        r = self.r
        total = self.token_sum(X_FF, image, r.ff_land)
        stream = (r.stream_cross[image, self.my_tokens(), :] + total).astype(jnp.bfloat16)
        self.token_rows(image)(r.x_last, self.me)[...] = stream
        self.spread(X_LAST, image, r.x_last, self.token_rows(image))

    def upsample(self, ref, image, values):
        twice = jnp.broadcast_to(values.reshape(MID, 1, MID, LANES), (MID, 2, MID, LANES)).reshape(PIXELS // 2, LANES)
        ref[image, pl.ds(0, PIXELS // 2, stride=2)] = twice
        ref[image, pl.ds(1, PIXELS // 2, stride=2)] = twice

    def finish(self, image):
        r = self.r
        self.spread_wait(X_LAST, image, r.x_last, self.token_rows(image))
        values = r.x_last[self.image_rows(image), :]
        after = r.after_res[image] + dot_nn(values, self.weight(SQ4)) * r.half_mask[image]
        self.upsample(r.merged, image, after)
        merged = r.merged[image] + r.first[image]
        r.merged[image] = merged
        mask = r.full_mask[image]
        centre, inv_std = norm_stats(merged, mask, self.share(image, 1), r.group_spread[...])
        r.final_stats[image, 0:1] = centre
        r.final_stats[image, 1:2] = inv_std
        values = (merged - centre) * inv_std * self.gain(4) + self.bias(4)
        last_in = (values * sigmoid(values) * mask).astype(jnp.bfloat16)
        r.last_in[image] = last_in
        part = dot_nt(r.last_w[image], last_in)
        if image == 0:
            r.out_taps[...] = part
        else:
            r.out_taps[...] += part

    def predict(self):
        r = self.r
        total = 0.0
        for tap in range(9):
            total = total + self.tap_lanes(r.out_taps[8 * tap : 8 * tap + 8], tap)
        r.predicted[self.me] = total
        self.spread(X_PREDICTED, 0, r.predicted, self.whole_slot)

    def loss(self):
        r = self.r
        self.spread_wait(X_PREDICTED, 0, r.predicted, self.whole_slot)
        predicted = jnp.sum(r.predicted[...], axis=0)
        signal, level = r.signal8[:, 0:1], r.level8[:, 0:1]
        error = (predicted - (signal * r.noise8[...] - level * r.latent8[...])) * r.lane_mask[...]
        per_row = jnp.sum(error * error, axis=1, keepdims=True)
        r.small[8 * 20 : 8 * 20 + 8] = jnp.broadcast_to(column_sum(per_row * r.hot8[...]), (8, LANES))
        counts = jnp.sum(r.counts_all[...].reshape(-1, 8, LANES), axis=0)[0:1]
        weight = jnp.sum(r.hot8[...] * ((1.0 / NBANDS) / (counts + 1.0)), axis=1, keepdims=True)
        grads = (2.0 * error * weight).astype(jnp.bfloat16).astype(jnp.float32)
        for tap in range(9):
            r.out_taps[8 * tap : 8 * tap + 8] = self.tap_lanes(grads, 8 - tap)

    def pool_sum(self, ref, image):
        paired = ref[image, pl.ds(0, PIXELS // 2, stride=2)] + ref[image, pl.ds(1, PIXELS // 2, stride=2)]
        return jnp.sum(paired.reshape(MID, 2, MID, LANES), axis=1).reshape(TOKENS, LANES)

    def add_small(self, row, image, values):
        if image == 0:
            self.r.small[row : row + values.shape[0]] = values
        else:
            self.r.small[row : row + values.shape[0]] += values

    def tap_rows(self, values, image):
        row = lax.rem(lax.broadcasted_iota(jnp.int32, values.shape, 0), 8)
        return jnp.where(row // LAT == image, values, 0.0)

    def back_last(self, image):
        r = self.r
        grads_taps = r.out_taps[...].astype(jnp.bfloat16)
        mask = r.full_mask[image]
        grads = dot_tn(grads_taps, r.last_w[image]) * mask
        self.add_small(72, image, self.tap_rows(dot_nn(grads_taps, r.last_in[image]), image))
        inv_std = r.final_stats[image, 1:2]
        normal = (r.merged[image] - r.final_stats[image, 0:1]) * inv_std
        values = normal * self.gain(4) + self.bias(4)
        gate = sigmoid(values)
        grads = grads * (gate * (1.0 + values * (1.0 - gate)))
        grads, gain_grad, bias_grad = norm_backward(
            grads, normal, inv_std, mask, self.gain(4), self.share(image, 1), r.group_spread[...]
        )
        self.add_small(144 + 8, image, gain_grad)
        self.add_small(144 + 9, image, bias_grad)
        r.merged[image] = grads
        after = self.pool_sum(r.merged, image)
        r.grad_after[image] = after
        r.g_proj[self.image_rows(image), self.mine()] = (after * r.half_mask[image]).astype(jnp.bfloat16)
        self.spread(X_G_PROJ, image, r.g_proj, self.columns(image))

    def back_feed(self, image):
        r = self.r
        self.spread_wait(X_G_PROJ, image, r.g_proj, self.columns(image))
        total = 0.0
        for m in range(self.mp_size):
            total = total + dot_nt(r.g_proj[self.image_rows(image), m * LANES : (m + 1) * LANES], self.wide(r.w_out, m))
        r.grad_stream[image] = total
        grads_low = total.astype(jnp.bfloat16)
        r.g_ffout[self.image_rows(image), :] = grads_low
        hidden = 0.0
        for m in range(self.mp_size):
            hidden = hidden + dot_nt(grads_low[:, m * LANES : (m + 1) * LANES], self.wide_hidden(m))
        r.g_hidden[...] = hidden
        for k in range(4):
            cut = slice(k * LANES, (k + 1) * LANES)
            value, gate, grads = r.ff_value[image, :, cut], r.ff_gate[image, :, cut], r.g_hidden[:, cut]
            half = 0.5 * (1.0 + erf(gate * math.sqrt(0.5)))
            slope = half + gate * (jnp.exp(-0.5 * gate * gate) * (1.0 / math.sqrt(2.0 * math.pi)))
            r.g_ffin[k, self.image_rows(image)] = (grads * (gate * half)).astype(jnp.bfloat16)
            r.g_ffin[4 + k, self.image_rows(image)] = (grads * value * slope).astype(jnp.bfloat16)
        total = 0.0
        for k in range(8):
            total = total + dot_nt(r.g_ffin[k, self.image_rows(image)], self.weight(FFIN, k))
        share = TOKENS // self.mp_size
        r.gff_send[image] = total.reshape(self.mp_size, share, C).astype(r.gff_send.dtype)
        self.token_deal(X_G_FF, image, r.gff_send, r.gff_land)

    def token_back(self, name, image, land, stream, norm, row):
        r = self.r
        grads = self.token_sum(name, image, land)
        values = stream[image, self.my_tokens(), :]
        gain = self.full_lane(norm, 0)
        _, normal, inv_std = token_norm(values, gain, 0.0)
        grads, gain_grad, bias_grad = token_norm_backward(grads, normal, inv_std, gain)
        for which, values in ((0, gain_grad), (1, bias_grad)):
            for m in range(self.mp_size):
                place = r.norm_send.at[m, row + which : row + which + 1]
                cut = values[:, m * LANES : (m + 1) * LANES]
                place[...] = cut if image == 0 else place[...] + cut
        total = r.grad_stream[image, self.my_tokens(), :] + grads
        r.grad_stream[image, self.my_tokens(), :] = total
        return total

    def back_cross(self, image):
        r = self.r
        total = self.token_back(X_G_FF, image, r.gff_land, r.stream_cross, 3, 2)
        r.gc_part[self.me, image : image + 1] = column_sum(total)
        self.token_rows(image)(r.g_attn, self.me)[...] = total.astype(jnp.bfloat16)
        self.spread(X_G_ATTN, image, r.g_attn, self.token_rows(image))

    def cross_one(self):
        r = self.r
        r.gc_part[self.me, self.images :] = jnp.zeros((8 - self.images, C), jnp.float32)
        self.spread(X_GC, 0, r.gc_part, self.whole_slot)

    def cross_two(self):
        r = self.r
        self.spread_wait(X_GC, 0, r.gc_part, self.whole_slot)
        r.gc_full[...] = jnp.sum(r.gc_part[...], axis=0)
        mine = r.gc_full[:, self.mine()].astype(jnp.bfloat16)
        for m in range(self.mp_size):
            r.dw[m * LANES : (m + 1) * LANES] = dot_tn(r.cross_val[m].astype(jnp.bfloat16), mine)
        self.emit(SQ3, r.dw[...])
        r.gv_part[self.me] = dot_nt(mine, self.weight(SQ3))
        self.spread(X_GV, 0, r.gv_part, self.whole_slot)

    def cross_three(self):
        r = self.r
        self.spread_wait(X_GV, 0, r.gv_part, self.whole_slot)
        r.gc_full[...] = jnp.sum(r.gv_part[...], axis=0)
        mine = r.gc_full[:, self.mine()].astype(jnp.bfloat16)
        for m in range(self.mp_size):
            r.dw[m * LANES : (m + 1) * LANES] = dot_tn(r.context_all[m].astype(jnp.bfloat16), mine)
        self.emit(SQ2, r.dw[...])
        r.gx_part[self.me] = dot_nt(mine, self.weight(SQ2))
        self.spread(X_GX, 0, r.gx_part, self.whole_slot)

    def cross_four(self):
        r = self.r
        self.spread_wait(X_GX, 0, r.gx_part, self.whole_slot)
        r.gc_full[...] = jnp.sum(r.gx_part[...], axis=0)
        row = lax.broadcasted_iota(jnp.int32, (8, LANES), 0)
        r.table_rows[0] = jnp.where(row < self.images, r.gc_full[:, self.mine()], r.labels8[...])

    def back_attention(self, image):
        r = self.r
        self.spread_wait(X_G_ATTN, image, r.g_attn, self.token_rows(image))
        total = 0.0
        for m in range(self.mp_size):
            total = total + dot_nt(r.g_attn[self.image_rows(image), m * LANES : (m + 1) * LANES], self.wide_mine(r.w_attn, m))
        grads = total.astype(jnp.bfloat16)
        queries, keys, vals = (r.qkv[j, self.image_rows(image)] for j in range(3))
        lane_head = lax.broadcasted_iota(jnp.int32, (TOKENS, LANES), 1) // HD
        zero = jnp.zeros((), jnp.bfloat16)
        results = [jnp.zeros((TOKENS, LANES), jnp.float32) for _ in range(3)]
        for head in range(LANES // HD):
            own = lane_head == head
            probs = r.probs[image, head]
            results[2] = jnp.where(own, dot_tn(probs.astype(jnp.bfloat16), grads), results[2])
            grad_probs = dot_nt(jnp.where(own, grads, zero), vals)
            grad_scores = (probs * (grad_probs - jnp.sum(probs * grad_probs, axis=-1, keepdims=True))).astype(jnp.bfloat16)
            results[0] = jnp.where(own, dot_nn(grad_scores, keys) * score_scale, results[0])
            results[1] = jnp.where(own, dot_tn(grad_scores, queries) * score_scale, results[1])
        total = 0.0
        for j in range(3):
            low = results[j].astype(jnp.bfloat16)
            r.g_qkv[j, self.image_rows(image)] = low
            total = total + dot_nt(low, self.weight(QKV, j))
        share = TOKENS // self.mp_size
        r.gat_send[image] = total.reshape(self.mp_size, share, C).astype(r.gat_send.dtype)
        self.token_deal(X_G_AT, image, r.gat_send, r.gat_land)

    def back_in(self, image):
        r = self.r
        total = self.token_back(X_G_AT, image, r.gat_land, r.stream_in, 2, 0)
        self.token_rows(image)(r.g_in, self.me)[...] = total.astype(jnp.bfloat16)
        self.spread(X_G_IN, image, r.g_in, self.token_rows(image))

    def back_conv(self, image):
        r = self.r
        self.spread_wait(X_G_IN, image, r.g_in, self.token_rows(image))
        mask = r.half_mask[image]
        grads = 0.0
        for m in range(self.mp_size):
            grads = grads + dot_nt(r.g_in[self.image_rows(image), m * LANES : (m + 1) * LANES], self.wide_mine(r.w_in, m))
        after = r.after_res[image]
        centre, inv_std = norm_stats(after, mask, self.share(image, 2), r.group_spread[...])
        normal = (after - centre) * inv_std
        grads, gain_grad, bias_grad = norm_backward(
            grads * mask, normal, inv_std, mask, self.gain(1), self.share(image, 2), r.group_spread[...]
        )
        self.add_small(144 + 2, image, gain_grad)
        self.add_small(144 + 3, image, bias_grad)
        grads = r.grad_after[image] + grads
        r.grad_after[image] = grads
        masked = grads * mask
        r.grad_time[image : image + 1] = column_sum(masked).astype(jnp.bfloat16).astype(jnp.float32)
        low = masked.astype(jnp.bfloat16).astype(jnp.float32)
        column = lax.rem(lax.broadcasted_iota(jnp.int32, (TOKENS, LANES), 0), MID)
        total = 0.0
        for tap in range(9):
            i, j = divmod(tap, 3)
            moved = shift_rows(low, 1 - i)
            if j == 0:
                moved = jnp.where(column < MID - 1, pltpu.roll(moved, TOKENS - 1, 0), 0.0)
            elif j == 2:
                moved = jnp.where(column > 0, pltpu.roll(moved, 1, 0), 0.0)
            moved = moved.astype(jnp.bfloat16)
            r.g_taps[self.image_rows(image), tap * LANES : (tap + 1) * LANES] = moved
            total = total + dot_nt(moved, self.weight(CONV, tap))
        for m in range(self.mp_size):
            r.gres_send[image, m] = total[:, m * LANES : (m + 1) * LANES].astype(r.gres_send.dtype)
        self.token_deal(X_G_RES, image, r.gres_send, r.gres_land)

    def back_first(self, image):
        r = self.r
        grads = self.token_sum(X_G_RES, image, r.gres_land)
        mask = r.half_mask[image]
        pooled = r.pooled[image]
        centre, inv_std = norm_stats(pooled, mask, self.share(image, 2), r.group_spread[...])
        normal = (pooled - centre) * inv_std
        values = normal * self.gain(0) + self.bias(0)
        gate = sigmoid(values)
        grads = grads * mask * (gate * (1.0 + values * (1.0 - gate)))
        grads, gain_grad, bias_grad = norm_backward(
            grads, normal, inv_std, mask, self.gain(0), self.share(image, 2), r.group_spread[...]
        )
        self.add_small(144, image, gain_grad)
        self.add_small(144 + 1, image, bias_grad)
        self.upsample(r.first, image, 0.25 * (r.grad_after[image] + grads))
        low = ((r.merged[image] + r.first[image]) * r.full_mask[image]).astype(jnp.bfloat16)
        self.add_small(0, image, self.tap_rows(dot_nn(r.taps[...].astype(jnp.bfloat16), low), image))

    def back_time(self):
        r = self.r
        r.grad_time[self.images :] = jnp.zeros((8 - self.images, LANES), jnp.float32)
        grads = r.grad_time[...].astype(jnp.bfloat16)
        width = r.time_act.shape[2]
        for m in range(self.mp_size):
            r.dw_time[m * width : (m + 1) * width] = dot_tn(r.time_act[m].astype(jnp.bfloat16), grads)
        self.emit_rows(TOUT, r.dw_time[...], 2)
        total = dot_nt(grads, self.weight_rows(TOUT, 2))
        for m in range(self.mp_size):
            r.gt_send[m] = total[:, m * width : (m + 1) * width]
        r.gt_land[self.me] = r.gt_send[self.me]
        self.deal(X_GT, 0, lambda m: r.gt_send.at[m], lambda m: r.gt_land.at[m])
        r.norm_land[self.me] = r.norm_send[self.me]
        self.deal(X_NORM_SUMS, 0, lambda m: r.norm_send.at[m], lambda m: r.norm_land.at[m])

    def back_time_in(self):
        r = self.r
        self.deal_wait(X_GT, 0, lambda m: r.gt_land.at[m])
        grads = jnp.sum(r.gt_land[...], axis=0)
        hidden = r.hidden_time[...]
        gate = sigmoid(hidden)
        grads = (grads * (gate * (1.0 + hidden * (1.0 - gate)))).astype(jnp.bfloat16)
        total = 0.0
        for h in range(r.embedded.shape[0]):
            total = total + dot_tn(r.embedded[h], grads[:, h * LANES : (h + 1) * LANES])
        self.emit(TIN, total)
        self.deal_wait(X_NORM_SUMS, 0, lambda m: r.norm_land.at[m])
        r.small[144 + 4 : 144 + 8] = jnp.sum(r.norm_land[...], axis=0)[0:4]
        r.small[144 + 10 : 160] = jnp.zeros((6, LANES), jnp.float32)

    def grads_out(self):
        r = self.r
        self.emit(SQ4, dot_tn(r.x_last[...], r.g_proj[:, self.mine()]))

    def grads_ffout(self):
        r = self.r
        share = self.dp_size // self.mp_size
        for m in range(self.mp_size):
            part = dot_tn(r.ff_hidden[...], r.g_ffout[:, m * LANES : (m + 1) * LANES])
            r.dw_ffout[m] = part.reshape(share, 4, self.rows, LANES).astype(jnp.bfloat16)
        low = STARTS[FFOUT]
        r.partials[pl.ds(self.me * share, share), low : low + 4] = r.dw_ffout[self.me]
        self.deal(X_DW_FFOUT, 0, lambda m: r.dw_ffout.at[m], lambda m: self.hidden_rows(r.partials, m))

    def grads_ffout_wait(self):
        self.deal_wait(X_DW_FFOUT, 0, lambda m: self.hidden_rows(self.r.partials, m))

    def grads_ffin(self):
        for k in range(8):
            self.emit(FFIN, dot_tn(self.r.ff_in[...], self.r.g_ffin[k]), k)

    def grads_attn(self):
        r = self.r
        self.emit(SQ1, dot_tn(r.x_attn[...], r.g_attn[:, self.mine()]))

    def grads_qkv(self):
        for j in range(3):
            self.emit(QKV, dot_tn(self.r.attn_in[...], self.r.g_qkv[j]), j)

    def grads_in(self):
        r = self.r
        self.emit(SQ0, dot_tn(r.x_norm[...], r.g_in[:, self.mine()]))

    def grads_conv(self, i):
        r = self.r
        for tap in range(3 * i, 3 * i + 3):
            self.emit(CONV, dot_tn(r.x_res[...], r.g_taps[:, tap * LANES : (tap + 1) * LANES]), tap)


SMALL_ROWS = 168
EXCHANGES = 64


def model_scratch(images, dp_size, mp_size, rows, time_local, hidden_local):
    bf16, f32 = jnp.bfloat16, jnp.float32
    tokens = images * TOKENS
    share = TOKENS // mp_size
    wide = lambda kind: pltpu.VMEM((tokens, C), kind)
    per_image = lambda width, kind=f32: pltpu.VMEM((images, TOKENS, width), kind)
    send = lambda kind: pltpu.VMEM((images, mp_size, share, C), kind)
    tiny = lambda width: pltpu.VMEM((mp_size, 8, width), f32)
    square = lambda: pltpu.VMEM((mp_size, dp_size, rows, LANES), bf16)
    dma = pltpu.SemaphoreType.DMA((EXCHANGES, mp_size))
    link = LINK
    return dict(
        ex_send=dma, ex_recv=dma,
        group_spread=pltpu.VMEM((LANES, LANES), bf16),
        norms_all=pltpu.VMEM((mp_size, 5, 2, LANES), f32),
        context_all=tiny(LANES), time_act=tiny(time_local), cross_val=tiny(LANES), cross_out=tiny(LANES),
        full_mask=pltpu.VMEM((images, PIXELS, LANES), f32), half_mask=per_image(LANES),
        latent8=pltpu.VMEM((8, PIXELS), f32), noise8=pltpu.VMEM((8, PIXELS), f32), lane_mask=pltpu.VMEM((8, PIXELS), f32),
        taps=pltpu.VMEM((72, PIXELS), f32), out_taps=pltpu.VMEM((72, PIXELS), f32),
        first=pltpu.VMEM((images, PIXELS, LANES), f32), merged=pltpu.VMEM((images, PIXELS, LANES), f32),
        last_in=pltpu.VMEM((images, PIXELS, LANES), bf16),
        pooled=per_image(LANES), after_res=per_image(LANES), grad_after=per_image(LANES),
        final_stats=pltpu.VMEM((images, 8, LANES), f32),
        hidden_time=pltpu.VMEM((8, time_local), f32), time_vec=pltpu.VMEM((8, LANES), f32), grad_time=pltpu.VMEM((8, LANES), f32),
        x_res=wide(bf16), x_norm=wide(bf16), x_attn=wide(bf16), x_last=wide(bf16),
        g_proj=wide(bf16), g_ffout=wide(bf16), g_attn=wide(bf16), g_in=wide(bf16),
        attn_in=wide(bf16), ff_in=wide(bf16), ff_hidden=pltpu.VMEM((tokens, hidden_local), bf16),
        stream_in=per_image(C), stream_cross=per_image(C), grad_stream=per_image(C),
        ff_value=per_image(hidden_local), ff_gate=per_image(hidden_local),
        g_hidden=pltpu.VMEM((TOKENS, hidden_local), f32), g_ffin=pltpu.VMEM((8, tokens, LANES), bf16),
        qkv=pltpu.VMEM((3, tokens, LANES), bf16), g_qkv=pltpu.VMEM((3, tokens, LANES), bf16),
        probs=pltpu.VMEM((images, LANES // HD, TOKENS, TOKENS), f32),
        w_in=square(), w_attn=square(), w_out=square(),
        w_ffout=pltpu.VMEM((mp_size, dp_size // mp_size, 4, rows, LANES), bf16),
        dw_ffout=pltpu.VMEM((mp_size, dp_size // mp_size, 4, rows, LANES), bf16),
        ff_send=send(link), ff_land=send(link), gff_send=send(link), gff_land=send(link),
        gat_send=send(link), gat_land=send(link),
        gres_send=pltpu.VMEM((images, mp_size, TOKENS, LANES), link), gres_land=pltpu.VMEM((images, mp_size, TOKENS, LANES), link),
        predicted=pltpu.VMEM((mp_size, 8, PIXELS), f32),
        norm_send=tiny(LANES), norm_land=tiny(LANES),
        gc_part=tiny(C), gv_part=tiny(C), gx_part=tiny(C), gc_full=pltpu.VMEM((8, C), f32),
        dw=pltpu.VMEM((C, LANES), f32), dw_time=pltpu.VMEM((mp_size * time_local, LANES), f32),
        gt_send=tiny(time_local), gt_land=tiny(time_local),
        conv_sum=pltpu.VMEM((images, 3, TOKENS, LANES), f32),
        hot8=pltpu.VMEM((8, LANES), f32), signal8=pltpu.VMEM((8, LANES), f32), level8=pltpu.VMEM((8, LANES), f32),
        labels8=pltpu.VMEM((8, LANES), f32), context=pltpu.VMEM((8, LANES), f32), counts=pltpu.VMEM((1, 8, LANES), f32),
        embedded=pltpu.VMEM((time_local // LANES, 8, TE * time_local // LANES), bf16),
        first_f=pltpu.VMEM((images, 72, LANES), f32), last_f=pltpu.VMEM((images, 72, LANES), f32),
        first_w=pltpu.VMEM((images, 72, LANES), bf16), last_w=pltpu.VMEM((images, 72, LANES), bf16),
        tin_rows=pltpu.VMEM((rows, LANES), f32), shard=pltpu.VMEM((SECTION_COUNT, rows, LANES), bf16),
        full=pltpu.VMEM((dp_size, SECTION_COUNT, rows, LANES), bf16), partials=pltpu.VMEM((dp_size, SECTION_COUNT, rows, LANES), bf16),
        small=pltpu.VMEM((SMALL_ROWS, LANES), f32), table_rows=pltpu.VMEM((1, 8, LANES), f32),
        g_taps=pltpu.VMEM((tokens, 9 * LANES), bf16),
    )


class Reducer:
    def __init__(self, place, refs, dp_size):
        self.place = place
        self.r = refs
        self.dp_size = dp_size
        r = refs
        self.scatter = Scatter(
            place, r.partials, r.total, r.near, r.sums, r.far, (r.sc_a, r.sc_b, r.sc_c, r.sc_d), SCATTER_PIECES
        )
        self.slots = r.root_own.shape[0]
        self.gather = Gather(
            place, r.root_own, r.roots, (r.ro_a, r.ro_b, r.ro_c, r.ro_d), tuple((s, 1) for s in range(self.slots))
        )
        self.table = Gather(place, r.table_rows, r.table_all, (r.ta_a, r.ta_b, r.ta_c, r.ta_d), ((0, 1),))
        self.started, self.pumped, self.finished, self.sent = 0, 0, 0, set()

    def start(self, count):
        while self.started < count:
            self.scatter.start(self.started)
            self.started += 1

    def pump(self, count):
        while self.pumped < count:
            self.scatter.pump(self.pumped)
            self.pumped += 1

    def finish(self, count):
        while self.finished < count:
            self.scatter.finish(self.finished)
            low, sections = SCATTER_PIECES[self.finished]
            self.r.total_low[pl.ds(low, sections)] = self.r.total[pl.ds(low, sections)].astype(jnp.bfloat16)
            self.finished += 1
            done = {k for start, number in SCATTER_PIECES[: self.finished] for k in range(start, start + number)}
            for position, block in enumerate(ORDER):
                low, sections = BLOCKS[block]
                if position not in self.sent and all(k in done for k in range(low, low + sections)):
                    self.sent.add(position)
                    self.send_block(position)

    def owned_by(self, positions):
        owner = self.place.dp == positions[0] % self.dp_size
        for position in positions[1:]:
            owner = owner | (self.place.dp == position % self.dp_size)
        return owner

    def block_copy(self, position, other, source):
        r = self.r
        block = ORDER[position]
        slot = position // self.dp_size
        if block in BY_GRAM:
            out, land = r.gram_out.at[BY_GRAM.index(block)], r.gram_land.at[slot, source]
        else:
            out, land = r.total_low.at[BLOCKS[block][0]], r.rows_land.at[slot, source]
        return remote(out, land, r.bl_send.at[position], r.bl_recv.at[slot, source], (other, self.place.mp))

    def send_block(self, position):
        r = self.r
        place = self.place
        block = ORDER[position]
        low, sections = BLOCKS[block]
        owner, slot = position % self.dp_size, position // self.dp_size
        if block in BY_GRAM:
            values = r.total[pl.ds(low, sections)].reshape(-1, LANES)
            r.gram_out[BY_GRAM.index(block)] = gram_of(values).astype(jnp.bfloat16)

        @pl.when(place.dp != owner)
        def _():
            self.block_copy(position, owner, place.dp).start()

        @pl.when(place.dp == owner)
        def _():
            if block in BY_GRAM:
                r.gram_land[slot, place.dp] = r.gram_out[BY_GRAM.index(block)]
            else:
                r.rows_land[slot, place.dp] = r.total_low[low]

    def gram(self, slot):
        r = self.r
        place = self.place
        positions = [p for p in range(len(ORDER)) if p // self.dp_size == slot]
        kinds = (
            [p for p in positions if ORDER[p] in BY_GRAM],
            [p for p in positions if ORDER[p] in TIN_BLOCKS],
            [p for p in positions if ORDER[p] not in BY_GRAM + TIN_BLOCKS],
        )
        for kind, members in enumerate(kinds):
            if not members:
                continue

            @pl.when(self.owned_by(members))
            def _(kind=kind, members=members):
                def receive(step):
                    source = lax.rem(place.dp + step, self.dp_size)
                    self.block_copy(members[0], source, source).wait_recv()

                steps(1, self.dp_size, receive)
                if kind == 0:
                    r.gram_own[slot] = jnp.sum(r.gram_land[slot].astype(jnp.float32), axis=0)
                    return
                values = r.rows_land[slot]
                if values.shape[1] % 16 == 0 and kind == 2:
                    values = values.reshape(-1, LANES)
                else:
                    values = values.astype(jnp.float32).reshape(-1, LANES)
                    if kind == 1:
                        parity = lax.rem(lax.broadcasted_iota(jnp.int32, values.shape, 0), len(TIN_BLOCKS))
                        values = jnp.where(parity == place.dp - members[0] % self.dp_size, values, 0.0)
                    values = values.astype(jnp.bfloat16)
                r.gram_own[slot] = dot_tn(values, values)

    def root(self, slots):
        if not slots:
            return
        r = self.r
        renewed = []
        for slot in slots:
            self.gram(slot)
            gram = r.gram_own[slot]
            old = r.stats[ORDER[slot * self.dp_size]]
            for position in range(slot * self.dp_size + 1, min((slot + 1) * self.dp_size, len(ORDER))):
                old = jnp.where(self.place.dp == position % self.dp_size, r.stats[ORDER[position]], old)
            renewed.append(shampoo_beta * old + gram)
            r.root_own[slot, 1] = gram.astype(jnp.bfloat16)
        for slot, root in zip(slots, inverse_roots(renewed)):
            r.root_own[slot, 0] = root.astype(jnp.bfloat16)
            self.gather.start(slot)
            r.roots[self.place.dp, slot] = r.root_own[slot]

    def small_copy(self, step):
        r = self.r
        if isinstance(step, int) and step == 0:
            return remote(r.small, r.small_near, r.sm_send.at[0], r.sm_recv.at[0], self.place.partner())
        return remote(
            r.small_far.at[0], r.small_far.at[step], r.sm_send.at[step], r.sm_recv.at[step], self.place.across(step)
        )

    def small_start(self):
        self.small_copy(0).start()
        self.table.start(0)
        self.r.table_all[self.place.dp] = self.r.table_rows[...]

    def small_pump(self):
        r = self.r
        self.small_copy(0).wait_recv()
        r.small_far[0] = r.small[...] + r.small_near[...]
        steps(1, self.place.outer_size, lambda step: self.small_copy(step).start())
        self.table.pump(0)

    def small_finish(self):
        r = self.r
        steps(1, self.place.outer_size, lambda step: self.small_copy(step).wait_recv())
        r.small_sum[...] = jnp.sum(r.small_far[...], axis=0)
        self.table.ready(0)

    def drain(self):
        for piece in range(len(SCATTER_PIECES)):
            self.scatter.drain(piece)
        for slot in range(self.slots):
            self.gather.drain(slot)
        self.table.drain(0)
        steps(0, self.place.outer_size, lambda step: self.small_copy(step).wait_send())
        for position in range(len(ORDER)):
            @pl.when(self.place.dp != position % self.dp_size)
            def _(position=position):
                self.block_copy(position, position % self.dp_size, self.place.dp).wait_send()


def reducer_scratch(dp_size, rows):
    bf16, f32 = jnp.bfloat16, jnp.float32
    outer = dp_size // 2
    slots = -(-len(ORDER) // dp_size)
    dma = pltpu.SemaphoreType.DMA
    held = lambda: pltpu.VMEM((outer, SECTION_COUNT, rows, LANES), bf16)
    scatter_sem = dma((len(SCATTER_PIECES), outer))
    gather_sem = dma((len(GATHER_PIECES), outer))
    root_sem = dma((slots, outer))
    one_sem = dma((1, outer))
    return dict(
        near=held(), sums=held(), far=held(),
        total_low=pltpu.VMEM((SECTION_COUNT, rows, LANES), bf16),
        gram_out=pltpu.VMEM((len(BY_GRAM), LANES, LANES), bf16),
        gram_land=pltpu.VMEM((slots, dp_size, LANES, LANES), bf16),
        rows_land=pltpu.VMEM((slots, dp_size, rows, LANES), bf16),
        gram_own=pltpu.VMEM((slots, LANES, LANES), f32),
        root_own=pltpu.VMEM((slots, 2, LANES, LANES), bf16),
        small_near=pltpu.VMEM((SMALL_ROWS, LANES), f32), small_far=pltpu.VMEM((outer, SMALL_ROWS, LANES), f32),
        sc_a=scatter_sem, sc_b=scatter_sem, sc_c=scatter_sem, sc_d=scatter_sem,
        ga_a=gather_sem, ga_b=gather_sem, ga_c=gather_sem, ga_d=gather_sem,
        ro_a=root_sem, ro_b=root_sem, ro_c=root_sem, ro_d=root_sem,
        ta_a=one_sem, ta_b=one_sem, ta_c=one_sem, ta_d=one_sem,
        co_a=one_sem, co_b=one_sem, co_c=one_sem, co_d=one_sem,
        sm_send=dma((outer,)), sm_recv=dma((outer,)),
        bl_send=dma((len(ORDER),)), bl_recv=dma((slots, dp_size)),
    )


class Refs:
    pass


def step_kernel(images, dp_size, mp_size, names, *refs):
    r = Refs()
    for name, ref in zip(names, refs):
        setattr(r, name, ref)
    place = Place(dp_size, mp_size)
    model = Model(place, r, images, dp_size, mp_size)
    reducer = Reducer(place, r, dp_size)
    weights = Gather(place, r.shard, r.full, (r.ga_a, r.ga_b, r.ga_c, r.ga_d), GATHER_PIECES)
    counts = Gather(place, r.counts, r.counts_all, (r.co_a, r.co_b, r.co_c, r.co_d), ((0, 1),))
    every = range(images)
    model.greet_all(pltpu.get_barrier_semaphore())
    model.pack()
    for piece in range(len(GATHER_PIECES)):
        weights.start(piece)
    model.prepare()
    counts.start(0)
    r.full[place.dp] = r.shard[...]
    r.counts_all[place.dp] = r.counts[...]
    model.setup()
    for image in every:
        model.entry(image)
    weights.pump(0)
    weights.ready(0)
    model.time_in()
    model.share_square(SQ0, r.w_in)
    counts.pump(0)
    weights.pump(1)
    model.time_out()
    for image in every:
        model.res_wait(image)
    for i in range(3):
        weights.ready(1 + i)
        for image in every:
            model.convolve(image, i)
        weights.pump(2 + i)
    for image in every:
        model.convolved(image)
    weights.ready(4)
    model.share_square(SQ1, r.w_attn)
    model.cross_first()
    model.spread_wait(X_NORMS, 0, r.norms_all, model.whole_slot)
    model.share_square_wait(SQ0, r.w_in)
    weights.pump(5)
    for image in every:
        model.attention(image)
    model.cross_second()
    weights.ready(5)
    model.share_ffout()
    weights.pump(6)
    weights.pump(7)
    model.share_square_wait(SQ1, r.w_attn)
    model.cross_last()
    model.share_ffout_wait()
    weights.ready(6)
    weights.ready(7)
    model.share_square(SQ4, r.w_out)
    counts.ready(0)
    for image in every:
        model.feed(image)
    for image in every:
        model.leave(image)
    for image in every:
        model.finish(image)
    model.predict()
    model.share_square_wait(SQ4, r.w_out)
    model.loss()
    for image in every:
        model.back_last(image)
    model.grads_out()
    reducer.start(1)
    for image in every:
        model.back_feed(image)
    model.grads_ffout()
    for image in every:
        model.back_cross(image)
    model.cross_one()
    model.grads_ffin()
    reducer.start(3)
    model.grads_ffout_wait()
    reducer.start(4)
    for image in every:
        model.back_attention(image)
    reducer.pump(2)
    model.cross_two()
    model.grads_attn()
    model.grads_qkv()
    reducer.start(5)
    for image in every:
        model.back_in(image)
    model.cross_three()
    reducer.start(6)
    reducer.pump(4)
    for image in every:
        model.back_conv(image)
    model.grads_in()
    reducer.start(7)
    for i in range(3):
        model.grads_conv(i)
        reducer.start(8 + i)
    reducer.pump(6)
    model.back_time()
    for image in every:
        model.back_first(image)
    model.cross_four()
    model.back_time_in()
    reducer.start(11)
    reducer.small_start()
    reducer.pump(7)
    reducer.finish(4)
    reducer.pump(9)
    reducer.finish(6)
    reducer.pump(11)
    reducer.small_pump()
    slots = list(range(reducer.slots))
    reducer.root(slots[:-1])
    reducer.finish(11)
    reducer.root(slots[-1:])
    for slot in slots:
        reducer.gather.pump(slot)
    reducer.small_finish()
    for slot in slots:
        reducer.gather.ready(slot)
    model.drain()
    reducer.drain()
    for piece in range(len(GATHER_PIECES)):
        weights.drain(piece)
    counts.drain(0)


def train_step(images, dp_size, mp_size, scalars, arrays):
    vmem = pl.BlockSpec(memory_space=pltpu.VMEM)
    smem = pl.BlockSpec(memory_space=pltpu.SMEM)
    rows = arrays["w_square"].shape[1]
    f32, bf16 = jnp.float32, jnp.bfloat16
    slots = -(-len(ORDER) // dp_size)
    outs = dict(
        total=jax.ShapeDtypeStruct((SECTION_COUNT, rows, LANES), f32),
        roots=jax.ShapeDtypeStruct((dp_size, slots, 2, LANES, LANES), bf16),
        small_sum=jax.ShapeDtypeStruct((SMALL_ROWS, LANES), f32),
        table_all=jax.ShapeDtypeStruct((dp_size, 1, 8, LANES), f32),
        counts_all=jax.ShapeDtypeStruct((dp_size, 1, 8, LANES), f32),
    )
    time_local = arrays["w_tin"].shape[1]
    hidden_local = arrays["w_fi"].shape[2]
    scratch = model_scratch(images, dp_size, mp_size, rows, time_local, hidden_local)
    scratch.update(reducer_scratch(dp_size, rows))
    names = list(scalars) + list(arrays) + list(outs) + list(scratch)
    return pl.pallas_call(
        functools.partial(step_kernel, images, dp_size, mp_size, names),
        out_shape=tuple(outs.values()),
        in_specs=[smem] * len(scalars) + [vmem] * len(arrays),
        out_specs=(vmem,) * len(outs),
        scratch_shapes=list(scratch.values()),
        compiler_params=pltpu.CompilerParams(
            collective_id=1, has_side_effects=True, vmem_limit_bytes=VMEM_LIMIT
        ),
        name="train_step",
    )(*scalars.values(), *arrays.values())


def adam(weight, mean, variance, gradient, rate):
    mean = beta_one * mean + (1 - beta_one) * gradient
    variance = beta_two * variance + (1 - beta_two) * gradient * gradient
    step = mean * (1.0 / (1 - beta_one**STEP)) / (jnp.sqrt(variance * (1.0 / (1 - beta_two**STEP))) + adam_eps)
    return weight - rate * (step + decay * weight), mean, variance


def update_kernel(images, dp_size, names, *refs):
    r = Refs()
    for name, ref in zip(names, refs):
        setattr(r, name, ref)
    rows = r.total.shape[1]
    parity = lax.rem(lax.broadcasted_iota(jnp.int32, (rows, LANES), 0), 2)
    where = {block: (position % dp_size, position // dp_size) for position, block in enumerate(ORDER)}
    for block in range(len(ORDER)):
        owner, slot = where[block]
        r.stats_new[block] = shampoo_beta * r.stats[block] + r.roots[owner, slot, 1].astype(jnp.float32)

    def turned(moment, block):
        owner, slot = where[block]
        high, low = split(moment)
        root = r.roots[owner, slot, 0]
        return dot_nn(high, root) + dot_nn(low, root)

    def renew(section, block, old, momentum):
        moment = shampoo_momentum * momentum + r.total[section]
        return old - shampoo_rate * (turned(moment, block) + decay * old), moment

    for k, name in enumerate(SQUARES):
        r.square_new[k], r.square_mom[k] = renew(STARTS[name], k, r.w_square[k], r.m_square[k])
    for k in range(9):
        r.conv_new[k], r.conv_mom[k] = renew(STARTS[CONV] + k, 5, r.w_conv[k], r.m_conv[k])
    for j in range(3):
        new, moment = renew(STARTS[QKV] + j, 6 + j, r.w_qkv[:, j, :], r.m_qkv[:, j, :])
        r.qkv_new[:, j, :] = new
        r.qkv_mom[:, j, :] = moment
    for k in range(8):
        j, cut = k // 4, slice(k % 4 * LANES, (k % 4 + 1) * LANES)
        new, moment = renew(STARTS[FFIN] + k, 9 + k, r.w_fi[:, j, cut], r.m_fi[:, j, cut])
        r.fi_new[:, j, cut] = new
        r.fi_mom[:, j, cut] = moment
    for k in range(4):
        cut = slice(k * rows, (k + 1) * rows)
        r.fo_new[cut], r.fo_mom[cut] = renew(STARTS[FFOUT] + k, 17, r.w_fo[cut], r.m_fo[cut])
    for k in range(2):
        cut = slice(k * rows, (k + 1) * rows)
        r.tout_new[cut], r.tout_mom[cut] = renew(STARTS[TOUT] + k, 20, r.w_tout[cut], r.m_tout[cut])
    halves = r.w_tin.shape[1] // LANES
    r.tin_rows[0] = r.total[STARTS[TIN]]
    for h in range(halves):
        cut = slice(h * LANES, (h + 1) * LANES)
        gradient = r.tin_rows[0, pl.ds(h, rows // halves, stride=halves)]
        moment = shampoo_momentum * r.m_tin[:, cut] + gradient
        r.tin_mom[:, cut] = moment
        old = r.w_tin[:, cut]
        r.tin_new[:, cut] = old - shampoo_rate * (turned(moment, 18 + h) + decay * old)
    for image in range(images):
        for tap in range(9):
            low = 8 * tap + LAT * image
            gradient = r.small_sum[low : low + LAT]
            if image > 0:
                gradient = r.first_grad[tap] + gradient
            r.first_grad[tap] = gradient
    r.first_new[...], r.first_mean_new[...], r.first_var_new[...] = adam(
        r.conv_first[...], r.first_mean[...], r.first_var[...], r.first_grad[...], rate_first
    )
    for k in range(5):
        gradient = r.small_sum[144 + 2 * k : 146 + 2 * k]
        r.norm_new[k], r.norm_mean_new[k], r.norm_var_new[k] = adam(
            r.norms[k], r.norm_mean[k], r.norm_var[k], gradient, rate_gain
        )
    count = r.class_table.shape[0]
    row = lax.broadcasted_iota(jnp.int32, (count, LANES), 0).astype(jnp.float32)
    r.table_grad[...] = jnp.zeros((count, LANES), jnp.float32)

    def add(source):
        for image in range(images):
            label = r.table_all[source, 0, images + image : images + image + 1]
            gradient = r.table_all[source, 0, image : image + 1]
            r.table_grad[...] += jnp.where(row == label, gradient, 0.0)

    steps(0, dp_size, add)
    r.table_new[...], r.table_mean_new[...], r.table_var_new[...] = adam(
        r.class_table[...], r.table_mean[...], r.table_var[...], r.table_grad[...], rate_table
    )
    counts = jnp.sum(r.counts_all[...].reshape(dp_size, 8, LANES), axis=0)
    r.loss_terms[0:1] = r.small_sum[160:161, 0:NBANDS]
    r.loss_terms[1:2] = counts[0:1, 0:NBANDS]


def apply_update(images, dp_size, arrays, outs):
    vmem = pl.BlockSpec(memory_space=pltpu.VMEM)
    rows = arrays["total"].shape[1]
    scratch = dict(
        tin_rows=pltpu.VMEM((1, rows, LANES), jnp.float32),
        first_grad=pltpu.VMEM(arrays["conv_first"].shape, jnp.float32),
        table_grad=pltpu.VMEM(arrays["class_table"].shape, jnp.float32),
    )
    names = list(arrays) + list(outs) + list(scratch)
    return pl.pallas_call(
        functools.partial(update_kernel, images, dp_size, names),
        out_shape=tuple(outs.values()),
        in_specs=[vmem] * len(arrays),
        out_specs=(vmem,) * len(outs),
        scratch_shapes=list(scratch.values()),
        compiler_params=pltpu.CompilerParams(vmem_limit_bytes=VMEM_LIMIT),
        name="apply_update",
    )(*arrays.values())


def local(
    clean_latent,
    noise_latent,
    timesteps,
    labels,
    image_sides,
    w_square,
    mom_square,
    w_conv,
    mom_conv,
    w_qkv,
    mom_qkv,
    w_ffin,
    mom_ffin,
    w_ffout,
    mom_ffout,
    w_time_in,
    mom_time_in,
    w_time_out,
    mom_time_out,
    kron_stats,
    class_table,
    table_mean,
    table_var,
    conv_first,
    first_mean,
    first_var,
    conv_last,
    last_mean,
    last_var,
    norm_params,
    norm_mean,
    norm_var,
):
    dp_size = lax.axis_size(DP)
    mp_size = lax.axis_size(MP)
    images = clean_latent.shape[0]
    weights = dict(
        w_square=w_square, w_conv=w_conv, w_qkv=w_qkv, w_fi=w_ffin, w_fo=w_ffout, w_tin=w_time_in, w_tout=w_time_out
    )
    total, roots, small, table_all, counts_all = train_step(
        images,
        dp_size,
        mp_size,
        dict(timesteps=timesteps, labels=labels, sides=image_sides),
        dict(
            latent=clean_latent,
            noise=noise_latent,
            class_table=class_table,
            norms=norm_params,
            conv_first=conv_first,
            conv_last=conv_last.transpose(0, 2, 1),
            stats=kron_stats,
            **weights,
        ),
    )

    def like(array):
        return jax.ShapeDtypeStruct(array.shape, jnp.float32)

    results = apply_update(
        images,
        dp_size,
        dict(
            total=total, roots=roots, small_sum=small, table_all=table_all, counts_all=counts_all, stats=kron_stats,
            m_square=mom_square, m_conv=mom_conv, m_qkv=mom_qkv, m_fi=mom_ffin, m_fo=mom_ffout, m_tin=mom_time_in, m_tout=mom_time_out,
            class_table=class_table, table_mean=table_mean, table_var=table_var,
            conv_first=conv_first, first_mean=first_mean, first_var=first_var,
            norms=norm_params, norm_mean=norm_mean, norm_var=norm_var,
            **weights,
        ),
        dict(
            square_new=like(w_square), square_mom=like(w_square), conv_new=like(w_conv), conv_mom=like(w_conv),
            qkv_new=like(w_qkv), qkv_mom=like(w_qkv), fi_new=like(w_ffin), fi_mom=like(w_ffin),
            fo_new=like(w_ffout), fo_mom=like(w_ffout), tin_new=like(w_time_in), tin_mom=like(w_time_in),
            tout_new=like(w_time_out), tout_mom=like(w_time_out), stats_new=like(kron_stats),
            table_new=like(class_table), table_mean_new=like(class_table), table_var_new=like(class_table),
            first_new=like(conv_first), first_mean_new=like(conv_first), first_var_new=like(conv_first),
            norm_new=like(norm_params), norm_mean_new=like(norm_params), norm_var_new=like(norm_params),
            loss_terms=jax.ShapeDtypeStruct((2, NBANDS), jnp.float32),
        ),
    )
    last_rows = small[72:144].reshape(9, 8, -1)
    last_grad = sum(last_rows[:, LAT * k : LAT * k + LAT] for k in range(images)).transpose(0, 2, 1)
    last_out = adam(conv_last, last_mean, last_var, last_grad, rate_last)
    return results[:21] + last_out + results[21:]


def solution(mesh):
    return jax.shard_map(
        local,
        mesh=mesh,
        in_specs=(
            P(DP, None, None),
            P(DP, None, None),
            P(DP),
            P(DP),
            P(DP),
            P(None, DP, MP),
            P(None, DP, MP),
            P(None, DP, MP),
            P(None, DP, MP),
            P(DP, None, MP),
            P(DP, None, MP),
            P(DP, None, MP),
            P(DP, None, MP),
            P(DP, MP),
            P(DP, MP),
            P(DP, MP),
            P(DP, MP),
            P(DP, MP),
            P(DP, MP),
            P(MP, None, None),
            P(None, MP),
            P(None, MP),
            P(None, MP),
            P(None, None, MP),
            P(None, None, MP),
            P(None, None, MP),
            P(None, MP, None),
            P(None, MP, None),
            P(None, MP, None),
            P(None, None, MP),
            P(None, None, MP),
            P(None, None, MP),
        ),
        out_specs=(
            P(None, DP, MP),
            P(None, DP, MP),
            P(None, DP, MP),
            P(None, DP, MP),
            P(DP, None, MP),
            P(DP, None, MP),
            P(DP, None, MP),
            P(DP, None, MP),
            P(DP, MP),
            P(DP, MP),
            P(DP, MP),
            P(DP, MP),
            P(DP, MP),
            P(DP, MP),
            P(MP, None, None),
            P(None, MP),
            P(None, MP),
            P(None, MP),
            P(None, None, MP),
            P(None, None, MP),
            P(None, None, MP),
            P(None, MP, None),
            P(None, MP, None),
            P(None, MP, None),
            P(None, None, MP),
            P(None, None, MP),
            P(None, None, MP),
            P(),
        ),
        check_vma=False,
    )
```

```python
import functools
import math

import jax
import jax.numpy as jnp
from jax import lax
from jax.experimental import pallas as pl
from jax.experimental.pallas import tpu as pltpu
from jax.sharding import PartitionSpec as P

C = 512
GROUPS = 32
HD = 64
TE = 256
NCLS = 1000
LAT = 3
SIDE = 32
NBANDS = 4
NS_ITERS = 6
STEP = 5


LINK = jnp.bfloat16
norm_eps = 1e-05
steps_total = 1000
beta_one = 0.9
beta_two = 0.95
adam_eps = 1e-08
decay = 0.01
shampoo_momentum = 0.9
shampoo_beta = 0.95
shampoo_rate = 0.5
rate_table = 0.5
rate_first = 0.2
rate_last = 0.015
rate_gain = 0.1
score_scale = 0.125
masked_score = -1000000000.0


DP, MP = "dp", "mp"
MESH_ID = pl.DeviceIdType.MESH
VMEM_LIMIT = 60 * 1024 * 1024


def remote(src, dst, send_sem, recv_sem, device):
    return pltpu.make_async_remote_copy(
        src_ref=src, dst_ref=dst, send_sem=send_sem, recv_sem=recv_sem, device_id=device, device_id_type=MESH_ID
    )


def steps(low, high, body):
    if high - low <= 8:
        for index in range(low, high):
            body(index)
    else:
        lax.fori_loop(low, high, lambda index, carry: (body(index), carry)[1], 0)


class Place:
    def __init__(self, dp_size, mp_size):
        self.dp_size = dp_size
        self.mp_size = mp_size
        self.outer_size = dp_size // 2
        self.dp = lax.axis_index(DP)
        self.mp = lax.axis_index(MP)
        self.outer = self.dp // 2
        self.inner = lax.rem(self.dp, 2)

    def at(self, outer, inner):
        return outer * 2 + inner

    def ahead(self, step):
        return lax.rem(self.outer + step, self.outer_size)

    def behind(self, step):
        return lax.rem(self.outer + self.outer_size - step, self.outer_size)

    def partner(self):
        return (self.at(self.outer, 1 - self.inner), self.mp)

    def across(self, step):
        return (self.at(self.ahead(step), self.inner), self.mp)


class Gather:
    def __init__(self, place, shard, full, sems, pieces):
        self.place = place
        self.shard = shard
        self.full = full
        self.out_send, self.out_recv, self.in_send, self.in_recv = sems
        self.pieces = pieces

    def part(self, ref, piece):
        low, count = self.pieces[piece]
        return ref.at[pl.ds(low, count)]

    def slot(self, source, piece):
        low, count = self.pieces[piece]
        return self.full.at[source, pl.ds(low, count)]

    def out_copy(self, piece, step, source):
        return remote(
            self.part(self.shard, piece), self.slot(source, piece), self.out_send.at[piece], self.out_recv.at[piece], self.place.across(step)
        )

    def in_copy(self, piece, source, src=None):
        return remote(
            self.slot(source, piece) if src is None else src,
            self.slot(source, piece),
            self.in_send.at[piece],
            self.in_recv.at[piece],
            self.place.partner(),
        )

    def both(self, piece, count, sems):
        low, number = self.pieces[piece]
        region = self.full.at[pl.ds(0, count), pl.ds(low, number)]
        return remote(region, region, sems[0].at[piece], sems[1].at[piece], self.place.partner())

    def start(self, piece):
        place = self.place
        steps(1, place.outer_size, lambda step: self.out_copy(piece, step, place.dp).start())
        self.in_copy(piece, place.dp, self.part(self.shard, piece)).start()

    def pump(self, piece):
        place = self.place
        self.both(piece, place.outer_size - 1, (self.out_send, self.out_recv)).wait_recv()
        steps(1, place.outer_size, lambda step: self.in_copy(piece, place.at(place.behind(step), place.inner)).start())

    def ready(self, piece):
        self.both(piece, self.place.outer_size, (self.in_send, self.in_recv)).wait_recv()

    def drain(self, piece):
        self.both(piece, self.place.outer_size - 1, (self.out_send, self.out_recv)).wait_send()
        self.both(piece, self.place.outer_size, (self.in_send, self.in_recv)).wait_send()


class Scatter:
    def __init__(self, place, partials, total, near, sums, far, sems, pieces):
        self.place = place
        self.partials = partials
        self.total = total
        self.near = near
        self.sums = sums
        self.far = far
        self.in_send, self.in_recv, self.out_send, self.out_recv = sems
        self.pieces = pieces

    def cut(self, ref, index, piece):
        low, count = self.pieces[piece]
        return ref.at[index, pl.ds(low, count)]

    def in_copy(self, piece, step):
        place = self.place
        return remote(
            self.cut(self.partials, place.at(place.ahead(step), 1 - place.inner), piece),
            self.cut(self.near, step, piece),
            self.in_send.at[piece],
            self.in_recv.at[piece],
            place.partner(),
        )

    def out_copy(self, piece, step):
        return remote(
            self.cut(self.sums, step, piece), self.cut(self.far, step, piece), self.out_send.at[piece], self.out_recv.at[piece], self.place.across(step)
        )

    def both(self, ref, piece, first, sems):
        low, count = self.pieces[piece]
        region = ref.at[pl.ds(first, self.place.outer_size - first), pl.ds(low, count)]
        return remote(region, region, sems[0].at[piece], sems[1].at[piece], self.place.partner())

    def start(self, piece):
        last = self.place.outer_size
        steps(1, last, lambda step: self.in_copy(piece, step).start())
        self.in_copy(piece, 0).start()

    def pump(self, piece):
        place = self.place
        low, count = self.pieces[piece]
        self.both(self.near, piece, 0, (self.in_send, self.in_recv)).wait_recv()

        def one(step):
            mine = self.partials[place.at(place.ahead(step), place.inner), pl.ds(low, count)]
            theirs = self.near[step, pl.ds(low, count)]
            self.sums[step, pl.ds(low, count)] = (
                mine.astype(jnp.float32) + theirs.astype(jnp.float32)
            ).astype(jnp.bfloat16)
            self.out_copy(piece, step).start()

        steps(1, place.outer_size, one)
        self.total[pl.ds(low, count)] = self.partials[
            place.dp, pl.ds(low, count)
        ].astype(jnp.float32) + self.near[0, pl.ds(low, count)].astype(jnp.float32)

    def finish(self, piece):
        low, count = self.pieces[piece]
        self.both(self.far, piece, 1, (self.out_send, self.out_recv)).wait_recv()

        def one(step):
            self.total[pl.ds(low, count)] += self.far[step, pl.ds(low, count)].astype(jnp.float32)

        steps(1, self.place.outer_size, one)

    def drain(self, piece):
        self.both(self.near, piece, 0, (self.in_send, self.in_recv)).wait_send()
        self.both(self.far, piece, 1, (self.out_send, self.out_recv)).wait_send()


def split(values):
    high = values.astype(jnp.bfloat16)
    return high, (values - high.astype(jnp.float32)).astype(jnp.bfloat16)


def dot_nn(left, right):
    return lax.dot_general(left, right, (((1,), (0,)), ((), ())), preferred_element_type=jnp.float32)


def dot_tn(left, right):
    return lax.dot_general(left, right, (((0,), (0,)), ((), ())), preferred_element_type=jnp.float32)


def dot_nt(left, right):
    return lax.dot_general(left, right, (((1,), (1,)), ((), ())), preferred_element_type=jnp.float32)


def exact(left, right):
    left_high, left_low = split(left)
    right_high, right_low = split(right)
    return dot_nn(left_high, right_high) + (dot_nn(left_high, right_low) + dot_nn(left_low, right_high))


def gram_of(values):
    high, low = split(values)
    cross = dot_tn(high, low)
    return dot_tn(high, high) + (cross + cross.T)


TIN, TOUT, SQ0, CONV, QKV, SQ1, SQ2, SQ3, FFOUT, FFIN, SQ4 = range(11)
SQUARES = (SQ0, SQ1, SQ2, SQ3, SQ4)
COUNTS = {TIN: 1, TOUT: 2, SQ0: 1, CONV: 9, QKV: 3, SQ1: 1, SQ2: 1, SQ3: 1, FFOUT: 4, FFIN: 8, SQ4: 1}
STARTS = {name: sum(COUNTS[other] for other in range(name)) for name in COUNTS}
SECTION_COUNT = sum(COUNTS.values())
WINDOW = 2
GATHER_PIECES = ((0, 4), (4, 3), (7, 3), (10, 3), (13, 3), (16, 3), (19, 4), (23, 2), (25, 2), (27, 2), (29, 2), (31, 1))
SCATTER_PIECES = ((31, 1), (27, 4), (23, 4), (19, 4), (13, 4), (17, 2), (3, 1), (4, 3), (7, 3), (10, 3), (0, 3))
BLOCKS = (
    tuple((STARTS[name], 1) for name in SQUARES)
    + ((STARTS[CONV], 9),)
    + tuple((STARTS[QKV] + k, 1) for k in range(3))
    + tuple((STARTS[FFIN] + 2 * k + j, 1) for j in range(2) for k in range(4))
    + ((STARTS[FFOUT], 4), (STARTS[TIN], 1), (STARTS[TIN], 1), (STARTS[TOUT], 2))
)
ORDER = (4, 9, 10, 11, 12, 13, 14, 15, 16, 17, 3, 2, 1, 6, 7, 8, 0, 20, 5, 18, 19)
TIN_BLOCKS = (18, 19)
BY_GRAM = (5, 17, 20)


def inverse_roots(matrices):
    size = matrices[0].shape[-1]
    rows = lax.broadcasted_iota(jnp.int32, (size, size), 0)
    columns = lax.broadcasted_iota(jnp.int32, (size, size), 1)
    identity = (rows == columns).astype(jnp.float32)
    traces = [jnp.sum(matrix * identity) for matrix in matrices]
    current = [matrix * (1.0 / trace) for matrix, trace in zip(matrices, traces)]
    inverse = [identity for _ in matrices]
    for sweep in range(NS_ITERS):
        if sweep == 0:
            middle = [1.5 * identity - 0.5 * c for c in current]
            inverse = middle
        else:
            middle = [1.5 * identity - 0.5 * exact(z, c) for z, c in zip(inverse, current)]
            inverse = [exact(m, z) for m, z in zip(middle, inverse)]
        if sweep < NS_ITERS - 1:
            current = [exact(c, m) for c, m in zip(current, middle)]
    return [z * lax.rsqrt(jnp.full((1, size), trace, jnp.float32)) for z, trace in zip(inverse, traces)]


MID = SIDE // 2
TOKENS = MID * MID
PIXELS = SIDE * SIDE
LANES = 128


def sigmoid(values):
    return 1.0 / (1.0 + jnp.exp(-values))


ERF_TOP = (-2.72614225801306e-10, 2.77068142495902e-08, -2.10102402082508e-06, -5.69250639462346e-05, -7.34990630326855e-04, -2.95459980854025e-03, -1.60960333262415e-02)
ERF_LOW = (-1.45660718464996e-05, -2.13374055278905e-04, -1.68282697438203e-03, -7.37332916720468e-03, -1.42647390514189e-02)


def erf(values):
    values = jnp.clip(values, -4.0, 4.0)
    square = values * values
    top = jnp.full_like(square, ERF_TOP[0])
    for factor in ERF_TOP[1:]:
        top = top * square + factor
    low = jnp.full_like(square, ERF_LOW[0])
    for factor in ERF_LOW[1:]:
        low = low * square + factor
    return values * top / low


def group_sums(rows, spread):
    parts = []
    for row in rows:
        for _ in range(3):
            high = row.astype(jnp.bfloat16)
            parts.append(high)
            row = row - high.astype(jnp.float32)
    parts.append(jnp.zeros((16 - len(parts), LANES), jnp.bfloat16))
    summed = dot_nn(jnp.concatenate([part.astype(jnp.float32) for part in parts], axis=0).astype(jnp.bfloat16), spread)
    return [jnp.sum(summed[3 * k : 3 * k + 3], axis=0, keepdims=True) for k in range(len(rows))]


def column_sum(values):
    return jnp.sum(values, axis=0, keepdims=True)


def norm_stats(values, mask, share, spread):
    centre = group_sums([column_sum(values * mask)], spread)[0] * share
    off = (values - centre) * mask
    variance = group_sums([column_sum(off * off)], spread)[0] * share
    return centre, lax.rsqrt(variance + norm_eps)


def norm_backward(grads, normal, inv_std, mask, gain, share, spread):
    bias_grad = column_sum(grads)
    gain_grad = column_sum(grads * normal)
    first, second = group_sums([bias_grad * gain, gain_grad * gain], spread)
    return (
        inv_std * (grads * gain - mask * (first * share + normal * (second * share))),
        gain_grad,
        bias_grad,
    )


def token_norm(values, gain, bias):
    centre = jnp.mean(values, axis=-1, keepdims=True)
    variance = jnp.mean(values * values, axis=-1, keepdims=True) - centre * centre
    inv_std = lax.rsqrt(variance + norm_eps)
    normal = (values - centre) * inv_std
    return normal * gain + bias, normal, inv_std


def token_norm_backward(grads, normal, inv_std, gain):
    scaled = grads * gain
    width = grads.shape[-1]
    first = jnp.sum(scaled, axis=-1, keepdims=True) * (1.0 / width)
    second = jnp.sum(scaled * normal, axis=-1, keepdims=True) * (1.0 / width)
    return (scaled - first - normal * second) * inv_std, column_sum(grads * normal), column_sum(grads)


def shift_rows(values, rows):
    if rows == 0:
        return values
    count = abs(rows) * MID
    zeros = jnp.zeros((count, values.shape[1]), values.dtype)
    if rows > 0:
        return jnp.concatenate([values[count:], zeros], axis=0)
    return jnp.concatenate([zeros, values[:-count]], axis=0)


(X_NORMS, X_CONTEXT, X_TIME, X_RES, X_NORM, X_FFOUT_W, X_CROSS_VAL, X_CROSS_OUT, X_ATTN, X_FF, X_LAST, X_PREDICTED, X_G_PROJ, X_G_FF, X_GC, X_GV, X_GX, X_G_ATTN, X_G_AT, X_G_IN, X_G_RES, X_GT, X_NORM_SUMS, X_DW_FFOUT) = range(100, 124)


def turn(angle):
    quarter = jnp.floor(angle * (2.0 / math.pi) + 0.5)
    rest = angle - quarter * 1.5703125
    rest = rest - quarter * 4.837512969970703e-04
    rest = rest - quarter * 7.549789948768648e-08
    square = rest * rest
    sine = ((-1.9515295891e-04 * square + 8.3321608736e-03) * square - 1.6666654611e-01) * square * rest + rest
    cosine = ((2.443315711809948e-05 * square - 1.388731625493765e-03) * square + 4.166664568298827e-02) * square
    cosine = cosine * square - 0.5 * square + 1.0
    turns = quarter - 4.0 * jnp.floor(quarter * 0.25)
    odd = (turns == 1.0) | (turns == 3.0)
    first, second = jnp.where(odd, sine, cosine), jnp.where(odd, cosine, sine)
    return (
        jnp.where((turns == 1.0) | (turns == 2.0), -first, first),
        jnp.where(turns >= 2.0, -second, second),
    )


class Model:
    def __init__(self, place, refs, images, dp_size, mp_size):
        self.place = place
        self.r = refs
        self.images = images
        self.dp_size = dp_size
        self.mp_size = mp_size
        self.rows = refs.full.shape[2]
        self.me = place.mp
        self.exchange_ids = {}
        self.relays = {}
        self.pending = []

    def peer(self, step):
        return (self.place.dp, lax.rem(self.me + step, self.mp_size))

    def source(self, step):
        return lax.rem(self.me + self.mp_size - step, self.mp_size)

    def index_of(self, name, part):
        key = (name, part)
        if key not in self.exchange_ids:
            self.exchange_ids[key] = len(self.exchange_ids)
        return self.exchange_ids[key]

    def exchange(self, name, part, target, land):
        index = self.index_of(name, part)
        for step in range(1, self.mp_size):
            other = lax.rem(self.me + step, self.mp_size)
            remote(
                target(other), land(self.me, 1), self.r.ex_send.at[index], self.r.ex_recv.at[index], self.peer(step)
            ).start()
        self.pending.append(self.exchanged(name, part, land))

    def exchanged(self, name, part, land):
        index = self.index_of(name, part)
        region = land(0, self.mp_size - 1)
        return remote(region, region, self.r.ex_send.at[index], self.r.ex_recv.at[index], self.peer(1))

    def pair(self):
        return self.me + 1 - 2 * lax.rem(self.me, 2)

    def beyond(self):
        return lax.rem(self.me + 2, self.mp_size)

    def two_step(self, name, part, ref, cut):
        index = self.index_of(name, part)
        pair, beyond = (self.place.dp, self.pair()), (self.place.dp, self.beyond())
        mine = cut(ref, self.me, 1)
        sems = (self.r.ex_send.at[index], self.r.ex_recv.at[index], self.r.ex_far.at[index])
        remote(mine, mine, sems[0], sems[2], beyond).start()
        remote(mine, mine, sems[0], sems[1], pair).start()
        self.pending.append(self.exchanged(name, part, lambda m, count: cut(ref, m, count)))

        def relay():
            theirs = cut(ref, self.beyond(), 1)
            remote(theirs, theirs, sems[0], sems[2], beyond).wait_recv()
            remote(theirs, theirs, sems[0], sems[1], pair).start()

        self.relays[(name, part)] = relay

    def two_step_wait(self, name, part, ref, cut):
        index = self.index_of(name, part)
        region = cut(ref, 0, 2)
        remote(region, region, self.r.ex_send.at[index], self.r.ex_recv.at[index], self.peer(1)).wait_recv()

    def relay(self, name, part):
        self.relays.pop((name, part))()

    def spread(self, name, part, ref, cut):
        self.exchange(name, part, lambda other: cut(ref, self.me, 1), lambda m, count: cut(ref, m, count))

    def spread_wait(self, name, part, ref, cut):
        self.exchanged(name, part, lambda m, count: cut(ref, m, count)).wait_recv()

    def deal(self, name, part, out, land):
        self.exchange(name, part, out, land)

    def deal_wait(self, name, part, land):
        self.exchanged(name, part, land).wait_recv()

    def drain(self):
        for copies in self.pending:
            copies.wait_send()

    def flat(self, values):
        width = values.shape[-1]
        count = math.prod(values.shape[:-1])
        if values.shape[-2] % 16 == 0:
            return values.reshape(count, width)
        return values.astype(jnp.float32).reshape(count, width).astype(jnp.bfloat16)

    def weight(self, name, k=0):
        return self.flat(self.r.full[:, STARTS[name] + k])

    def weight_rows(self, name, count):
        return self.flat(self.r.full[:, STARTS[name] : STARTS[name] + count])

    def emit(self, name, values, k=0):
        self.r.partials[:, STARTS[name] + k] = values.reshape(self.dp_size, self.rows, LANES).astype(jnp.bfloat16)

    def emit_rows(self, name, values, count):
        low = STARTS[name]
        self.r.partials[:, low : low + count] = values.reshape(self.dp_size, count, self.rows, LANES).astype(jnp.bfloat16)

    def wide(self, ref, m):
        return self.flat(ref[m])

    def wide_mine(self, ref, m):
        share = self.dp_size // self.mp_size
        return self.flat(ref[m, pl.ds(self.me * share, share)])

    def columns(self, image):
        return lambda ref, m, count: ref.at[pl.ds(image * TOKENS, TOKENS), pl.ds(pl.multiple_of(m * LANES, LANES), count * LANES)]

    def token_rows(self, image):
        share = TOKENS // self.mp_size
        return lambda ref, m, count: ref.at[pl.ds(pl.multiple_of(image * TOKENS + m * share, share), count * share)]

    def mine(self):
        return pl.ds(pl.multiple_of(self.me * LANES, LANES), LANES)

    def my_tokens(self):
        share = TOKENS // self.mp_size
        return pl.ds(pl.multiple_of(self.me * share, share), share)

    def image_rows(self, image):
        return pl.ds(image * TOKENS, TOKENS)

    @staticmethod
    def whole_slot(ref, m, count):
        return ref.at[pl.ds(m, count)]

    def across_lanes(self, image):
        key = lax.broadcasted_iota(jnp.int32, (1, TOKENS), 1)
        side = self.r.sides[image] // 2
        return (key // MID < side) & (lax.rem(key, MID) < side)

    def full_lane(self, norm, which):
        return jnp.concatenate([self.r.norms_all[m, norm, which : which + 1] for m in range(self.mp_size)], axis=1)

    def gain(self, norm):
        return self.r.norms[norm, 0:1]

    def bias(self, norm):
        return self.r.norms[norm, 1:2]

    def tap_lanes(self, values, tap):
        i, j = divmod(tap, 3)
        offset = (i - 1) * SIDE + (j - 1)
        moved = values if offset == 0 else pltpu.roll(values, (-offset) % PIXELS, 1)
        pixel = lax.broadcasted_iota(jnp.int32, values.shape, 1)
        row, column = pixel // SIDE + (i - 1), lax.rem(pixel, SIDE) + (j - 1)
        inside = (row >= 0) & (row < SIDE) & (column >= 0) & (column < SIDE)
        return jnp.where(inside, moved, 0.0)

    def greet_all(self, barrier):
        for step in range(1, self.mp_size):
            pl.semaphore_signal(barrier, inc=1, device_id=self.peer(step), device_id_type=MESH_ID)

        def hello(step):
            other = lax.rem(self.place.dp + step, self.dp_size)
            pl.semaphore_signal(barrier, inc=1, device_id=(other, self.me), device_id_type=MESH_ID)

        steps(1, self.dp_size, hello)
        pl.semaphore_wait(barrier, self.mp_size + self.dp_size - 2)

    def pack(self):
        r = self.r
        bf16 = jnp.bfloat16
        rows = self.rows
        for h in range(r.w_tin.shape[1] // LANES):
            stride = r.w_tin.shape[1] // LANES
            r.tin_rows[pl.ds(h, rows // stride, stride=stride)] = r.w_tin[:, h * LANES : (h + 1) * LANES]
        r.shard[STARTS[TIN]] = r.tin_rows[...].astype(bf16)
        r.shard[STARTS[TOUT] : STARTS[TOUT] + 2] = r.w_tout[...].reshape(2, rows, LANES).astype(bf16)
        for k, name in enumerate(SQUARES):
            r.shard[STARTS[name]] = r.w_square[k].astype(bf16)
        r.shard[STARTS[CONV] : STARTS[CONV] + 9] = r.w_conv[...].astype(bf16)
        for j in range(3):
            r.shard[STARTS[QKV] + j] = r.w_qkv[j].astype(bf16)
        r.shard[STARTS[FFOUT] : STARTS[FFOUT] + 4] = r.w_fo[...].reshape(4, rows, LANES).astype(bf16)
        for j in range(2):
            for k in range(4):
                r.shard[STARTS[FFIN] + 2 * k + j] = r.w_fi[:, j, k * LANES : (k + 1) * LANES].astype(bf16)

    def by_row(self, values):
        row = lax.broadcasted_iota(jnp.int32, (8, LANES), 0) // LAT
        total = jnp.zeros((8, LANES), jnp.float32)
        for image in range(self.images):
            total = jnp.where(row == image, values[image], total)
        return total

    def share(self, image, halves):
        side = self.r.sides[image] // halves
        return (GROUPS / C) / jnp.full((1, LANES), side * side, jnp.int32).astype(jnp.float32)

    def prepare(self):
        r = self.r
        images = range(self.images)
        lane = lax.broadcasted_iota(jnp.int32, (8, LANES), 1)
        row = lax.broadcasted_iota(jnp.int32, (8, LANES), 0)
        hot = [(lane[0:1] == r.timesteps[k] * NBANDS // steps_total).astype(jnp.float32) for k in images]
        r.hot8[...] = self.by_row(hot)
        counts = jnp.zeros((1, LANES), jnp.float32)
        for k in images:
            side = r.sides[k]
            counts = counts + hot[k] * jnp.full((1, LANES), LAT * side * side, jnp.int32).astype(jnp.float32)
        r.counts[0] = jnp.where(row == 0, counts, 0.0)
        times = [jnp.full((1, LANES), r.timesteps[k], jnp.int32).astype(jnp.float32) for k in images]
        angle = (0.5 * math.pi / steps_total) * (self.by_row(times) + 0.5)
        cosine, sine = turn(angle)
        r.signal8[...] = cosine
        r.level8[...] = sine
        labels = jnp.zeros((8, LANES), jnp.float32)
        for k in images:
            label = jnp.full((8, LANES), r.labels[k], jnp.int32).astype(jnp.float32)
            labels = jnp.where(row == self.images + k, label, labels)
        r.labels8[...] = labels
        r.context[...] = jnp.zeros((8, LANES), jnp.float32)
        for k in images:
            chosen = r.class_table[pl.ds(r.labels[k], 1), :]
            r.context[k : k + 1] = chosen.astype(jnp.bfloat16).astype(jnp.float32)
        halves = r.embedded.shape[0]
        width = TE * halves
        place = lax.broadcasted_iota(jnp.int32, (8, width), 1)
        channel = place // halves
        half = TE // 2
        frequency = jnp.exp((-math.log(10000.0) / half) * lax.rem(channel, half).astype(jnp.float32))
        row = lax.broadcasted_iota(jnp.int32, (8, width), 0)
        time = jnp.zeros((8, width), jnp.float32)
        for k in images:
            time = jnp.where(row == k, jnp.full((8, width), r.timesteps[k], jnp.int32).astype(jnp.float32), time)
        cosine, sine = turn(time * frequency)
        values = jnp.where(channel < half, cosine, sine)
        for h in range(halves):
            r.embedded[h] = jnp.where((row < self.images) & (lax.rem(place, halves) == h), values, 0.0).astype(jnp.bfloat16)
        r.first_f[...] = jnp.zeros(r.first_f.shape, jnp.float32)
        r.last_f[...] = jnp.zeros(r.last_f.shape, jnp.float32)
        for image in images:
            for tap in range(9):
                low = 8 * tap + LAT * image
                r.first_f[image, low : low + LAT] = r.conv_first[tap]
                r.last_f[image, low : low + LAT] = r.conv_last[tap]
            r.first_w[image] = r.first_f[image].astype(jnp.bfloat16)
            r.last_w[image] = r.last_f[image].astype(jnp.bfloat16)

    def setup(self):
        r = self.r
        lane = lax.broadcasted_iota(jnp.int32, (LANES, LANES), 1) // (C // GROUPS)
        row = lax.broadcasted_iota(jnp.int32, (LANES, LANES), 0) // (C // GROUPS)
        r.group_spread[...] = (lane == row).astype(jnp.bfloat16)
        r.norms_all[self.me] = r.norms[...]
        self.spread(X_NORMS, 0, r.norms_all, self.whole_slot)
        r.context_all[self.me] = r.context[...]
        self.spread(X_CONTEXT, 0, r.context_all, self.whole_slot)
        for image in range(self.images):
            side = r.sides[image]
            pixel = lax.broadcasted_iota(jnp.int32, (PIXELS, LANES), 0)
            r.full_mask[image] = ((pixel // SIDE < side) & (lax.rem(pixel, SIDE) < side)).astype(jnp.float32)
            half = side // 2
            token = lax.broadcasted_iota(jnp.int32, (TOKENS, LANES), 0)
            r.half_mask[image] = ((token // MID < half) & (lax.rem(token, MID) < half)).astype(jnp.float32)
        for image in range(self.images):
            for channel in range(LAT):
                low = LAT * image + channel
                r.latent8[low : low + 1] = r.latent[channel, image : image + 1]
                r.noise8[low : low + 1] = r.noise[channel, image : image + 1]
        rest = LAT * self.images
        r.latent8[rest:] = jnp.zeros((8 - rest, PIXELS), jnp.float32)
        r.noise8[rest:] = jnp.zeros((8 - rest, PIXELS), jnp.float32)
        lane_row = lax.broadcasted_iota(jnp.int32, (8, PIXELS), 0)
        pixel = lax.broadcasted_iota(jnp.int32, (8, PIXELS), 1)
        side = jnp.zeros((8, PIXELS), jnp.int32)
        for image in range(self.images):
            side = jnp.where(lane_row // LAT == image, r.sides[image], side)
        r.lane_mask[...] = ((pixel // SIDE < side) & (lax.rem(pixel, SIDE) < side)).astype(jnp.float32)
        signal, level = r.signal8[:, 0:1], r.level8[:, 0:1]
        noisy = (signal * r.latent8[...] + level * r.noise8[...]) * r.lane_mask[...]
        noisy = noisy.astype(jnp.bfloat16).astype(jnp.float32)
        for tap in range(9):
            r.taps[8 * tap : 8 * tap + 8] = self.tap_lanes(noisy, tap)

    def entry(self, image):
        r = self.r
        first = dot_tn(r.taps[...].astype(jnp.bfloat16), r.first_w[image]) * r.full_mask[image]
        r.first[image] = first
        paired = r.first[image, pl.ds(0, PIXELS // 2, stride=2)] + r.first[image, pl.ds(1, PIXELS // 2, stride=2)]
        pooled = jnp.sum(paired.reshape(MID, 2, MID, LANES), axis=1).reshape(TOKENS, LANES) * 0.25
        r.pooled[image] = pooled
        mask = r.half_mask[image]
        centre, inv_std = norm_stats(pooled, mask, self.share(image, 2), r.group_spread[...])
        values = (pooled - centre) * inv_std * self.gain(0) + self.bias(0)
        r.x_res[self.image_rows(image), self.mine()] = (values * sigmoid(values) * mask).astype(jnp.bfloat16)
        self.two_step(X_RES, image, r.x_res, self.columns(image))

    def time_in(self):
        r = self.r
        table = self.weight(TIN)
        hidden = jnp.concatenate([dot_nn(r.embedded[h], table) for h in range(r.embedded.shape[0])], axis=1)
        r.hidden_time[...] = hidden
        r.time_act[self.me] = (hidden * sigmoid(hidden)).astype(jnp.bfloat16).astype(jnp.float32)
        self.spread(X_TIME, 0, r.time_act, self.whole_slot)

    def time_out(self):
        r = self.r
        self.spread_wait(X_TIME, 0, r.time_act, self.whole_slot)
        table = self.weight_rows(TOUT, 2)
        width = r.time_act.shape[2]
        total = 0.0
        for m in range(self.mp_size):
            total = total + dot_nn(r.time_act[m].astype(jnp.bfloat16), table[m * width : (m + 1) * width])
        r.time_vec[...] = total

    def res_wait(self, image):
        self.two_step_wait(X_RES, image, self.r.x_res, self.columns(image))

    def convolve(self, image, i):
        r = self.r
        values = r.x_res[self.image_rows(image), :]
        for j in range(3):
            moved = shift_rows(dot_nn(values, self.weight(CONV, 3 * i + j)), i - 1)
            if i > 0:
                moved = r.conv_sum[image, j] + moved
            r.conv_sum[image, j] = moved

    def convolved(self, image):
        r = self.r
        column = lax.rem(lax.broadcasted_iota(jnp.int32, (TOKENS, LANES), 0), MID)
        total = r.conv_sum[image, 1]
        total = total + jnp.where(column > 0, pltpu.roll(r.conv_sum[image, 0], 1, 0), 0.0)
        total = total + jnp.where(column < MID - 1, pltpu.roll(r.conv_sum[image, 2], TOKENS - 1, 0), 0.0)
        mask = r.half_mask[image]
        after = r.pooled[image] + (total + r.time_vec[image : image + 1]) * mask
        r.after_res[image] = after
        centre, inv_std = norm_stats(after, mask, self.share(image, 2), r.group_spread[...])
        values = (after - centre) * inv_std * self.gain(1) + self.bias(1)
        r.x_norm[self.image_rows(image), self.mine()] = (values * mask).astype(jnp.bfloat16)
        self.two_step(X_NORM, image, r.x_norm, self.columns(image))

    def share_square(self, name, ref):
        ref[self.me] = self.r.full[:, STARTS[name]]
        self.two_step(name, 0, ref, self.whole_slot)

    def share_square_wait(self, name, ref):
        self.two_step_wait(name, 0, ref, self.whole_slot)

    def hidden_rows(self, ref, m, count):
        share = self.dp_size // self.mp_size
        return ref.at[pl.ds(m * share, count * share), pl.ds(STARTS[FFOUT], 4)]

    def share_ffout(self):
        r = self.r
        share = self.dp_size // self.mp_size
        low = STARTS[FFOUT]
        r.w_ffout[self.me] = r.full[pl.ds(self.me * share, share), low : low + 4]
        self.deal(
            X_FFOUT_W, 0, lambda m: self.hidden_rows(r.full, m, 1), lambda m, count: r.w_ffout.at[m] if count == 1 else r.w_ffout.at[pl.ds(m, count)]
        )

    def share_ffout_wait(self):
        self.deal_wait(X_FFOUT_W, 0, lambda m, count: self.r.w_ffout.at[pl.ds(m, count)])

    def cross_first(self):
        r = self.r
        self.spread_wait(X_CONTEXT, 0, r.context_all, self.whole_slot)
        table = self.weight(SQ2)
        total = 0.0
        for m in range(self.mp_size):
            total = total + dot_nn(r.context_all[m].astype(jnp.bfloat16), table[m * LANES : (m + 1) * LANES])
        r.cross_val[self.me] = total.astype(jnp.bfloat16).astype(jnp.float32)
        self.spread(X_CROSS_VAL, 0, r.cross_val, self.whole_slot)

    def cross_second(self):
        r = self.r
        self.spread_wait(X_CROSS_VAL, 0, r.cross_val, self.whole_slot)
        table = self.weight(SQ3)
        total = 0.0
        for m in range(self.mp_size):
            total = total + dot_nn(r.cross_val[m].astype(jnp.bfloat16), table[m * LANES : (m + 1) * LANES])
        r.cross_out[self.me] = total
        self.spread(X_CROSS_OUT, 0, r.cross_out, self.whole_slot)

    def cross_last(self):
        self.spread_wait(X_CROSS_OUT, 0, self.r.cross_out, self.whole_slot)

    def attention(self, image):
        r = self.r
        self.two_step_wait(X_NORM, image, r.x_norm, self.columns(image))
        values = r.x_norm[self.image_rows(image), :]
        for m in range(self.mp_size):
            r.stream_in[image, :, m * LANES : (m + 1) * LANES] = dot_nn(values, self.wide(r.w_in, m))
        attn_in = token_norm(r.stream_in[image], self.full_lane(2, 0), self.full_lane(2, 1))[0].astype(jnp.bfloat16)
        r.attn_in[self.image_rows(image), :] = attn_in
        for j in range(3):
            r.qkv[j, self.image_rows(image)] = dot_nn(attn_in, self.weight(QKV, j)).astype(jnp.bfloat16)
        keep = self.across_lanes(image)
        lane_head = lax.broadcasted_iota(jnp.int32, (TOKENS, LANES), 1) // HD
        queries, keys, vals = (r.qkv[j, self.image_rows(image)] for j in range(3))
        zero = jnp.zeros((), jnp.bfloat16)
        attended = jnp.zeros((TOKENS, LANES), jnp.float32)
        for head in range(LANES // HD):
            own = lane_head == head
            scores = dot_nt(jnp.where(own, queries, zero), keys) * score_scale
            scores = jnp.where(keep, scores, masked_score)
            peak = jnp.max(scores, axis=-1, keepdims=True)
            expo = jnp.exp(scores - peak)
            probs = expo / jnp.sum(expo, axis=-1, keepdims=True)
            r.probs[image, head] = probs
            attended = jnp.where(own, dot_nn(probs.astype(jnp.bfloat16), vals), attended)
        r.x_attn[self.image_rows(image), self.mine()] = attended.astype(jnp.bfloat16)
        self.two_step(X_ATTN, image, r.x_attn, self.columns(image))

    def feed(self, image):
        r = self.r
        self.two_step_wait(X_ATTN, image, r.x_attn, self.columns(image))
        values = r.x_attn[self.image_rows(image), :]
        for m in range(self.mp_size):
            cut = slice(m * LANES, (m + 1) * LANES)
            r.stream_cross[image, :, cut] = (
                r.stream_in[image, :, cut] + dot_nn(values, self.wide(r.w_attn, m)) + r.cross_out[m, image : image + 1]
            )
        ff_in = token_norm(r.stream_cross[image], self.full_lane(3, 0), self.full_lane(3, 1))[0].astype(jnp.bfloat16)
        r.ff_in[self.image_rows(image), :] = ff_in

    def feed_part(self, image, k):
        r = self.r
        ff_in = r.ff_in[self.image_rows(image), :]
        cut = slice(k * LANES, (k + 1) * LANES)
        value = dot_nn(ff_in, self.weight(FFIN, 2 * k))
        gate = dot_nn(ff_in, self.weight(FFIN, 2 * k + 1))
        r.ff_value[image, :, cut] = value
        r.ff_gate[image, :, cut] = gate
        half = 0.5 * (1.0 + erf(gate * math.sqrt(0.5)))
        r.ff_hidden[self.image_rows(image), cut] = (value * (gate * half)).astype(jnp.bfloat16)

    def feed_out(self, image):
        r = self.r
        hidden = r.ff_hidden[self.image_rows(image), :]
        total = jnp.concatenate([dot_nn(hidden, self.wide_hidden(m)) for m in range(self.mp_size)], axis=1)
        self.deal_sum(X_FF, image, self.by_token(total), r.ff_send, r.ff_land, r.ff_total)

    def by_token(self, values):
        share = TOKENS // self.mp_size
        return [values[m * share : (m + 1) * share] for m in range(self.mp_size)]

    def wide_hidden(self, m):
        return self.flat(self.r.w_ffout[m])

    def deal_sum(self, name, image, parts, send, land, total):
        index = self.index_of(name, image)
        pair, beyond = (self.place.dp, self.pair()), (self.place.dp, self.beyond())
        sems = (self.r.ex_send.at[index], self.r.ex_recv.at[index], self.r.ex_far.at[index])
        for m in range(self.mp_size):
            send[image, m % 2, m // 2] = parts[m].astype(send.dtype)
        core, far = lax.rem(self.me, 2), self.me // 2
        near = remote(send.at[image, 1 - core], land.at[image, pl.ds(0, 2)], sems[0], sems[1], pair)
        near.start()
        away = remote(send.at[image, 2, 0], land.at[image, 2], sems[0], sems[2], beyond)
        self.pending.append(remote(land.at[image], land.at[image], sems[0], sems[1], pair))

        def relay():
            near.wait_recv()
            send[image, 2, 0] = (
                send[image, core, 1 - far].astype(jnp.float32) + land[image, 1 - far].astype(jnp.float32)
            ).astype(send.dtype)
            away.start()
            total[image] = send[image, core, far].astype(jnp.float32) + land[image, far].astype(jnp.float32)

        self.relays[(name, image)] = relay

    def deal_total(self, name, image, land, total):
        index = self.index_of(name, image)
        region = land.at[image, 2]
        remote(region, region, self.r.ex_send.at[index], self.r.ex_far.at[index], self.peer(1)).wait_recv()
        return total[image] + land[image, 2].astype(jnp.float32)

    def leave(self, image):
        r = self.r
        total = self.deal_total(X_FF, image, r.ff_land, r.ff_total)
        stream = (r.stream_cross[image, self.my_tokens(), :] + total).astype(jnp.bfloat16)
        self.token_rows(image)(r.x_last, self.me, 1)[...] = stream
        self.two_step(X_LAST, image, r.x_last, self.token_rows(image))

    def upsample(self, ref, image, values):
        twice = jnp.broadcast_to(values.reshape(MID, 1, MID, LANES), (MID, 2, MID, LANES)).reshape(PIXELS // 2, LANES)
        ref[image, pl.ds(0, PIXELS // 2, stride=2)] = twice
        ref[image, pl.ds(1, PIXELS // 2, stride=2)] = twice

    def finish(self, image):
        r = self.r
        self.two_step_wait(X_LAST, image, r.x_last, self.token_rows(image))
        values = r.x_last[self.image_rows(image), :]
        after = r.after_res[image] + dot_nn(values, self.weight(SQ4)) * r.half_mask[image]
        self.upsample(r.merged, image, after)
        merged = r.merged[image] + r.first[image]
        r.merged[image] = merged
        mask = r.full_mask[image]
        centre, inv_std = norm_stats(merged, mask, self.share(image, 1), r.group_spread[...])
        r.final_stats[image, 0:1] = centre
        r.final_stats[image, 1:2] = inv_std
        values = (merged - centre) * inv_std * self.gain(4) + self.bias(4)
        last_in = (values * sigmoid(values) * mask).astype(jnp.bfloat16)
        r.last_in[image] = last_in
        part = dot_nt(r.last_w[image], last_in)
        if image == 0:
            r.out_taps[...] = part
        else:
            r.out_taps[...] += part

    def predict(self):
        r = self.r
        total = 0.0
        for tap in range(9):
            total = total + self.tap_lanes(r.out_taps[8 * tap : 8 * tap + 8], tap)
        r.predicted[self.me] = total
        self.spread(X_PREDICTED, 0, r.predicted, self.whole_slot)

    def loss(self):
        r = self.r
        self.spread_wait(X_PREDICTED, 0, r.predicted, self.whole_slot)
        predicted = jnp.sum(r.predicted[...], axis=0)
        signal, level = r.signal8[:, 0:1], r.level8[:, 0:1]
        error = (predicted - (signal * r.noise8[...] - level * r.latent8[...])) * r.lane_mask[...]
        per_row = jnp.sum(error * error, axis=1, keepdims=True)
        r.small[88:96] = jnp.broadcast_to(column_sum(per_row * r.hot8[...]), (8, LANES))
        counts = jnp.sum(r.counts_all[...].reshape(-1, 8, LANES), axis=0)[0:1]
        weight = jnp.sum(r.hot8[...] * ((1.0 / NBANDS) / (counts + 1.0)), axis=1, keepdims=True)
        grads = (2.0 * error * weight).astype(jnp.bfloat16).astype(jnp.float32)
        for tap in range(9):
            r.out_taps[8 * tap : 8 * tap + 8] = self.tap_lanes(grads, 8 - tap)

    def pool_sum(self, ref, image):
        paired = ref[image, pl.ds(0, PIXELS // 2, stride=2)] + ref[image, pl.ds(1, PIXELS // 2, stride=2)]
        return jnp.sum(paired.reshape(MID, 2, MID, LANES), axis=1).reshape(TOKENS, LANES)

    def add_small(self, row, image, values, more=False):
        if image == 0 and not more:
            self.r.small[row : row + values.shape[0]] = values
        else:
            self.r.small[row : row + values.shape[0]] += values

    def tap_rows(self, values, image, low):
        row = lax.rem(lax.broadcasted_iota(jnp.int32, values.shape, 0), 8)
        kept = jnp.where(row // LAT == image, values, 0.0)
        shift = (low - LAT * image) % values.shape[0]
        return pltpu.roll(kept, shift, 0) if shift else kept

    def back_last(self, image):
        r = self.r
        grads_taps = r.out_taps[...].astype(jnp.bfloat16)
        mask = r.full_mask[image]
        grads = dot_tn(grads_taps, r.last_w[image]) * mask
        self.add_small(0, image, self.tap_rows(dot_nn(grads_taps, r.last_in[image]), image, LAT))
        inv_std = r.final_stats[image, 1:2]
        normal = (r.merged[image] - r.final_stats[image, 0:1]) * inv_std
        values = normal * self.gain(4) + self.bias(4)
        gate = sigmoid(values)
        grads = grads * (gate * (1.0 + values * (1.0 - gate)))
        grads, gain_grad, bias_grad = norm_backward(
            grads, normal, inv_std, mask, self.gain(4), self.share(image, 1), r.group_spread[...]
        )
        self.add_small(72 + 8, image, gain_grad)
        self.add_small(72 + 9, image, bias_grad)
        r.merged[image] = grads
        after = self.pool_sum(r.merged, image)
        r.grad_after[image] = after
        r.g_proj[self.image_rows(image), self.mine()] = (after * r.half_mask[image]).astype(jnp.bfloat16)
        self.two_step(X_G_PROJ, image, r.g_proj, self.columns(image))

    def back_feed(self, image):
        r = self.r
        self.two_step_wait(X_G_PROJ, image, r.g_proj, self.columns(image))
        total = 0.0
        for m in range(self.mp_size):
            total = total + dot_nt(r.g_proj[self.image_rows(image), m * LANES : (m + 1) * LANES], self.wide(r.w_out, m))
        r.grad_stream[image] = total
        grads_low = total.astype(jnp.bfloat16)
        r.g_ffout[self.image_rows(image), :] = grads_low
        hidden = 0.0
        for m in range(self.mp_size):
            hidden = hidden + dot_nt(grads_low[:, m * LANES : (m + 1) * LANES], self.wide_hidden(m))
        r.g_hidden[...] = hidden
        for k in range(4):
            cut = slice(k * LANES, (k + 1) * LANES)
            value, gate, grads = r.ff_value[image, :, cut], r.ff_gate[image, :, cut], r.g_hidden[:, cut]
            half = 0.5 * (1.0 + erf(gate * math.sqrt(0.5)))
            slope = half + gate * (jnp.exp(-0.5 * gate * gate) * (1.0 / math.sqrt(2.0 * math.pi)))
            r.g_ffin[2 * k, self.image_rows(image)] = (grads * (gate * half)).astype(jnp.bfloat16)
            r.g_ffin[2 * k + 1, self.image_rows(image)] = (grads * value * slope).astype(jnp.bfloat16)
        total = 0.0
        for k in range(8):
            total = total + dot_nt(r.g_ffin[k, self.image_rows(image)], self.weight(FFIN, k))
        self.deal_sum(X_G_FF, image, self.by_token(total), r.gff_send, r.gff_land, r.gff_total)

    def token_back(self, name, image, land, total, stream, norm, row):
        r = self.r
        grads = self.deal_total(name, image, land, total)
        values = stream[image, self.my_tokens(), :]
        gain = self.full_lane(norm, 0)
        _, normal, inv_std = token_norm(values, gain, 0.0)
        grads, gain_grad, bias_grad = token_norm_backward(grads, normal, inv_std, gain)
        for which, values in ((0, gain_grad), (1, bias_grad)):
            for m in range(self.mp_size):
                place = r.norm_send.at[m, row + which : row + which + 1]
                cut = values[:, m * LANES : (m + 1) * LANES]
                place[...] = cut if image == 0 else place[...] + cut
        total = r.grad_stream[image, self.my_tokens(), :] + grads
        r.grad_stream[image, self.my_tokens(), :] = total
        return total

    def back_cross(self, image):
        r = self.r
        total = self.token_back(X_G_FF, image, r.gff_land, r.gff_total, r.stream_cross, 3, 2)
        r.gc_part[self.me, image : image + 1] = column_sum(total)
        self.token_rows(image)(r.g_attn, self.me, 1)[...] = total.astype(jnp.bfloat16)
        self.two_step(X_G_ATTN, image, r.g_attn, self.token_rows(image))

    def cross_one(self):
        r = self.r
        r.gc_part[self.me, self.images :] = jnp.zeros((8 - self.images, C), jnp.float32)
        self.spread(X_GC, 0, r.gc_part, self.whole_slot)

    def cross_two(self):
        r = self.r
        self.spread_wait(X_GC, 0, r.gc_part, self.whole_slot)
        r.gc_full[...] = jnp.sum(r.gc_part[...], axis=0)
        mine = r.gc_full[:, self.mine()].astype(jnp.bfloat16)
        for m in range(self.mp_size):
            r.dw[m * LANES : (m + 1) * LANES] = dot_tn(r.cross_val[m].astype(jnp.bfloat16), mine)
        self.emit(SQ3, r.dw[...])
        r.gv_part[self.me] = dot_nt(mine, self.weight(SQ3))
        self.spread(X_GV, 0, r.gv_part, self.whole_slot)

    def cross_three(self):
        r = self.r
        self.spread_wait(X_GV, 0, r.gv_part, self.whole_slot)
        r.gc_full[...] = jnp.sum(r.gv_part[...], axis=0)
        mine = r.gc_full[:, self.mine()].astype(jnp.bfloat16)
        for m in range(self.mp_size):
            r.dw[m * LANES : (m + 1) * LANES] = dot_tn(r.context_all[m].astype(jnp.bfloat16), mine)
        self.emit(SQ2, r.dw[...])
        r.gx_part[self.me] = dot_nt(mine, self.weight(SQ2))
        self.spread(X_GX, 0, r.gx_part, self.whole_slot)

    def cross_four(self):
        r = self.r
        self.spread_wait(X_GX, 0, r.gx_part, self.whole_slot)
        r.gc_full[...] = jnp.sum(r.gx_part[...], axis=0)
        row = lax.broadcasted_iota(jnp.int32, (8, LANES), 0)
        r.table_rows[0] = jnp.where(row < self.images, r.gc_full[:, self.mine()], r.labels8[...])

    def back_attention(self, image):
        r = self.r
        self.two_step_wait(X_G_ATTN, image, r.g_attn, self.token_rows(image))
        total = 0.0
        for m in range(self.mp_size):
            total = total + dot_nt(r.g_attn[self.image_rows(image), m * LANES : (m + 1) * LANES], self.wide_mine(r.w_attn, m))
        grads = total.astype(jnp.bfloat16)
        queries, keys, vals = (r.qkv[j, self.image_rows(image)] for j in range(3))
        lane_head = lax.broadcasted_iota(jnp.int32, (TOKENS, LANES), 1) // HD
        zero = jnp.zeros((), jnp.bfloat16)
        results = [jnp.zeros((TOKENS, LANES), jnp.float32) for _ in range(3)]
        for head in range(LANES // HD):
            own = lane_head == head
            probs = r.probs[image, head]
            results[2] = jnp.where(own, dot_tn(probs.astype(jnp.bfloat16), grads), results[2])
            grad_probs = dot_nt(jnp.where(own, grads, zero), vals)
            grad_scores = (probs * (grad_probs - jnp.sum(probs * grad_probs, axis=-1, keepdims=True))).astype(jnp.bfloat16)
            results[0] = jnp.where(own, dot_nn(grad_scores, keys) * score_scale, results[0])
            results[1] = jnp.where(own, dot_tn(grad_scores, queries) * score_scale, results[1])
        total = 0.0
        for j in range(3):
            low = results[j].astype(jnp.bfloat16)
            r.g_qkv[j, self.image_rows(image)] = low
            total = total + dot_nt(low, self.weight(QKV, j))
        self.deal_sum(X_G_AT, image, self.by_token(total), r.gat_send, r.gat_land, r.gat_total)

    def back_in(self, image):
        r = self.r
        total = self.token_back(X_G_AT, image, r.gat_land, r.gat_total, r.stream_in, 2, 0)
        self.token_rows(image)(r.g_in, self.me, 1)[...] = total.astype(jnp.bfloat16)
        self.two_step(X_G_IN, image, r.g_in, self.token_rows(image))

    def back_conv(self, image):
        r = self.r
        self.two_step_wait(X_G_IN, image, r.g_in, self.token_rows(image))
        mask = r.half_mask[image]
        grads = 0.0
        for m in range(self.mp_size):
            grads = grads + dot_nt(r.g_in[self.image_rows(image), m * LANES : (m + 1) * LANES], self.wide_mine(r.w_in, m))
        after = r.after_res[image]
        centre, inv_std = norm_stats(after, mask, self.share(image, 2), r.group_spread[...])
        normal = (after - centre) * inv_std
        grads, gain_grad, bias_grad = norm_backward(
            grads * mask, normal, inv_std, mask, self.gain(1), self.share(image, 2), r.group_spread[...]
        )
        self.add_small(72 + 2, image, gain_grad)
        self.add_small(72 + 3, image, bias_grad)
        grads = r.grad_after[image] + grads
        r.grad_after[image] = grads
        masked = grads * mask
        r.grad_time[image : image + 1] = column_sum(masked).astype(jnp.bfloat16).astype(jnp.float32)
        low = masked.astype(jnp.bfloat16).astype(jnp.float32)
        column = lax.rem(lax.broadcasted_iota(jnp.int32, (TOKENS, LANES), 0), MID)
        total = 0.0
        for tap in range(9):
            i, j = divmod(tap, 3)
            moved = shift_rows(low, 1 - i)
            if j == 0:
                moved = jnp.where(column < MID - 1, pltpu.roll(moved, TOKENS - 1, 0), 0.0)
            elif j == 2:
                moved = jnp.where(column > 0, pltpu.roll(moved, 1, 0), 0.0)
            moved = moved.astype(jnp.bfloat16)
            r.g_taps[self.image_rows(image), tap * LANES : (tap + 1) * LANES] = moved
            total = total + dot_nt(moved, self.weight(CONV, tap))
        parts = [total[:, m * LANES : (m + 1) * LANES] for m in range(self.mp_size)]
        self.deal_sum(X_G_RES, image, parts, r.gres_send, r.gres_land, r.gres_total)

    def back_first(self, image):
        r = self.r
        grads = self.deal_total(X_G_RES, image, r.gres_land, r.gres_total)
        mask = r.half_mask[image]
        pooled = r.pooled[image]
        centre, inv_std = norm_stats(pooled, mask, self.share(image, 2), r.group_spread[...])
        normal = (pooled - centre) * inv_std
        values = normal * self.gain(0) + self.bias(0)
        gate = sigmoid(values)
        grads = grads * mask * (gate * (1.0 + values * (1.0 - gate)))
        grads, gain_grad, bias_grad = norm_backward(
            grads, normal, inv_std, mask, self.gain(0), self.share(image, 2), r.group_spread[...]
        )
        self.add_small(72, image, gain_grad)
        self.add_small(72 + 1, image, bias_grad)
        self.upsample(r.first, image, 0.25 * (r.grad_after[image] + grads))
        low = ((r.merged[image] + r.first[image]) * r.full_mask[image]).astype(jnp.bfloat16)
        self.add_small(0, image, self.tap_rows(dot_nn(r.taps[...].astype(jnp.bfloat16), low), image, 0), True)

    def back_time(self):
        r = self.r
        r.grad_time[self.images :] = jnp.zeros((8 - self.images, LANES), jnp.float32)
        grads = r.grad_time[...].astype(jnp.bfloat16)
        width = r.time_act.shape[2]
        for m in range(self.mp_size):
            r.dw_time[m * width : (m + 1) * width] = dot_tn(r.time_act[m].astype(jnp.bfloat16), grads)
        self.emit_rows(TOUT, r.dw_time[...], 2)
        total = dot_nt(grads, self.weight_rows(TOUT, 2))
        for m in range(self.mp_size):
            r.gt_send[m] = total[:, m * width : (m + 1) * width]
        r.gt_land[self.me] = r.gt_send[self.me]
        self.deal(X_GT, 0, lambda m: r.gt_send.at[pl.ds(m, 1)], lambda m, count: r.gt_land.at[pl.ds(m, count)])
        r.norm_land[self.me] = r.norm_send[self.me]
        self.deal(X_NORM_SUMS, 0, lambda m: r.norm_send.at[pl.ds(m, 1)], lambda m, count: r.norm_land.at[pl.ds(m, count)])

    def back_time_in(self):
        r = self.r
        self.deal_wait(X_GT, 0, lambda m, count: r.gt_land.at[pl.ds(m, count)])
        grads = jnp.sum(r.gt_land[...], axis=0)
        hidden = r.hidden_time[...]
        gate = sigmoid(hidden)
        grads = (grads * (gate * (1.0 + hidden * (1.0 - gate)))).astype(jnp.bfloat16)
        total = 0.0
        for h in range(r.embedded.shape[0]):
            total = total + dot_tn(r.embedded[h], grads[:, h * LANES : (h + 1) * LANES])
        self.emit(TIN, total)
        self.deal_wait(X_NORM_SUMS, 0, lambda m, count: r.norm_land.at[pl.ds(m, count)])
        r.small[72 + 4 : 72 + 8] = jnp.sum(r.norm_land[...], axis=0)[0:4]
        r.small[72 + 10 : 88] = jnp.zeros((6, LANES), jnp.float32)

    def grads_out(self):
        r = self.r
        self.emit(SQ4, dot_tn(r.x_last[...], r.g_proj[:, self.mine()]))

    def grads_ffout(self):
        r = self.r
        share = self.dp_size // self.mp_size
        for m in range(self.mp_size):
            part = dot_tn(r.ff_hidden[...], r.g_ffout[:, m * LANES : (m + 1) * LANES])
            r.dw_ffout[m] = part.reshape(share, 4, self.rows, LANES).astype(jnp.bfloat16)
        low = STARTS[FFOUT]
        r.partials[pl.ds(self.me * share, share), low : low + 4] = r.dw_ffout[self.me]
        self.deal(X_DW_FFOUT, 0, lambda m: r.dw_ffout.at[m], lambda m, count: self.hidden_rows(r.partials, m, count))

    def grads_ffout_wait(self):
        self.deal_wait(X_DW_FFOUT, 0, lambda m, count: self.hidden_rows(self.r.partials, m, count))

    def grads_ffin(self):
        for k in range(8):
            self.emit(FFIN, dot_tn(self.r.ff_in[...], self.r.g_ffin[k]), k)

    def grads_attn(self):
        r = self.r
        self.emit(SQ1, dot_tn(r.x_attn[...], r.g_attn[:, self.mine()]))

    def grads_qkv(self):
        for j in range(3):
            self.emit(QKV, dot_tn(self.r.attn_in[...], self.r.g_qkv[j]), j)

    def grads_in(self):
        r = self.r
        self.emit(SQ0, dot_tn(r.x_norm[...], r.g_in[:, self.mine()]))

    def grads_conv(self, i):
        r = self.r
        for tap in range(3 * i, 3 * i + 3):
            self.emit(CONV, dot_tn(r.x_res[...], r.g_taps[:, tap * LANES : (tap + 1) * LANES]), tap)


SMALL_ROWS = 96
EXCHANGES = 40


def model_scratch(images, dp_size, mp_size, rows, time_local, hidden_local):
    bf16, f32 = jnp.bfloat16, jnp.float32
    tokens = images * TOKENS
    share = TOKENS // mp_size
    wide = lambda kind: pltpu.VMEM((tokens, C), kind)
    per_image = lambda width, kind=f32: pltpu.VMEM((images, TOKENS, width), kind)
    send = lambda: pltpu.VMEM((images, 3, 2, share, C), LINK)
    land = lambda: pltpu.VMEM((images, 3, share, C), LINK)
    own = lambda: pltpu.VMEM((images, share, C), f32)
    tiny = lambda width: pltpu.VMEM((mp_size, 8, width), f32)
    square = lambda: pltpu.VMEM((mp_size, dp_size, rows, LANES), bf16)
    dma = pltpu.SemaphoreType.DMA((EXCHANGES,))
    return dict(
        ex_send=dma, ex_recv=dma, ex_far=dma,
        group_spread=pltpu.VMEM((LANES, LANES), bf16),
        norms_all=pltpu.VMEM((mp_size, 5, 2, LANES), f32),
        context_all=tiny(LANES), time_act=tiny(time_local), cross_val=tiny(LANES), cross_out=tiny(LANES),
        full_mask=pltpu.VMEM((images, PIXELS, LANES), f32), half_mask=per_image(LANES),
        latent8=pltpu.VMEM((8, PIXELS), f32), noise8=pltpu.VMEM((8, PIXELS), f32), lane_mask=pltpu.VMEM((8, PIXELS), f32),
        taps=pltpu.VMEM((72, PIXELS), f32), out_taps=pltpu.VMEM((72, PIXELS), f32),
        first=pltpu.VMEM((images, PIXELS, LANES), f32), merged=pltpu.VMEM((images, PIXELS, LANES), f32),
        last_in=pltpu.VMEM((images, PIXELS, LANES), bf16),
        pooled=per_image(LANES), after_res=per_image(LANES), grad_after=per_image(LANES),
        final_stats=pltpu.VMEM((images, 8, LANES), f32),
        hidden_time=pltpu.VMEM((8, time_local), f32), time_vec=pltpu.VMEM((8, LANES), f32), grad_time=pltpu.VMEM((8, LANES), f32),
        x_res=wide(bf16), x_norm=wide(bf16), x_attn=wide(bf16), x_last=wide(bf16),
        g_proj=wide(bf16), g_ffout=wide(bf16), g_attn=wide(bf16), g_in=wide(bf16),
        attn_in=wide(bf16), ff_in=wide(bf16), ff_hidden=pltpu.VMEM((tokens, hidden_local), bf16),
        stream_in=per_image(C), stream_cross=per_image(C), grad_stream=per_image(C),
        ff_value=per_image(hidden_local), ff_gate=per_image(hidden_local),
        g_hidden=pltpu.VMEM((TOKENS, hidden_local), f32), g_ffin=pltpu.VMEM((8, tokens, LANES), bf16),
        qkv=pltpu.VMEM((3, tokens, LANES), bf16), g_qkv=pltpu.VMEM((3, tokens, LANES), bf16),
        probs=pltpu.VMEM((images, LANES // HD, TOKENS, TOKENS), f32),
        w_in=square(), w_attn=square(), w_out=square(),
        w_ffout=pltpu.VMEM((mp_size, dp_size // mp_size, 4, rows, LANES), bf16),
        dw_ffout=pltpu.VMEM((mp_size, dp_size // mp_size, 4, rows, LANES), bf16),
        ff_send=send(), ff_land=land(), ff_total=own(), gff_send=send(), gff_land=land(), gff_total=own(),
        gat_send=send(), gat_land=land(), gat_total=own(),
        gres_send=pltpu.VMEM((images, 3, 2, TOKENS, LANES), LINK), gres_land=pltpu.VMEM((images, 3, TOKENS, LANES), LINK),
        gres_total=per_image(LANES),
        predicted=pltpu.VMEM((mp_size, 8, PIXELS), f32),
        norm_send=tiny(LANES), norm_land=tiny(LANES),
        gc_part=tiny(C), gv_part=tiny(C), gx_part=tiny(C), gc_full=pltpu.VMEM((8, C), f32),
        dw=pltpu.VMEM((C, LANES), f32), dw_time=pltpu.VMEM((mp_size * time_local, LANES), f32),
        gt_send=tiny(time_local), gt_land=tiny(time_local),
        conv_sum=pltpu.VMEM((images, 3, TOKENS, LANES), f32),
        hot8=pltpu.VMEM((8, LANES), f32), signal8=pltpu.VMEM((8, LANES), f32), level8=pltpu.VMEM((8, LANES), f32),
        labels8=pltpu.VMEM((8, LANES), f32), context=pltpu.VMEM((8, LANES), f32), counts=pltpu.VMEM((1, 8, LANES), f32),
        embedded=pltpu.VMEM((time_local // LANES, 8, TE * time_local // LANES), bf16),
        first_f=pltpu.VMEM((images, 72, LANES), f32), last_f=pltpu.VMEM((images, 72, LANES), f32),
        first_w=pltpu.VMEM((images, 72, LANES), bf16), last_w=pltpu.VMEM((images, 72, LANES), bf16),
        tin_rows=pltpu.VMEM((rows, LANES), f32), shard=pltpu.VMEM((SECTION_COUNT, rows, LANES), bf16),
        full=pltpu.VMEM((dp_size, SECTION_COUNT, rows, LANES), bf16), partials=pltpu.VMEM((dp_size, SECTION_COUNT, rows, LANES), bf16),
        small=pltpu.VMEM((SMALL_ROWS, LANES), f32), table_rows=pltpu.VMEM((1, 8, LANES), f32),
        g_taps=pltpu.VMEM((tokens, 9 * LANES), bf16),
    )


class Reducer:
    def __init__(self, place, refs, dp_size):
        self.place = place
        self.r = refs
        self.dp_size = dp_size
        r = refs
        self.scatter = Scatter(
            place, r.partials, r.total, r.near, r.sums, r.far, (r.sc_a, r.sc_b, r.sc_c, r.sc_d), SCATTER_PIECES
        )
        self.slots = r.gram_low.shape[0]
        self.gather = Gather(
            place, r.gram_low, r.grams, (r.ro_a, r.ro_b, r.ro_c, r.ro_d), tuple((s, 1) for s in range(self.slots))
        )
        self.table = Gather(place, r.table_rows, r.table_all, (r.ta_a, r.ta_b, r.ta_c, r.ta_d), ((0, 1),))
        self.started, self.pumped, self.finished, self.sent = 0, 0, 0, set()

    def start(self, count):
        while self.started < count:
            self.scatter.start(self.started)
            self.started += 1

    def pump(self, count):
        while self.pumped < count:
            self.scatter.pump(self.pumped)
            self.pumped += 1

    def finish(self, count):
        while self.finished < count:
            self.scatter.finish(self.finished)
            low, sections = SCATTER_PIECES[self.finished]
            self.r.total_low[pl.ds(low, sections)] = self.r.total[pl.ds(low, sections)].astype(jnp.bfloat16)
            self.finished += 1
            done = {k for start, number in SCATTER_PIECES[: self.finished] for k in range(start, start + number)}
            for position, block in enumerate(ORDER):
                low, sections = BLOCKS[block]
                if position not in self.sent and all(k in done for k in range(low, low + sections)):
                    self.sent.add(position)
                    self.send_block(position)

    def owned_by(self, positions):
        owner = self.place.dp == positions[0] % self.dp_size
        for position in positions[1:]:
            owner = owner | (self.place.dp == position % self.dp_size)
        return owner

    def block_copy(self, position, other, source, count=1):
        r = self.r
        block = ORDER[position]
        slot = position // self.dp_size
        if block in BY_GRAM:
            out, land = r.gram_out.at[BY_GRAM.index(block)], r.gram_land
        else:
            out, land = r.total_low.at[BLOCKS[block][0]], r.rows_land
        land = land.at[slot, source] if count == 1 else land.at[slot, pl.ds(source, count)]
        return remote(
            out if count == 1 else land, land, r.bl_send.at[position], r.bl_recv.at[slot], (other, self.place.mp)
        )

    def send_block(self, position):
        r = self.r
        place = self.place
        block = ORDER[position]
        low, sections = BLOCKS[block]
        owner, slot = position % self.dp_size, position // self.dp_size
        if block in BY_GRAM:
            values = r.total[pl.ds(low, sections)].reshape(-1, LANES)
            r.gram_out[BY_GRAM.index(block)] = gram_of(values).astype(jnp.bfloat16)

        @pl.when(place.dp != owner)
        def _():
            self.block_copy(position, owner, place.dp).start()

        @pl.when(place.dp == owner)
        def _():
            if block in BY_GRAM:
                r.gram_land[slot, place.dp] = r.gram_out[BY_GRAM.index(block)]
            else:
                r.rows_land[slot, place.dp] = r.total_low[low]

    def gram(self, slot):
        r = self.r
        place = self.place
        positions = [p for p in range(len(ORDER)) if p // self.dp_size == slot]
        kinds = (
            [p for p in positions if ORDER[p] in BY_GRAM],
            [p for p in positions if ORDER[p] in TIN_BLOCKS],
            [p for p in positions if ORDER[p] not in BY_GRAM + TIN_BLOCKS],
        )
        for kind, members in enumerate(kinds):
            if not members:
                continue

            @pl.when(self.owned_by(members))
            def _(kind=kind, members=members):
                other = lax.rem(place.dp + 1, self.dp_size)
                self.block_copy(members[0], other, 0, self.dp_size - 1).wait_recv()
                if kind == 0:
                    r.gram_own[slot] = jnp.sum(r.gram_land[slot].astype(jnp.float32), axis=0)
                    return
                values = r.rows_land[slot]
                if values.shape[1] % 16 == 0 and kind == 2:
                    values = values.reshape(-1, LANES)
                else:
                    values = values.astype(jnp.float32).reshape(-1, LANES)
                    if kind == 1:
                        parity = lax.rem(lax.broadcasted_iota(jnp.int32, values.shape, 0), len(TIN_BLOCKS))
                        values = jnp.where(parity == place.dp - members[0] % self.dp_size, values, 0.0)
                    values = values.astype(jnp.bfloat16)
                r.gram_own[slot] = dot_tn(values, values)

    def share(self, slot):
        r = self.r
        self.gram(slot)
        r.gram_low[slot] = r.gram_own[slot].astype(jnp.bfloat16)
        self.gather.start(slot)
        r.grams[self.place.dp, slot] = r.gram_low[slot]

    def root(self, slot):
        r = self.r
        self.gather.ready(slot)
        positions = [p for p in range(len(ORDER)) if p // self.dp_size == slot]
        renewed = [
            shampoo_beta * r.stats[ORDER[p]] + r.grams[p % self.dp_size, slot].astype(jnp.float32) for p in positions
        ]
        for position, root in zip(positions, inverse_roots(renewed)):
            r.roots[ORDER[position]] = root

    def small_copy(self):
        r = self.r
        return remote(r.small, r.small_near, r.sm_send.at[0], r.sm_recv.at[0], self.place.partner())

    def far_copy(self, step, count=1):
        r = self.r
        return remote(
            r.small_far.at[pl.ds(0, count)], r.small_far.at[pl.ds(step, count)], r.sm_send.at[1], r.sm_recv.at[1], self.place.across(step)
        )

    def small_start(self):
        self.small_copy().start()
        self.table.start(0)
        self.r.table_all[self.place.dp] = self.r.table_rows[...]

    def small_pump(self):
        r = self.r
        self.small_copy().wait_recv()
        r.small_far[0] = r.small[...] + r.small_near[...]
        steps(1, self.place.outer_size, lambda step: self.far_copy(step).start())
        self.table.pump(0)

    def small_finish(self):
        r = self.r
        self.far_copy(1, self.place.outer_size - 1).wait_recv()
        r.small_sum[...] = jnp.sum(r.small_far[...], axis=0)
        self.table.ready(0)

    def drain(self):
        for piece in range(len(SCATTER_PIECES)):
            self.scatter.drain(piece)
        for slot in range(self.slots):
            self.gather.drain(slot)
        self.table.drain(0)
        self.small_copy().wait_send()
        self.far_copy(1, self.place.outer_size - 1).wait_send()
        for position in range(len(ORDER)):
            @pl.when(self.place.dp != position % self.dp_size)
            def _(position=position):
                self.block_copy(position, position % self.dp_size, self.place.dp).wait_send()


def reducer_scratch(dp_size, rows):
    bf16, f32 = jnp.bfloat16, jnp.float32
    outer = dp_size // 2
    slots = -(-len(ORDER) // dp_size)
    dma = pltpu.SemaphoreType.DMA
    held = lambda: pltpu.VMEM((outer, SECTION_COUNT, rows, LANES), bf16)
    scatter_sem = dma((len(SCATTER_PIECES),))
    gather_sem = dma((len(GATHER_PIECES),))
    root_sem = dma((slots,))
    one_sem = dma((1,))
    return dict(
        near=held(), sums=held(), far=held(),
        total_low=pltpu.VMEM((SECTION_COUNT, rows, LANES), bf16),
        gram_out=pltpu.VMEM((len(BY_GRAM), LANES, LANES), bf16),
        gram_land=pltpu.VMEM((slots, dp_size, LANES, LANES), bf16),
        rows_land=pltpu.VMEM((slots, dp_size, rows, LANES), bf16),
        gram_own=pltpu.VMEM((slots, LANES, LANES), f32),
        gram_low=pltpu.VMEM((slots, LANES, LANES), bf16),
        small_near=pltpu.VMEM((SMALL_ROWS, LANES), f32), small_far=pltpu.VMEM((outer, SMALL_ROWS, LANES), f32),
        sc_a=scatter_sem, sc_b=scatter_sem, sc_c=scatter_sem, sc_d=scatter_sem,
        ga_a=gather_sem, ga_b=gather_sem, ga_c=gather_sem, ga_d=gather_sem,
        ro_a=root_sem, ro_b=root_sem, ro_c=root_sem, ro_d=root_sem,
        ta_a=one_sem, ta_b=one_sem, ta_c=one_sem, ta_d=one_sem,
        co_a=one_sem, co_b=one_sem, co_c=one_sem, co_d=one_sem,
        sm_send=dma((2,)), sm_recv=dma((2,)),
        bl_send=dma((len(ORDER),)), bl_recv=dma((slots,)),
    )


class Refs:
    pass


def step_kernel(images, dp_size, mp_size, names, *refs):
    r = Refs()
    for name, ref in zip(names, refs):
        setattr(r, name, ref)
    place = Place(dp_size, mp_size)
    model = Model(place, r, images, dp_size, mp_size)
    reducer = Reducer(place, r, dp_size)
    weights = Gather(place, r.shard, r.full, (r.ga_a, r.ga_b, r.ga_c, r.ga_d), GATHER_PIECES)
    counts = Gather(place, r.counts, r.counts_all, (r.co_a, r.co_b, r.co_c, r.co_d), ((0, 1),))
    every = range(images)
    slots = list(range(reducer.slots))

    def each(stage, *rest):
        return [functools.partial(stage, image, *rest) for image in every]

    def own():
        r.full[place.dp] = r.shard[...]
        r.counts_all[place.dp] = r.counts[...]

    def do(function, *rest):
        return [functools.partial(function, *rest)]

    def pump(piece):
        weights.pump(piece)
        if piece + WINDOW < len(GATHER_PIECES):
            weights.start(piece + WINDOW)

    model.greet_all(pltpu.get_barrier_semaphore())
    def relay(name):
        return [functools.partial(model.relay, name, image) for image in every]

    schedule = do(model.pack)
    for piece in range(WINDOW):
        schedule += do(weights.start, piece)
    schedule += do(model.prepare) + do(counts.start, 0) + do(own) + do(model.setup)
    schedule += each(model.entry) + relay(X_RES) + do(pump, 0) + do(counts.pump, 0) + do(pump, 1)
    schedule += do(weights.ready, 0) + do(model.time_in) + do(model.share_square, SQ0, r.w_in)
    schedule += do(pump, 2) + do(model.time_out) + do(model.relay, SQ0, 0) + each(model.res_wait)
    for i in range(3):
        schedule += do(weights.ready, 1 + i) + each(model.convolve, i) + do(pump, 3 + i)
    schedule += each(model.convolved) + do(model.spread_wait, X_NORMS, 0, r.norms_all, model.whole_slot) + relay(X_NORM)
    schedule += do(model.share_square_wait, SQ0, r.w_in) + do(weights.ready, 4)
    schedule += do(model.attention, 0) + do(pump, 6) + do(weights.ready, 5)
    schedule += do(model.share_square, SQ1, r.w_attn) + do(model.cross_first) + do(model.attention, 1)
    schedule += do(model.relay, SQ1, 0) + relay(X_ATTN) + do(pump, 7) + do(weights.ready, 6) + do(model.share_ffout) + do(model.cross_second)
    schedule += do(model.share_square_wait, SQ1, r.w_attn) + do(pump, 8) + do(model.cross_last)
    schedule += each(model.feed)
    for k in range(4):
        schedule += do(weights.ready, 7 + k) + each(model.feed_part, k)
        schedule += do(pump, 9 + k) if k < 3 else []
    schedule += do(model.share_ffout_wait) + each(model.feed_out) + relay(X_FF)
    schedule += each(model.leave) + relay(X_LAST) + do(weights.ready, 11) + do(model.share_square, SQ4, r.w_out) + do(counts.ready, 0)
    schedule += each(model.finish) + do(model.predict) + do(model.relay, SQ4, 0)
    schedule += do(model.share_square_wait, SQ4, r.w_out) + do(model.loss) + each(model.back_last)
    schedule += relay(X_G_PROJ) + do(model.grads_out) + do(reducer.start, 1) + each(model.back_feed) + relay(X_G_FF) + do(model.grads_ffin)
    schedule += do(reducer.start, 3) + each(model.back_cross) + do(model.cross_one) + relay(X_G_ATTN)
    schedule += do(model.grads_ffout) + each(model.back_attention) + relay(X_G_AT) + do(reducer.pump, 2)
    schedule += do(model.cross_two) + do(model.grads_attn) + do(model.grads_qkv) + do(model.grads_ffout_wait) + do(reducer.start, 5)
    schedule += each(model.back_in) + relay(X_G_IN) + do(model.cross_three) + do(reducer.start, 6) + do(reducer.pump, 4)
    schedule += each(model.back_conv) + relay(X_G_RES) + do(model.grads_in) + do(reducer.start, 7)
    schedule += do(model.grads_conv, 0) + do(reducer.start, 8) + do(model.back_time)
    schedule += do(model.grads_conv, 1) + do(reducer.start, 9) + do(reducer.pump, 7)
    schedule += do(model.grads_conv, 2) + do(reducer.start, 10) + do(model.back_time_in) + do(reducer.start, 11) + do(reducer.pump, 8)
    schedule += do(model.back_first, 0) + do(reducer.pump, 9) + do(model.back_first, 1) + do(reducer.pump, 10)
    schedule += do(reducer.finish, 4) + do(reducer.pump, 11) + do(model.cross_four) + do(reducer.small_start) + do(reducer.finish, 6)
    schedule += do(reducer.finish, 9) + do(reducer.small_pump)
    for slot in slots[:-1]:
        schedule += do(reducer.share, slot)
    schedule += do(reducer.finish, 11)
    for slot in slots[:-1]:
        schedule += do(reducer.gather.pump, slot)
    schedule += do(reducer.share, slots[-1])
    for slot in slots[:-1]:
        schedule += do(reducer.root, slot)
        schedule += do(reducer.gather.pump, slots[-1]) if slot == slots[-2] else []
    schedule += do(reducer.gather.pump, slots[-1]) if len(slots) == 1 else []
    schedule += do(reducer.root, slots[-1]) + do(reducer.small_finish)
    schedule += do(model.drain) + do(reducer.drain)
    for piece in range(len(GATHER_PIECES)):
        schedule += do(weights.drain, piece)
    schedule += do(counts.drain, 0)
    for action in schedule:
        action()


def train_step(images, dp_size, mp_size, scalars, arrays):
    vmem = pl.BlockSpec(memory_space=pltpu.VMEM)
    smem = pl.BlockSpec(memory_space=pltpu.SMEM)
    rows = arrays["w_square"].shape[1]
    f32, bf16 = jnp.float32, jnp.bfloat16
    slots = -(-len(ORDER) // dp_size)
    outs = dict(
        total=jax.ShapeDtypeStruct((SECTION_COUNT, rows, LANES), f32),
        grams=jax.ShapeDtypeStruct((dp_size, slots, LANES, LANES), bf16),
        roots=jax.ShapeDtypeStruct((len(ORDER), LANES, LANES), f32),
        small_sum=jax.ShapeDtypeStruct((SMALL_ROWS, LANES), f32),
        table_all=jax.ShapeDtypeStruct((dp_size, 1, 8, LANES), f32),
        counts_all=jax.ShapeDtypeStruct((dp_size, 1, 8, LANES), f32),
    )
    time_local = arrays["w_tin"].shape[1]
    hidden_local = arrays["w_fi"].shape[2]
    scratch = model_scratch(images, dp_size, mp_size, rows, time_local, hidden_local)
    scratch.update(reducer_scratch(dp_size, rows))
    names = list(scalars) + list(arrays) + list(outs) + list(scratch)
    return pl.pallas_call(
        functools.partial(step_kernel, images, dp_size, mp_size, names),
        out_shape=tuple(outs.values()),
        in_specs=[smem] * len(scalars) + [vmem] * len(arrays),
        out_specs=(vmem,) * len(outs),
        scratch_shapes=list(scratch.values()),
        compiler_params=pltpu.CompilerParams(
            collective_id=1, has_side_effects=True, vmem_limit_bytes=VMEM_LIMIT
        ),
        name="train_step",
    )(*scalars.values(), *arrays.values())


def adam(weight, mean, variance, gradient, rate):
    mean = beta_one * mean + (1 - beta_one) * gradient
    variance = beta_two * variance + (1 - beta_two) * gradient * gradient
    step = mean * (1.0 / (1 - beta_one**STEP)) / (jnp.sqrt(variance * (1.0 / (1 - beta_two**STEP))) + adam_eps)
    return weight - rate * (step + decay * weight), mean, variance


def update_kernel(images, dp_size, names, *refs):
    r = Refs()
    for name, ref in zip(names, refs):
        setattr(r, name, ref)
    rows = r.total.shape[1]
    parity = lax.rem(lax.broadcasted_iota(jnp.int32, (rows, LANES), 0), 2)
    where = {block: (position % dp_size, position // dp_size) for position, block in enumerate(ORDER)}
    for block in range(len(ORDER)):
        owner, slot = where[block]
        r.stats_new[block] = shampoo_beta * r.stats[block] + r.grams[owner, slot].astype(jnp.float32)

    def turned(moment, block):
        return exact(moment, r.roots[block])

    def renew(section, block, old, momentum):
        moment = shampoo_momentum * momentum + r.total[section]
        return old - shampoo_rate * (turned(moment, block) + decay * old), moment

    for k, name in enumerate(SQUARES):
        r.square_new[k], r.square_mom[k] = renew(STARTS[name], k, r.w_square[k], r.m_square[k])
    for k in range(9):
        r.conv_new[k], r.conv_mom[k] = renew(STARTS[CONV] + k, 5, r.w_conv[k], r.m_conv[k])
    for j in range(3):
        r.qkv_new[j], r.qkv_mom[j] = renew(STARTS[QKV] + j, 6 + j, r.w_qkv[j], r.m_qkv[j])
    for k in range(8):
        j, cut = k // 4, slice(k % 4 * LANES, (k % 4 + 1) * LANES)
        new, moment = renew(STARTS[FFIN] + 2 * (k % 4) + j, 9 + k, r.w_fi[:, j, cut], r.m_fi[:, j, cut])
        r.fi_new[:, j, cut] = new
        r.fi_mom[:, j, cut] = moment
    for k in range(4):
        cut = slice(k * rows, (k + 1) * rows)
        r.fo_new[cut], r.fo_mom[cut] = renew(STARTS[FFOUT] + k, 17, r.w_fo[cut], r.m_fo[cut])
    for k in range(2):
        cut = slice(k * rows, (k + 1) * rows)
        r.tout_new[cut], r.tout_mom[cut] = renew(STARTS[TOUT] + k, 20, r.w_tout[cut], r.m_tout[cut])
    halves = r.w_tin.shape[1] // LANES
    r.tin_rows[0] = r.total[STARTS[TIN]]
    for h in range(halves):
        cut = slice(h * LANES, (h + 1) * LANES)
        gradient = r.tin_rows[0, pl.ds(h, rows // halves, stride=halves)]
        moment = shampoo_momentum * r.m_tin[:, cut] + gradient
        r.tin_mom[:, cut] = moment
        old = r.w_tin[:, cut]
        r.tin_new[:, cut] = old - shampoo_rate * (turned(moment, 18 + h) + decay * old)
    for tap in range(9):
        r.first_grad[tap] = r.small_sum[8 * tap : 8 * tap + LAT]
        r.last_grad[tap] = r.small_sum[8 * tap + LAT : 8 * tap + 2 * LAT]
    r.first_new[...], r.first_mean_new[...], r.first_var_new[...] = adam(
        r.conv_first[...], r.first_mean[...], r.first_var[...], r.first_grad[...], rate_first
    )
    r.last_new[...], r.last_mean_new[...], r.last_var_new[...] = adam(
        r.conv_last[...], r.last_mean[...], r.last_var[...], r.last_grad[...], rate_last
    )
    for k in range(5):
        gradient = r.small_sum[72 + 2 * k : 74 + 2 * k]
        r.norm_new[k], r.norm_mean_new[k], r.norm_var_new[k] = adam(
            r.norms[k], r.norm_mean[k], r.norm_var[k], gradient, rate_gain
        )
    count = r.class_table.shape[0]
    row = lax.broadcasted_iota(jnp.int32, (count, LANES), 0).astype(jnp.float32)
    r.table_grad[...] = jnp.zeros((count, LANES), jnp.float32)

    def add(source):
        for image in range(images):
            label = r.table_all[source, 0, images + image : images + image + 1]
            gradient = r.table_all[source, 0, image : image + 1]
            r.table_grad[...] += jnp.where(row == label, gradient, 0.0)

    steps(0, dp_size, add)
    r.table_new[...], r.table_mean_new[...], r.table_var_new[...] = adam(
        r.class_table[...], r.table_mean[...], r.table_var[...], r.table_grad[...], rate_table
    )
    counts = jnp.sum(r.counts_all[...].reshape(dp_size, 8, LANES), axis=0)
    r.loss_terms[0:1] = r.small_sum[88:89, 0:NBANDS]
    r.loss_terms[1:2] = counts[0:1, 0:NBANDS]


def apply_update(images, dp_size, arrays, outs):
    vmem = pl.BlockSpec(memory_space=pltpu.VMEM)
    rows = arrays["total"].shape[1]
    scratch = dict(
        tin_rows=pltpu.VMEM((1, rows, LANES), jnp.float32),
        first_grad=pltpu.VMEM(arrays["conv_first"].shape, jnp.float32),
        last_grad=pltpu.VMEM(arrays["conv_first"].shape, jnp.float32),
        table_grad=pltpu.VMEM(arrays["class_table"].shape, jnp.float32),
    )
    names = list(arrays) + list(outs) + list(scratch)
    return pl.pallas_call(
        functools.partial(update_kernel, images, dp_size, names),
        out_shape=tuple(outs.values()),
        in_specs=[vmem] * len(arrays),
        out_specs=(vmem,) * len(outs),
        scratch_shapes=list(scratch.values()),
        compiler_params=pltpu.CompilerParams(vmem_limit_bytes=VMEM_LIMIT),
        name="apply_update",
    )(*arrays.values())


def local(
    clean_latent,
    noise_latent,
    timesteps,
    labels,
    image_sides,
    w_square,
    mom_square,
    w_conv,
    mom_conv,
    w_qkv,
    mom_qkv,
    w_ffin,
    mom_ffin,
    w_ffout,
    mom_ffout,
    w_time_in,
    mom_time_in,
    w_time_out,
    mom_time_out,
    kron_stats,
    class_table,
    table_mean,
    table_var,
    conv_first,
    first_mean,
    first_var,
    conv_last,
    last_mean,
    last_var,
    norm_params,
    norm_mean,
    norm_var,
):
    dp_size = lax.axis_size(DP)
    mp_size = lax.axis_size(MP)
    images = clean_latent.shape[0]
    weights = dict(
        w_square=w_square, w_conv=w_conv, w_qkv=w_qkv.transpose(1, 0, 2), w_fi=w_ffin, w_fo=w_ffout, w_tin=w_time_in, w_tout=w_time_out
    )
    total, grams, roots, small, table_all, counts_all = train_step(
        images,
        dp_size,
        mp_size,
        dict(timesteps=timesteps, labels=labels, sides=image_sides),
        dict(
            latent=clean_latent.transpose(1, 0, 2),
            noise=noise_latent.transpose(1, 0, 2),
            class_table=class_table,
            norms=norm_params,
            conv_first=conv_first,
            conv_last=conv_last.transpose(0, 2, 1),
            stats=kron_stats,
            **weights,
        ),
    )

    def like(array):
        return jax.ShapeDtypeStruct(array.shape, jnp.float32)

    results = apply_update(
        images,
        dp_size,
        dict(
            total=total, grams=grams, roots=roots, small_sum=small, table_all=table_all, counts_all=counts_all, stats=kron_stats,
            m_square=mom_square, m_conv=mom_conv, m_qkv=mom_qkv.transpose(1, 0, 2), m_fi=mom_ffin, m_fo=mom_ffout, m_tin=mom_time_in, m_tout=mom_time_out,
            class_table=class_table, table_mean=table_mean, table_var=table_var,
            conv_first=conv_first, first_mean=first_mean, first_var=first_var,
            conv_last=conv_last.transpose(0, 2, 1), last_mean=last_mean.transpose(0, 2, 1), last_var=last_var.transpose(0, 2, 1),
            norms=norm_params, norm_mean=norm_mean, norm_var=norm_var,
            **weights,
        ),
        dict(
            square_new=like(w_square), square_mom=like(w_square), conv_new=like(w_conv), conv_mom=like(w_conv),
            qkv_new=like(weights["w_qkv"]), qkv_mom=like(weights["w_qkv"]), fi_new=like(w_ffin), fi_mom=like(w_ffin),
            fo_new=like(w_ffout), fo_mom=like(w_ffout), tin_new=like(w_time_in), tin_mom=like(w_time_in),
            tout_new=like(w_time_out), tout_mom=like(w_time_out), stats_new=like(kron_stats),
            table_new=like(class_table), table_mean_new=like(class_table), table_var_new=like(class_table),
            first_new=like(conv_first), first_mean_new=like(conv_first), first_var_new=like(conv_first),
            last_new=like(conv_first), last_mean_new=like(conv_first), last_var_new=like(conv_first),
            norm_new=like(norm_params), norm_mean_new=like(norm_params), norm_var_new=like(norm_params),
            loss_terms=jax.ShapeDtypeStruct((2, NBANDS), jnp.float32),
        ),
    )
    qkv_out = tuple(array.transpose(1, 0, 2) for array in results[4:6])
    last_out = tuple(array.transpose(0, 2, 1) for array in results[21:24])
    return results[:4] + qkv_out + results[6:21] + last_out + results[24:]


def solution(mesh):
    return jax.shard_map(
        local,
        mesh=mesh,
        in_specs=(
            P(DP, None, None),
            P(DP, None, None),
            P(DP),
            P(DP),
            P(DP),
            P(None, DP, MP),
            P(None, DP, MP),
            P(None, DP, MP),
            P(None, DP, MP),
            P(DP, None, MP),
            P(DP, None, MP),
            P(DP, None, MP),
            P(DP, None, MP),
            P(DP, MP),
            P(DP, MP),
            P(DP, MP),
            P(DP, MP),
            P(DP, MP),
            P(DP, MP),
            P(MP, None, None),
            P(None, MP),
            P(None, MP),
            P(None, MP),
            P(None, None, MP),
            P(None, None, MP),
            P(None, None, MP),
            P(None, MP, None),
            P(None, MP, None),
            P(None, MP, None),
            P(None, None, MP),
            P(None, None, MP),
            P(None, None, MP),
        ),
        out_specs=(
            P(None, DP, MP),
            P(None, DP, MP),
            P(None, DP, MP),
            P(None, DP, MP),
            P(DP, None, MP),
            P(DP, None, MP),
            P(DP, None, MP),
            P(DP, None, MP),
            P(DP, MP),
            P(DP, MP),
            P(DP, MP),
            P(DP, MP),
            P(DP, MP),
            P(DP, MP),
            P(MP, None, None),
            P(None, MP),
            P(None, MP),
            P(None, MP),
            P(None, None, MP),
            P(None, None, MP),
            P(None, None, MP),
            P(None, MP, None),
            P(None, MP, None),
            P(None, MP, None),
            P(None, None, MP),
            P(None, None, MP),
            P(None, None, MP),
            P(),
        ),
        check_vma=False,
    )
```

```python
import functools
import math

import jax
import jax.numpy as jnp
from jax import lax
from jax.experimental import pallas as pl
from jax.experimental.pallas import tpu as pltpu
from jax.sharding import PartitionSpec as P

C = 512
GROUPS = 32
HD = 64
TE = 256
NCLS = 1000
LAT = 3
SIDE = 32
NBANDS = 4
NS_ITERS = 6
STEP = 5


LINK = jnp.bfloat16
norm_eps = 1e-05
steps_total = 1000
beta_one = 0.9
beta_two = 0.95
adam_eps = 1e-08
decay = 0.01
shampoo_momentum = 0.9
shampoo_beta = 0.95
shampoo_rate = 0.5
rate_table = 0.5
rate_first = 0.2
rate_last = 0.015
rate_gain = 0.1
score_scale = 0.125
masked_score = -1000000000.0


DP, MP = "dp", "mp"
MESH_ID = pl.DeviceIdType.MESH
VMEM_LIMIT = 60 * 1024 * 1024


def remote(src, dst, send_sem, recv_sem, device):
    return pltpu.make_async_remote_copy(
        src_ref=src, dst_ref=dst, send_sem=send_sem, recv_sem=recv_sem, device_id=device, device_id_type=MESH_ID
    )


def steps(low, high, body):
    if high - low <= 8:
        for index in range(low, high):
            body(index)
    else:
        lax.fori_loop(low, high, lambda index, carry: (body(index), carry)[1], 0)


class Place:
    def __init__(self, dp_size, mp_size):
        self.dp_size = dp_size
        self.mp_size = mp_size
        self.outer_size = dp_size // 2
        self.dp = lax.axis_index(DP)
        self.mp = lax.axis_index(MP)
        self.outer = self.dp // 2
        self.inner = lax.rem(self.dp, 2)

    def at(self, outer, inner):
        return outer * 2 + inner

    def ahead(self, step):
        return lax.rem(self.outer + step, self.outer_size)

    def behind(self, step):
        return lax.rem(self.outer + self.outer_size - step, self.outer_size)

    def partner(self):
        return (self.at(self.outer, 1 - self.inner), self.mp)

    def across(self, step):
        return (self.at(self.ahead(step), self.inner), self.mp)


class Gather:
    def __init__(self, place, shard, full, sems, pieces):
        self.place = place
        self.shard = shard
        self.full = full
        self.out_send, self.out_recv, self.in_send, self.in_recv = sems
        self.pieces = pieces

    def part(self, ref, piece):
        low, count = self.pieces[piece]
        return ref.at[pl.ds(low, count)]

    def slot(self, source, piece):
        low, count = self.pieces[piece]
        return self.full.at[source, pl.ds(low, count)]

    def out_copy(self, piece, step, source):
        return remote(
            self.part(self.shard, piece), self.slot(source, piece), self.out_send.at[piece], self.out_recv.at[piece], self.place.across(step)
        )

    def in_copy(self, piece, source, src=None):
        return remote(
            self.slot(source, piece) if src is None else src,
            self.slot(source, piece),
            self.in_send.at[piece],
            self.in_recv.at[piece],
            self.place.partner(),
        )

    def both(self, piece, count, sems):
        low, number = self.pieces[piece]
        region = self.full.at[pl.ds(0, count), pl.ds(low, number)]
        return remote(region, region, sems[0].at[piece], sems[1].at[piece], self.place.partner())

    def start(self, piece):
        place = self.place
        steps(1, place.outer_size, lambda step: self.out_copy(piece, step, place.dp).start())
        self.in_copy(piece, place.dp, self.part(self.shard, piece)).start()

    def pump(self, piece):
        place = self.place
        self.both(piece, place.outer_size - 1, (self.out_send, self.out_recv)).wait_recv()
        steps(1, place.outer_size, lambda step: self.in_copy(piece, place.at(place.behind(step), place.inner)).start())

    def ready(self, piece):
        self.both(piece, self.place.outer_size, (self.in_send, self.in_recv)).wait_recv()

    def drain(self, piece):
        self.both(piece, self.place.outer_size - 1, (self.out_send, self.out_recv)).wait_send()
        self.both(piece, self.place.outer_size, (self.in_send, self.in_recv)).wait_send()


class Scatter:
    def __init__(self, place, partials, total, near, sums, far, sems, pieces):
        self.place = place
        self.partials = partials
        self.total = total
        self.near = near
        self.sums = sums
        self.far = far
        self.in_send, self.in_recv, self.out_send, self.out_recv = sems
        self.pieces = pieces

    def cut(self, ref, index, piece):
        low, count = self.pieces[piece]
        return ref.at[index, pl.ds(low, count)]

    def in_copy(self, piece, step):
        place = self.place
        return remote(
            self.cut(self.partials, place.at(place.ahead(step), 1 - place.inner), piece),
            self.cut(self.near, step, piece),
            self.in_send.at[piece],
            self.in_recv.at[piece],
            place.partner(),
        )

    def out_copy(self, piece, step):
        return remote(
            self.cut(self.sums, step, piece), self.cut(self.far, step, piece), self.out_send.at[piece], self.out_recv.at[piece], self.place.across(step)
        )

    def both(self, ref, piece, first, sems):
        low, count = self.pieces[piece]
        region = ref.at[pl.ds(first, self.place.outer_size - first), pl.ds(low, count)]
        return remote(region, region, sems[0].at[piece], sems[1].at[piece], self.place.partner())

    def start(self, piece):
        last = self.place.outer_size
        steps(1, last, lambda step: self.in_copy(piece, step).start())
        self.in_copy(piece, 0).start()

    def pump(self, piece):
        place = self.place
        low, count = self.pieces[piece]
        self.both(self.near, piece, 0, (self.in_send, self.in_recv)).wait_recv()

        def one(step):
            mine = self.partials[place.at(place.ahead(step), place.inner), pl.ds(low, count)]
            theirs = self.near[step, pl.ds(low, count)]
            self.sums[step, pl.ds(low, count)] = (
                mine.astype(jnp.float32) + theirs.astype(jnp.float32)
            ).astype(jnp.bfloat16)
            self.out_copy(piece, step).start()

        steps(1, place.outer_size, one)
        self.total[pl.ds(low, count)] = self.partials[
            place.dp, pl.ds(low, count)
        ].astype(jnp.float32) + self.near[0, pl.ds(low, count)].astype(jnp.float32)

    def finish(self, piece):
        low, count = self.pieces[piece]
        self.both(self.far, piece, 1, (self.out_send, self.out_recv)).wait_recv()

        def one(step):
            self.total[pl.ds(low, count)] += self.far[step, pl.ds(low, count)].astype(jnp.float32)

        steps(1, self.place.outer_size, one)

    def drain(self, piece):
        self.both(self.near, piece, 0, (self.in_send, self.in_recv)).wait_send()
        self.both(self.far, piece, 1, (self.out_send, self.out_recv)).wait_send()


def split(values):
    high = values.astype(jnp.bfloat16)
    return high, (values - high.astype(jnp.float32)).astype(jnp.bfloat16)


def dot_nn(left, right):
    return lax.dot_general(left, right, (((1,), (0,)), ((), ())), preferred_element_type=jnp.float32)


def dot_tn(left, right):
    return lax.dot_general(left, right, (((0,), (0,)), ((), ())), preferred_element_type=jnp.float32)


def dot_nt(left, right):
    return lax.dot_general(left, right, (((1,), (1,)), ((), ())), preferred_element_type=jnp.float32)


def exact(left, right):
    left_high, left_low = split(left)
    right_high, right_low = split(right)
    return dot_nn(left_high, right_high) + (dot_nn(left_high, right_low) + dot_nn(left_low, right_high))


def gram_of(values):
    high, low = split(values)
    cross = dot_tn(high, low)
    return dot_tn(high, high) + (cross + cross.T)


TIN, TOUT, SQ0, CONV, QKV, SQ1, SQ2, SQ3, FFOUT, FFIN, SQ4 = range(11)
SQUARES = (SQ0, SQ1, SQ2, SQ3, SQ4)
COUNTS = {TIN: 1, TOUT: 2, SQ0: 1, CONV: 9, QKV: 3, SQ1: 1, SQ2: 1, SQ3: 1, FFOUT: 4, FFIN: 8, SQ4: 1}
STARTS = {name: sum(COUNTS[other] for other in range(name)) for name in COUNTS}
SECTION_COUNT = sum(COUNTS.values())
WINDOW = 2
GATHER_PIECES = ((0, 4), (4, 3), (7, 3), (10, 3), (13, 3), (16, 3), (19, 4), (23, 2), (25, 2), (27, 2), (29, 2), (31, 1))
SCATTER_PIECES = ((31, 1), (27, 4), (23, 4), (19, 4), (13, 4), (17, 2), (3, 1), (4, 3), (7, 3), (0, 3), (10, 3))
BLOCKS = (
    tuple((STARTS[name], 1) for name in SQUARES)
    + ((STARTS[CONV], 9),)
    + tuple((STARTS[QKV] + k, 1) for k in range(3))
    + tuple((STARTS[FFIN] + 2 * k + j, 1) for j in range(2) for k in range(4))
    + ((STARTS[FFOUT], 4), (STARTS[TIN], 1), (STARTS[TIN], 1), (STARTS[TOUT], 2))
)
ORDER = (4, 9, 10, 11, 12, 13, 14, 15, 16, 17, 3, 2, 1, 6, 7, 8, 0, 20, 5, 18, 19)
TIN_BLOCKS = (18, 19)
BY_GRAM = (5, 17, 20)


def inverse_roots(matrices):
    size = matrices[0].shape[-1]
    rows = lax.broadcasted_iota(jnp.int32, (size, size), 0)
    columns = lax.broadcasted_iota(jnp.int32, (size, size), 1)
    identity = (rows == columns).astype(jnp.float32)
    traces = [jnp.sum(matrix * identity) for matrix in matrices]
    current = [matrix * (1.0 / trace) for matrix, trace in zip(matrices, traces)]
    inverse = [identity for _ in matrices]
    for sweep in range(NS_ITERS):
        if sweep == 0:
            middle = [1.5 * identity - 0.5 * c for c in current]
            inverse = middle
        else:
            middle = [1.5 * identity - 0.5 * exact(z, c) for z, c in zip(inverse, current)]
            inverse = [exact(m, z) for m, z in zip(middle, inverse)]
        if sweep < NS_ITERS - 1:
            current = [exact(c, m) for c, m in zip(current, middle)]
    return [z * lax.rsqrt(jnp.full((1, size), trace, jnp.float32)) for z, trace in zip(inverse, traces)]


MID = SIDE // 2
TOKENS = MID * MID
PIXELS = SIDE * SIDE
LANES = 128


def sigmoid(values):
    return 1.0 / (1.0 + jnp.exp(-values))


ERF_TOP = (-2.72614225801306e-10, 2.77068142495902e-08, -2.10102402082508e-06, -5.69250639462346e-05, -7.34990630326855e-04, -2.95459980854025e-03, -1.60960333262415e-02)
ERF_LOW = (-1.45660718464996e-05, -2.13374055278905e-04, -1.68282697438203e-03, -7.37332916720468e-03, -1.42647390514189e-02)


def erf(values):
    values = jnp.clip(values, -4.0, 4.0)
    square = values * values
    top = jnp.full_like(square, ERF_TOP[0])
    for factor in ERF_TOP[1:]:
        top = top * square + factor
    low = jnp.full_like(square, ERF_LOW[0])
    for factor in ERF_LOW[1:]:
        low = low * square + factor
    return values * top / low


def group_sums(rows, spread):
    parts = []
    for row in rows:
        for _ in range(3):
            high = row.astype(jnp.bfloat16)
            parts.append(high)
            row = row - high.astype(jnp.float32)
    parts.append(jnp.zeros((16 - len(parts), LANES), jnp.bfloat16))
    summed = dot_nn(jnp.concatenate([part.astype(jnp.float32) for part in parts], axis=0).astype(jnp.bfloat16), spread)
    return [jnp.sum(summed[3 * k : 3 * k + 3], axis=0, keepdims=True) for k in range(len(rows))]


def column_sum(values):
    return jnp.sum(values, axis=0, keepdims=True)


def norm_stats(values, mask, share, spread):
    centre = group_sums([column_sum(values * mask)], spread)[0] * share
    off = (values - centre) * mask
    variance = group_sums([column_sum(off * off)], spread)[0] * share
    return centre, lax.rsqrt(variance + norm_eps)


def norm_backward(grads, normal, inv_std, mask, gain, share, spread):
    bias_grad = column_sum(grads)
    gain_grad = column_sum(grads * normal)
    first, second = group_sums([bias_grad * gain, gain_grad * gain], spread)
    return (
        inv_std * (grads * gain - mask * (first * share + normal * (second * share))),
        gain_grad,
        bias_grad,
    )


def token_norm(values, gain, bias):
    centre = jnp.mean(values, axis=-1, keepdims=True)
    variance = jnp.mean(values * values, axis=-1, keepdims=True) - centre * centre
    inv_std = lax.rsqrt(variance + norm_eps)
    normal = (values - centre) * inv_std
    return normal * gain + bias, normal, inv_std


def token_norm_backward(grads, normal, inv_std, gain):
    scaled = grads * gain
    width = grads.shape[-1]
    first = jnp.sum(scaled, axis=-1, keepdims=True) * (1.0 / width)
    second = jnp.sum(scaled * normal, axis=-1, keepdims=True) * (1.0 / width)
    return (scaled - first - normal * second) * inv_std, column_sum(grads * normal), column_sum(grads)


def shift_rows(values, rows):
    if rows == 0:
        return values
    count = abs(rows) * MID
    zeros = jnp.zeros((count, values.shape[1]), values.dtype)
    if rows > 0:
        return jnp.concatenate([values[count:], zeros], axis=0)
    return jnp.concatenate([zeros, values[:-count]], axis=0)


(X_NORMS, X_CONTEXT, X_TIME, X_RES, X_NORM, X_FFOUT_W, X_CROSS_VAL, X_CROSS_OUT, X_ATTN, X_FF, X_LAST, X_PREDICTED, X_G_PROJ, X_G_FF, X_GC, X_GV, X_GX, X_G_ATTN, X_G_AT, X_G_IN, X_G_RES, X_GT, X_NORM_SUMS, X_DW_FFOUT) = range(100, 124)


def turn(angle):
    quarter = jnp.floor(angle * (2.0 / math.pi) + 0.5)
    rest = angle - quarter * 1.5703125
    rest = rest - quarter * 4.837512969970703e-04
    rest = rest - quarter * 7.549789948768648e-08
    square = rest * rest
    sine = ((-1.9515295891e-04 * square + 8.3321608736e-03) * square - 1.6666654611e-01) * square * rest + rest
    cosine = ((2.443315711809948e-05 * square - 1.388731625493765e-03) * square + 4.166664568298827e-02) * square
    cosine = cosine * square - 0.5 * square + 1.0
    turns = quarter - 4.0 * jnp.floor(quarter * 0.25)
    odd = (turns == 1.0) | (turns == 3.0)
    first, second = jnp.where(odd, sine, cosine), jnp.where(odd, cosine, sine)
    return (
        jnp.where((turns == 1.0) | (turns == 2.0), -first, first),
        jnp.where(turns >= 2.0, -second, second),
    )


class Model:
    def __init__(self, place, refs, images, dp_size, mp_size):
        self.place = place
        self.r = refs
        self.images = images
        self.dp_size = dp_size
        self.mp_size = mp_size
        self.rows = refs.full.shape[2]
        self.me = place.mp
        self.exchange_ids = {}
        self.relays = {}
        self.pending = []

    def peer(self, step):
        return (self.place.dp, lax.rem(self.me + step, self.mp_size))

    def source(self, step):
        return lax.rem(self.me + self.mp_size - step, self.mp_size)

    def index_of(self, name, part):
        key = (name, part)
        if key not in self.exchange_ids:
            self.exchange_ids[key] = len(self.exchange_ids)
        return self.exchange_ids[key]

    def exchange(self, name, part, target, land):
        index = self.index_of(name, part)
        for step in range(1, self.mp_size):
            other = lax.rem(self.me + step, self.mp_size)
            remote(
                target(other), land(self.me, 1), self.r.ex_send.at[index], self.r.ex_recv.at[index], self.peer(step)
            ).start()
        self.pending.append(self.exchanged(name, part, land))

    def exchanged(self, name, part, land):
        index = self.index_of(name, part)
        region = land(0, self.mp_size - 1)
        return remote(region, region, self.r.ex_send.at[index], self.r.ex_recv.at[index], self.peer(1))

    def pair(self):
        return self.me + 1 - 2 * lax.rem(self.me, 2)

    def beyond(self):
        return lax.rem(self.me + 2, self.mp_size)

    def two_step(self, name, part, ref, cut):
        index = self.index_of(name, part)
        pair, beyond = (self.place.dp, self.pair()), (self.place.dp, self.beyond())
        mine = cut(ref, self.me, 1)
        sems = (self.r.ex_send.at[index], self.r.ex_recv.at[index], self.r.ex_far.at[index])
        remote(mine, mine, sems[0], sems[2], beyond).start()
        remote(mine, mine, sems[0], sems[1], pair).start()
        self.pending.append(self.exchanged(name, part, lambda m, count: cut(ref, m, count)))

        def relay():
            theirs = cut(ref, self.beyond(), 1)
            remote(theirs, theirs, sems[0], sems[2], beyond).wait_recv()
            remote(theirs, theirs, sems[0], sems[1], pair).start()

        self.relays[(name, part)] = relay

    def two_step_wait(self, name, part, ref, cut):
        if (name, part) in self.relays:
            self.relay(name, part)
        index = self.index_of(name, part)
        region = cut(ref, 0, 2)
        remote(region, region, self.r.ex_send.at[index], self.r.ex_recv.at[index], self.peer(1)).wait_recv()

    def relay(self, name, part):
        self.relays.pop((name, part))()

    def spread(self, name, part, ref, cut):
        self.exchange(name, part, lambda other: cut(ref, self.me, 1), lambda m, count: cut(ref, m, count))

    def spread_wait(self, name, part, ref, cut):
        self.exchanged(name, part, lambda m, count: cut(ref, m, count)).wait_recv()

    def deal(self, name, part, out, land):
        self.exchange(name, part, out, land)

    def deal_wait(self, name, part, land):
        self.exchanged(name, part, land).wait_recv()

    def drain(self):
        for copies in self.pending:
            copies.wait_send()

    def flat(self, values):
        width = values.shape[-1]
        count = math.prod(values.shape[:-1])
        if values.shape[-2] % 16 == 0:
            return values.reshape(count, width)
        return values.astype(jnp.float32).reshape(count, width).astype(jnp.bfloat16)

    def weight(self, name, k=0):
        return self.flat(self.r.full[:, STARTS[name] + k])

    def weight_rows(self, name, count):
        return self.flat(self.r.full[:, STARTS[name] : STARTS[name] + count])

    def emit(self, name, values, k=0):
        self.r.partials[:, STARTS[name] + k] = values.reshape(self.dp_size, self.rows, LANES).astype(jnp.bfloat16)

    def emit_rows(self, name, values, count):
        low = STARTS[name]
        self.r.partials[:, low : low + count] = values.reshape(self.dp_size, count, self.rows, LANES).astype(jnp.bfloat16)

    def wide(self, ref, m):
        return self.flat(ref[m])

    def wide_mine(self, ref, m):
        share = self.dp_size // self.mp_size
        return self.flat(ref[m, pl.ds(self.me * share, share)])

    def columns(self, image):
        return lambda ref, m, count: ref.at[pl.ds(image * TOKENS, TOKENS), pl.ds(pl.multiple_of(m * LANES, LANES), count * LANES)]

    def token_rows(self, image):
        share = TOKENS // self.mp_size
        return lambda ref, m, count: ref.at[pl.ds(pl.multiple_of(image * TOKENS + m * share, share), count * share)]

    def mine(self):
        return pl.ds(pl.multiple_of(self.me * LANES, LANES), LANES)

    def my_tokens(self):
        share = TOKENS // self.mp_size
        return pl.ds(pl.multiple_of(self.me * share, share), share)

    def image_rows(self, image):
        return pl.ds(image * TOKENS, TOKENS)

    @staticmethod
    def whole_slot(ref, m, count):
        return ref.at[pl.ds(m, count)]

    def across_lanes(self, image):
        key = lax.broadcasted_iota(jnp.int32, (1, TOKENS), 1)
        side = self.r.sides[image] // 2
        return (key // MID < side) & (lax.rem(key, MID) < side)

    def full_lane(self, norm, which):
        return jnp.concatenate([self.r.norms_all[m, norm, which : which + 1] for m in range(self.mp_size)], axis=1)

    def gain(self, norm):
        return self.r.norms[norm, 0:1]

    def bias(self, norm):
        return self.r.norms[norm, 1:2]

    def tap_lanes(self, values, tap):
        i, j = divmod(tap, 3)
        offset = (i - 1) * SIDE + (j - 1)
        moved = values if offset == 0 else pltpu.roll(values, (-offset) % PIXELS, 1)
        pixel = lax.broadcasted_iota(jnp.int32, values.shape, 1)
        row, column = pixel // SIDE + (i - 1), lax.rem(pixel, SIDE) + (j - 1)
        inside = (row >= 0) & (row < SIDE) & (column >= 0) & (column < SIDE)
        return jnp.where(inside, moved, 0.0)

    def greet_all(self, barrier):
        for step in range(1, self.mp_size):
            pl.semaphore_signal(barrier, inc=1, device_id=self.peer(step), device_id_type=MESH_ID)

        def hello(step):
            other = lax.rem(self.place.dp + step, self.dp_size)
            pl.semaphore_signal(barrier, inc=1, device_id=(other, self.me), device_id_type=MESH_ID)

        steps(1, self.dp_size, hello)
        pl.semaphore_wait(barrier, self.mp_size + self.dp_size - 2)

    def pack(self):
        r = self.r
        bf16 = jnp.bfloat16
        rows = self.rows
        for h in range(r.w_tin.shape[1] // LANES):
            stride = r.w_tin.shape[1] // LANES
            r.tin_rows[pl.ds(h, rows // stride, stride=stride)] = r.w_tin[:, h * LANES : (h + 1) * LANES]
        r.shard[STARTS[TIN]] = r.tin_rows[...].astype(bf16)
        r.shard[STARTS[TOUT] : STARTS[TOUT] + 2] = r.w_tout[...].reshape(2, rows, LANES).astype(bf16)
        for k, name in enumerate(SQUARES):
            r.shard[STARTS[name]] = r.w_square[k].astype(bf16)
        r.shard[STARTS[CONV] : STARTS[CONV] + 9] = r.w_conv[...].astype(bf16)
        for j in range(3):
            r.shard[STARTS[QKV] + j] = r.w_qkv[j].astype(bf16)
        r.shard[STARTS[FFOUT] : STARTS[FFOUT] + 4] = r.w_fo[...].reshape(4, rows, LANES).astype(bf16)
        for j in range(2):
            for k in range(4):
                r.shard[STARTS[FFIN] + 2 * k + j] = r.w_fi[:, j, k * LANES : (k + 1) * LANES].astype(bf16)

    def by_row(self, values):
        row = lax.broadcasted_iota(jnp.int32, (8, LANES), 0) // LAT
        total = jnp.zeros((8, LANES), jnp.float32)
        for image in range(self.images):
            total = jnp.where(row == image, values[image], total)
        return total

    def share(self, image, halves):
        side = self.r.sides[image] // halves
        return (GROUPS / C) / jnp.full((1, LANES), side * side, jnp.int32).astype(jnp.float32)

    def prepare(self):
        r = self.r
        images = range(self.images)
        lane = lax.broadcasted_iota(jnp.int32, (8, LANES), 1)
        row = lax.broadcasted_iota(jnp.int32, (8, LANES), 0)
        hot = [(lane[0:1] == r.timesteps[k] * NBANDS // steps_total).astype(jnp.float32) for k in images]
        r.hot8[...] = self.by_row(hot)
        counts = jnp.zeros((1, LANES), jnp.float32)
        for k in images:
            side = r.sides[k]
            counts = counts + hot[k] * jnp.full((1, LANES), LAT * side * side, jnp.int32).astype(jnp.float32)
        r.counts[0] = jnp.where(row == 0, counts, 0.0)
        times = [jnp.full((1, LANES), r.timesteps[k], jnp.int32).astype(jnp.float32) for k in images]
        angle = (0.5 * math.pi / steps_total) * (self.by_row(times) + 0.5)
        cosine, sine = turn(angle)
        r.signal8[...] = cosine
        r.level8[...] = sine
        labels = jnp.zeros((8, LANES), jnp.float32)
        for k in images:
            label = jnp.full((8, LANES), r.labels[k], jnp.int32).astype(jnp.float32)
            labels = jnp.where(row == self.images + k, label, labels)
        r.labels8[...] = labels
        r.context[...] = jnp.zeros((8, LANES), jnp.float32)
        for k in images:
            chosen = r.class_table[pl.ds(r.labels[k], 1), :]
            r.context[k : k + 1] = chosen.astype(jnp.bfloat16).astype(jnp.float32)
        halves = r.embedded.shape[0]
        width = TE * halves
        place = lax.broadcasted_iota(jnp.int32, (8, width), 1)
        channel = place // halves
        half = TE // 2
        frequency = jnp.exp((-math.log(10000.0) / half) * lax.rem(channel, half).astype(jnp.float32))
        row = lax.broadcasted_iota(jnp.int32, (8, width), 0)
        time = jnp.zeros((8, width), jnp.float32)
        for k in images:
            time = jnp.where(row == k, jnp.full((8, width), r.timesteps[k], jnp.int32).astype(jnp.float32), time)
        cosine, sine = turn(time * frequency)
        values = jnp.where(channel < half, cosine, sine)
        for h in range(halves):
            r.embedded[h] = jnp.where((row < self.images) & (lax.rem(place, halves) == h), values, 0.0).astype(jnp.bfloat16)
        r.first_f[...] = jnp.zeros(r.first_f.shape, jnp.float32)
        r.last_f[...] = jnp.zeros(r.last_f.shape, jnp.float32)
        for image in images:
            for tap in range(9):
                low = 8 * tap + LAT * image
                r.first_f[image, low : low + LAT] = r.conv_first[tap]
                r.last_f[image, low : low + LAT] = r.conv_last[tap]
            r.first_w[image] = r.first_f[image].astype(jnp.bfloat16)
            r.last_w[image] = r.last_f[image].astype(jnp.bfloat16)

    def setup(self):
        r = self.r
        lane = lax.broadcasted_iota(jnp.int32, (LANES, LANES), 1) // (C // GROUPS)
        row = lax.broadcasted_iota(jnp.int32, (LANES, LANES), 0) // (C // GROUPS)
        r.group_spread[...] = (lane == row).astype(jnp.bfloat16)
        r.norms_all[self.me] = r.norms[...]
        self.spread(X_NORMS, 0, r.norms_all, self.whole_slot)
        r.context_all[self.me] = r.context[...]
        self.spread(X_CONTEXT, 0, r.context_all, self.whole_slot)
        for image in range(self.images):
            side = r.sides[image]
            pixel = lax.broadcasted_iota(jnp.int32, (PIXELS, LANES), 0)
            r.full_mask[image] = ((pixel // SIDE < side) & (lax.rem(pixel, SIDE) < side)).astype(jnp.float32)
            half = side // 2
            token = lax.broadcasted_iota(jnp.int32, (TOKENS, LANES), 0)
            r.half_mask[image] = ((token // MID < half) & (lax.rem(token, MID) < half)).astype(jnp.float32)
        for image in range(self.images):
            for channel in range(LAT):
                low = LAT * image + channel
                r.latent8[low : low + 1] = r.latent[channel, image : image + 1]
                r.noise8[low : low + 1] = r.noise[channel, image : image + 1]
        rest = LAT * self.images
        r.latent8[rest:] = jnp.zeros((8 - rest, PIXELS), jnp.float32)
        r.noise8[rest:] = jnp.zeros((8 - rest, PIXELS), jnp.float32)
        lane_row = lax.broadcasted_iota(jnp.int32, (8, PIXELS), 0)
        pixel = lax.broadcasted_iota(jnp.int32, (8, PIXELS), 1)
        side = jnp.zeros((8, PIXELS), jnp.int32)
        for image in range(self.images):
            side = jnp.where(lane_row // LAT == image, r.sides[image], side)
        r.lane_mask[...] = ((pixel // SIDE < side) & (lax.rem(pixel, SIDE) < side)).astype(jnp.float32)
        signal, level = r.signal8[:, 0:1], r.level8[:, 0:1]
        noisy = (signal * r.latent8[...] + level * r.noise8[...]) * r.lane_mask[...]
        noisy = noisy.astype(jnp.bfloat16).astype(jnp.float32)
        for tap in range(9):
            r.taps[8 * tap : 8 * tap + 8] = self.tap_lanes(noisy, tap)

    def entry(self, image):
        r = self.r
        first = dot_tn(r.taps[...].astype(jnp.bfloat16), r.first_w[image]) * r.full_mask[image]
        r.first[image] = first
        paired = r.first[image, pl.ds(0, PIXELS // 2, stride=2)] + r.first[image, pl.ds(1, PIXELS // 2, stride=2)]
        pooled = jnp.sum(paired.reshape(MID, 2, MID, LANES), axis=1).reshape(TOKENS, LANES) * 0.25
        r.pooled[image] = pooled
        mask = r.half_mask[image]
        centre, inv_std = norm_stats(pooled, mask, self.share(image, 2), r.group_spread[...])
        values = (pooled - centre) * inv_std * self.gain(0) + self.bias(0)
        r.x_res[self.image_rows(image), self.mine()] = (values * sigmoid(values) * mask).astype(jnp.bfloat16)
        self.two_step(X_RES, image, r.x_res, self.columns(image))

    def time_in(self):
        r = self.r
        table = self.weight(TIN)
        hidden = jnp.concatenate([dot_nn(r.embedded[h], table) for h in range(r.embedded.shape[0])], axis=1)
        r.hidden_time[...] = hidden
        r.time_act[self.me] = (hidden * sigmoid(hidden)).astype(jnp.bfloat16).astype(jnp.float32)
        self.spread(X_TIME, 0, r.time_act, self.whole_slot)

    def time_out(self):
        r = self.r
        self.spread_wait(X_TIME, 0, r.time_act, self.whole_slot)
        table = self.weight_rows(TOUT, 2)
        width = r.time_act.shape[2]
        total = 0.0
        for m in range(self.mp_size):
            total = total + dot_nn(r.time_act[m].astype(jnp.bfloat16), table[m * width : (m + 1) * width])
        r.time_vec[...] = total

    def res_wait(self, image):
        self.two_step_wait(X_RES, image, self.r.x_res, self.columns(image))

    def convolve(self, image, i):
        r = self.r
        values = r.x_res[self.image_rows(image), :]
        for j in range(3):
            moved = shift_rows(dot_nn(values, self.weight(CONV, 3 * i + j)), i - 1)
            if i > 0:
                moved = r.conv_sum[image, j] + moved
            r.conv_sum[image, j] = moved

    def convolved(self, image):
        r = self.r
        column = lax.rem(lax.broadcasted_iota(jnp.int32, (TOKENS, LANES), 0), MID)
        total = r.conv_sum[image, 1]
        total = total + jnp.where(column > 0, pltpu.roll(r.conv_sum[image, 0], 1, 0), 0.0)
        total = total + jnp.where(column < MID - 1, pltpu.roll(r.conv_sum[image, 2], TOKENS - 1, 0), 0.0)
        mask = r.half_mask[image]
        after = r.pooled[image] + (total + r.time_vec[image : image + 1]) * mask
        r.after_res[image] = after
        centre, inv_std = norm_stats(after, mask, self.share(image, 2), r.group_spread[...])
        values = (after - centre) * inv_std * self.gain(1) + self.bias(1)
        r.x_norm[self.image_rows(image), self.mine()] = (values * mask).astype(jnp.bfloat16)
        self.two_step(X_NORM, image, r.x_norm, self.columns(image))

    def share_square(self, name, ref):
        ref[self.me] = self.r.full[:, STARTS[name]]
        self.two_step(name, 0, ref, self.whole_slot)

    def share_square_wait(self, name, ref):
        self.two_step_wait(name, 0, ref, self.whole_slot)

    def hidden_rows(self, ref, m, count):
        share = self.dp_size // self.mp_size
        return ref.at[pl.ds(m * share, count * share), pl.ds(STARTS[FFOUT], 4)]

    def share_ffout(self):
        r = self.r
        share = self.dp_size // self.mp_size
        low = STARTS[FFOUT]
        r.w_ffout[self.me] = r.full[pl.ds(self.me * share, share), low : low + 4]
        self.deal(
            X_FFOUT_W, 0, lambda m: self.hidden_rows(r.full, m, 1), lambda m, count: r.w_ffout.at[m] if count == 1 else r.w_ffout.at[pl.ds(m, count)]
        )

    def share_ffout_wait(self):
        self.deal_wait(X_FFOUT_W, 0, lambda m, count: self.r.w_ffout.at[pl.ds(m, count)])

    def cross_first(self):
        r = self.r
        self.spread_wait(X_CONTEXT, 0, r.context_all, self.whole_slot)
        table = self.weight(SQ2)
        total = 0.0
        for m in range(self.mp_size):
            total = total + dot_nn(r.context_all[m].astype(jnp.bfloat16), table[m * LANES : (m + 1) * LANES])
        r.cross_val[self.me] = total.astype(jnp.bfloat16).astype(jnp.float32)
        self.spread(X_CROSS_VAL, 0, r.cross_val, self.whole_slot)

    def cross_second(self):
        r = self.r
        self.spread_wait(X_CROSS_VAL, 0, r.cross_val, self.whole_slot)
        table = self.weight(SQ3)
        total = 0.0
        for m in range(self.mp_size):
            total = total + dot_nn(r.cross_val[m].astype(jnp.bfloat16), table[m * LANES : (m + 1) * LANES])
        r.cross_out[self.me] = total
        self.spread(X_CROSS_OUT, 0, r.cross_out, self.whole_slot)

    def cross_last(self):
        self.spread_wait(X_CROSS_OUT, 0, self.r.cross_out, self.whole_slot)

    def attention(self, image):
        r = self.r
        self.two_step_wait(X_NORM, image, r.x_norm, self.columns(image))
        values = r.x_norm[self.image_rows(image), :]
        for m in range(self.mp_size):
            r.stream_in[image, :, m * LANES : (m + 1) * LANES] = dot_nn(values, self.wide(r.w_in, m))
        attn_in = token_norm(r.stream_in[image], self.full_lane(2, 0), self.full_lane(2, 1))[0].astype(jnp.bfloat16)
        r.attn_in[self.image_rows(image), :] = attn_in
        for j in range(3):
            r.qkv[j, self.image_rows(image)] = dot_nn(attn_in, self.weight(QKV, j)).astype(jnp.bfloat16)
        keep = self.across_lanes(image)
        lane_head = lax.broadcasted_iota(jnp.int32, (TOKENS, LANES), 1) // HD
        queries, keys, vals = (r.qkv[j, self.image_rows(image)] for j in range(3))
        zero = jnp.zeros((), jnp.bfloat16)
        attended = jnp.zeros((TOKENS, LANES), jnp.float32)
        for head in range(LANES // HD):
            own = lane_head == head
            scores = dot_nt(jnp.where(own, queries, zero), keys) * score_scale
            scores = jnp.where(keep, scores, masked_score)
            peak = jnp.max(scores, axis=-1, keepdims=True)
            expo = jnp.exp(scores - peak)
            probs = expo / jnp.sum(expo, axis=-1, keepdims=True)
            r.probs[image, head] = probs
            attended = jnp.where(own, dot_nn(probs.astype(jnp.bfloat16), vals), attended)
        r.x_attn[self.image_rows(image), self.mine()] = attended.astype(jnp.bfloat16)
        self.two_step(X_ATTN, image, r.x_attn, self.columns(image))

    def feed(self, image):
        r = self.r
        self.two_step_wait(X_ATTN, image, r.x_attn, self.columns(image))
        values = r.x_attn[self.image_rows(image), :]
        for m in range(self.mp_size):
            cut = slice(m * LANES, (m + 1) * LANES)
            r.stream_cross[image, :, cut] = (
                r.stream_in[image, :, cut] + dot_nn(values, self.wide(r.w_attn, m)) + r.cross_out[m, image : image + 1]
            )
        ff_in = token_norm(r.stream_cross[image], self.full_lane(3, 0), self.full_lane(3, 1))[0].astype(jnp.bfloat16)
        r.ff_in[self.image_rows(image), :] = ff_in

    def feed_part(self, image, k):
        r = self.r
        ff_in = r.ff_in[self.image_rows(image), :]
        cut = slice(k * LANES, (k + 1) * LANES)
        value = dot_nn(ff_in, self.weight(FFIN, 2 * k))
        gate = dot_nn(ff_in, self.weight(FFIN, 2 * k + 1))
        r.ff_value[image, :, cut] = value
        r.ff_gate[image, :, cut] = gate
        half = 0.5 * (1.0 + erf(gate * math.sqrt(0.5)))
        r.ff_hidden[self.image_rows(image), cut] = (value * (gate * half)).astype(jnp.bfloat16)

    def feed_out(self, image):
        r = self.r
        hidden = r.ff_hidden[self.image_rows(image), :]
        total = jnp.concatenate([dot_nn(hidden, self.wide_hidden(m)) for m in range(self.mp_size)], axis=1)
        self.deal_sum(X_FF, image, self.by_token(total), r.ff_send, r.ff_land, r.ff_total)

    def by_token(self, values):
        share = TOKENS // self.mp_size
        return [values[m * share : (m + 1) * share] for m in range(self.mp_size)]

    def wide_hidden(self, m):
        return self.flat(self.r.w_ffout[m])

    def deal_sum(self, name, image, parts, send, land, total):
        index = self.index_of(name, image)
        pair, beyond = (self.place.dp, self.pair()), (self.place.dp, self.beyond())
        sems = (self.r.ex_send.at[index], self.r.ex_recv.at[index], self.r.ex_far.at[index])
        for m in range(self.mp_size):
            send[image, m % 2, m // 2] = parts[m].astype(send.dtype)
        core, far = lax.rem(self.me, 2), self.me // 2
        near = remote(send.at[image, 1 - core], land.at[image, pl.ds(0, 2)], sems[0], sems[1], pair)
        near.start()
        away = remote(send.at[image, 2, 0], land.at[image, 2], sems[0], sems[2], beyond)
        self.pending.append(remote(land.at[image], land.at[image], sems[0], sems[1], pair))

        def relay():
            near.wait_recv()
            send[image, 2, 0] = (
                send[image, core, 1 - far].astype(jnp.float32) + land[image, 1 - far].astype(jnp.float32)
            ).astype(send.dtype)
            away.start()
            total[image] = send[image, core, far].astype(jnp.float32) + land[image, far].astype(jnp.float32)

        self.relays[(name, image)] = relay

    def deal_total(self, name, image, land, total):
        index = self.index_of(name, image)
        region = land.at[image, 2]
        remote(region, region, self.r.ex_send.at[index], self.r.ex_far.at[index], self.peer(1)).wait_recv()
        return total[image] + land[image, 2].astype(jnp.float32)

    def leave(self, image):
        r = self.r
        total = self.deal_total(X_FF, image, r.ff_land, r.ff_total)
        stream = (r.stream_cross[image, self.my_tokens(), :] + total).astype(jnp.bfloat16)
        self.token_rows(image)(r.x_last, self.me, 1)[...] = stream
        self.two_step(X_LAST, image, r.x_last, self.token_rows(image))

    def upsample(self, ref, image, values):
        twice = jnp.broadcast_to(values.reshape(MID, 1, MID, LANES), (MID, 2, MID, LANES)).reshape(PIXELS // 2, LANES)
        ref[image, pl.ds(0, PIXELS // 2, stride=2)] = twice
        ref[image, pl.ds(1, PIXELS // 2, stride=2)] = twice

    def finish(self, image):
        r = self.r
        self.two_step_wait(X_LAST, image, r.x_last, self.token_rows(image))
        values = r.x_last[self.image_rows(image), :]
        after = r.after_res[image] + dot_nn(values, self.weight(SQ4)) * r.half_mask[image]
        self.upsample(r.merged, image, after)
        merged = r.merged[image] + r.first[image]
        r.merged[image] = merged
        mask = r.full_mask[image]
        centre, inv_std = norm_stats(merged, mask, self.share(image, 1), r.group_spread[...])
        r.final_stats[image, 0:1] = centre
        r.final_stats[image, 1:2] = inv_std
        values = (merged - centre) * inv_std * self.gain(4) + self.bias(4)
        last_in = (values * sigmoid(values) * mask).astype(jnp.bfloat16)
        r.last_in[image] = last_in
        part = dot_nt(r.last_w[image], last_in)
        if image == 0:
            r.out_taps[...] = part
        else:
            r.out_taps[...] += part

    def predict(self):
        r = self.r
        total = 0.0
        for tap in range(9):
            total = total + self.tap_lanes(r.out_taps[8 * tap : 8 * tap + 8], tap)
        r.predicted[self.me] = total
        self.spread(X_PREDICTED, 0, r.predicted, self.whole_slot)

    def loss(self):
        r = self.r
        self.spread_wait(X_PREDICTED, 0, r.predicted, self.whole_slot)
        predicted = jnp.sum(r.predicted[...], axis=0)
        signal, level = r.signal8[:, 0:1], r.level8[:, 0:1]
        error = (predicted - (signal * r.noise8[...] - level * r.latent8[...])) * r.lane_mask[...]
        per_row = jnp.sum(error * error, axis=1, keepdims=True)
        r.small[88:96] = jnp.broadcast_to(column_sum(per_row * r.hot8[...]), (8, LANES))
        counts = jnp.sum(r.counts_all[...].reshape(-1, 8, LANES), axis=0)[0:1]
        weight = jnp.sum(r.hot8[...] * ((1.0 / NBANDS) / (counts + 1.0)), axis=1, keepdims=True)
        grads = (2.0 * error * weight).astype(jnp.bfloat16).astype(jnp.float32)
        for tap in range(9):
            r.out_taps[8 * tap : 8 * tap + 8] = self.tap_lanes(grads, 8 - tap)

    def pool_sum(self, ref, image):
        paired = ref[image, pl.ds(0, PIXELS // 2, stride=2)] + ref[image, pl.ds(1, PIXELS // 2, stride=2)]
        return jnp.sum(paired.reshape(MID, 2, MID, LANES), axis=1).reshape(TOKENS, LANES)

    def add_small(self, row, image, values, more=False):
        if image == 0 and not more:
            self.r.small[row : row + values.shape[0]] = values
        else:
            self.r.small[row : row + values.shape[0]] += values

    def tap_rows(self, values, image, low):
        row = lax.rem(lax.broadcasted_iota(jnp.int32, values.shape, 0), 8)
        kept = jnp.where(row // LAT == image, values, 0.0)
        shift = (low - LAT * image) % values.shape[0]
        return pltpu.roll(kept, shift, 0) if shift else kept

    def back_last(self, image):
        r = self.r
        grads_taps = r.out_taps[...].astype(jnp.bfloat16)
        mask = r.full_mask[image]
        grads = dot_tn(grads_taps, r.last_w[image]) * mask
        self.add_small(0, image, self.tap_rows(dot_nn(grads_taps, r.last_in[image]), image, LAT))
        inv_std = r.final_stats[image, 1:2]
        normal = (r.merged[image] - r.final_stats[image, 0:1]) * inv_std
        values = normal * self.gain(4) + self.bias(4)
        gate = sigmoid(values)
        grads = grads * (gate * (1.0 + values * (1.0 - gate)))
        grads, gain_grad, bias_grad = norm_backward(
            grads, normal, inv_std, mask, self.gain(4), self.share(image, 1), r.group_spread[...]
        )
        self.add_small(72 + 8, image, gain_grad)
        self.add_small(72 + 9, image, bias_grad)
        r.merged[image] = grads
        after = self.pool_sum(r.merged, image)
        r.grad_after[image] = after
        r.g_proj[self.image_rows(image), self.mine()] = (after * r.half_mask[image]).astype(jnp.bfloat16)
        self.two_step(X_G_PROJ, image, r.g_proj, self.columns(image))

    def back_feed(self, image):
        r = self.r
        self.two_step_wait(X_G_PROJ, image, r.g_proj, self.columns(image))
        total = 0.0
        for m in range(self.mp_size):
            total = total + dot_nt(r.g_proj[self.image_rows(image), m * LANES : (m + 1) * LANES], self.wide(r.w_out, m))
        r.grad_stream[image] = total
        grads_low = total.astype(jnp.bfloat16)
        r.g_ffout[self.image_rows(image), :] = grads_low
        hidden = 0.0
        for m in range(self.mp_size):
            hidden = hidden + dot_nt(grads_low[:, m * LANES : (m + 1) * LANES], self.wide_hidden(m))
        r.g_hidden[...] = hidden
        for k in range(4):
            cut = slice(k * LANES, (k + 1) * LANES)
            value, gate, grads = r.ff_value[image, :, cut], r.ff_gate[image, :, cut], r.g_hidden[:, cut]
            half = 0.5 * (1.0 + erf(gate * math.sqrt(0.5)))
            slope = half + gate * (jnp.exp(-0.5 * gate * gate) * (1.0 / math.sqrt(2.0 * math.pi)))
            r.g_ffin[2 * k, self.image_rows(image)] = (grads * (gate * half)).astype(jnp.bfloat16)
            r.g_ffin[2 * k + 1, self.image_rows(image)] = (grads * value * slope).astype(jnp.bfloat16)
        total = 0.0
        for k in range(8):
            total = total + dot_nt(r.g_ffin[k, self.image_rows(image)], self.weight(FFIN, k))
        self.deal_sum(X_G_FF, image, self.by_token(total), r.gff_send, r.gff_land, r.gff_total)

    def token_back(self, name, image, land, total, stream, norm, row):
        r = self.r
        grads = self.deal_total(name, image, land, total)
        values = stream[image, self.my_tokens(), :]
        gain = self.full_lane(norm, 0)
        _, normal, inv_std = token_norm(values, gain, 0.0)
        grads, gain_grad, bias_grad = token_norm_backward(grads, normal, inv_std, gain)
        for which, values in ((0, gain_grad), (1, bias_grad)):
            for m in range(self.mp_size):
                place = r.norm_send.at[m, row + which : row + which + 1]
                cut = values[:, m * LANES : (m + 1) * LANES]
                place[...] = cut if image == 0 else place[...] + cut
        total = r.grad_stream[image, self.my_tokens(), :] + grads
        r.grad_stream[image, self.my_tokens(), :] = total
        return total

    def back_cross(self, image):
        r = self.r
        total = self.token_back(X_G_FF, image, r.gff_land, r.gff_total, r.stream_cross, 3, 2)
        r.gc_part[self.me, image : image + 1] = column_sum(total)
        self.token_rows(image)(r.g_attn, self.me, 1)[...] = total.astype(jnp.bfloat16)
        self.two_step(X_G_ATTN, image, r.g_attn, self.token_rows(image))

    def cross_one(self):
        r = self.r
        r.gc_part[self.me, self.images :] = jnp.zeros((8 - self.images, C), jnp.float32)
        self.spread(X_GC, 0, r.gc_part, self.whole_slot)

    def cross_two(self):
        r = self.r
        self.spread_wait(X_GC, 0, r.gc_part, self.whole_slot)
        r.gc_full[...] = jnp.sum(r.gc_part[...], axis=0)
        mine = r.gc_full[:, self.mine()].astype(jnp.bfloat16)
        for m in range(self.mp_size):
            r.dw[m * LANES : (m + 1) * LANES] = dot_tn(r.cross_val[m].astype(jnp.bfloat16), mine)
        self.emit(SQ3, r.dw[...])
        r.gv_part[self.me] = dot_nt(mine, self.weight(SQ3))
        self.spread(X_GV, 0, r.gv_part, self.whole_slot)

    def cross_three(self):
        r = self.r
        self.spread_wait(X_GV, 0, r.gv_part, self.whole_slot)
        r.gc_full[...] = jnp.sum(r.gv_part[...], axis=0)
        mine = r.gc_full[:, self.mine()].astype(jnp.bfloat16)
        for m in range(self.mp_size):
            r.dw[m * LANES : (m + 1) * LANES] = dot_tn(r.context_all[m].astype(jnp.bfloat16), mine)
        self.emit(SQ2, r.dw[...])
        r.gx_part[self.me] = dot_nt(mine, self.weight(SQ2))
        self.spread(X_GX, 0, r.gx_part, self.whole_slot)

    def cross_four(self):
        r = self.r
        self.spread_wait(X_GX, 0, r.gx_part, self.whole_slot)
        r.gc_full[...] = jnp.sum(r.gx_part[...], axis=0)
        row = lax.broadcasted_iota(jnp.int32, (8, LANES), 0)
        r.table_rows[0] = jnp.where(row < self.images, r.gc_full[:, self.mine()], r.labels8[...])

    def back_attention(self, image):
        r = self.r
        self.two_step_wait(X_G_ATTN, image, r.g_attn, self.token_rows(image))
        total = 0.0
        for m in range(self.mp_size):
            total = total + dot_nt(r.g_attn[self.image_rows(image), m * LANES : (m + 1) * LANES], self.wide_mine(r.w_attn, m))
        grads = total.astype(jnp.bfloat16)
        queries, keys, vals = (r.qkv[j, self.image_rows(image)] for j in range(3))
        lane_head = lax.broadcasted_iota(jnp.int32, (TOKENS, LANES), 1) // HD
        zero = jnp.zeros((), jnp.bfloat16)
        results = [jnp.zeros((TOKENS, LANES), jnp.float32) for _ in range(3)]
        for head in range(LANES // HD):
            own = lane_head == head
            probs = r.probs[image, head]
            results[2] = jnp.where(own, dot_tn(probs.astype(jnp.bfloat16), grads), results[2])
            grad_probs = dot_nt(jnp.where(own, grads, zero), vals)
            grad_scores = (probs * (grad_probs - jnp.sum(probs * grad_probs, axis=-1, keepdims=True))).astype(jnp.bfloat16)
            results[0] = jnp.where(own, dot_nn(grad_scores, keys) * score_scale, results[0])
            results[1] = jnp.where(own, dot_tn(grad_scores, queries) * score_scale, results[1])
        total = 0.0
        for j in range(3):
            low = results[j].astype(jnp.bfloat16)
            r.g_qkv[j, self.image_rows(image)] = low
            total = total + dot_nt(low, self.weight(QKV, j))
        self.deal_sum(X_G_AT, image, self.by_token(total), r.gat_send, r.gat_land, r.gat_total)

    def back_in(self, image):
        r = self.r
        total = self.token_back(X_G_AT, image, r.gat_land, r.gat_total, r.stream_in, 2, 0)
        self.token_rows(image)(r.g_in, self.me, 1)[...] = total.astype(jnp.bfloat16)
        self.two_step(X_G_IN, image, r.g_in, self.token_rows(image))

    def back_conv(self, image):
        r = self.r
        self.two_step_wait(X_G_IN, image, r.g_in, self.token_rows(image))
        mask = r.half_mask[image]
        grads = 0.0
        for m in range(self.mp_size):
            grads = grads + dot_nt(r.g_in[self.image_rows(image), m * LANES : (m + 1) * LANES], self.wide_mine(r.w_in, m))
        after = r.after_res[image]
        centre, inv_std = norm_stats(after, mask, self.share(image, 2), r.group_spread[...])
        normal = (after - centre) * inv_std
        grads, gain_grad, bias_grad = norm_backward(
            grads * mask, normal, inv_std, mask, self.gain(1), self.share(image, 2), r.group_spread[...]
        )
        self.add_small(72 + 2, image, gain_grad)
        self.add_small(72 + 3, image, bias_grad)
        grads = r.grad_after[image] + grads
        r.grad_after[image] = grads
        masked = grads * mask
        r.grad_time[image : image + 1] = column_sum(masked).astype(jnp.bfloat16).astype(jnp.float32)
        low = masked.astype(jnp.bfloat16).astype(jnp.float32)
        column = lax.rem(lax.broadcasted_iota(jnp.int32, (TOKENS, LANES), 0), MID)
        total = 0.0
        for tap in range(9):
            i, j = divmod(tap, 3)
            moved = shift_rows(low, 1 - i)
            if j == 0:
                moved = jnp.where(column < MID - 1, pltpu.roll(moved, TOKENS - 1, 0), 0.0)
            elif j == 2:
                moved = jnp.where(column > 0, pltpu.roll(moved, 1, 0), 0.0)
            moved = moved.astype(jnp.bfloat16)
            r.g_taps[self.image_rows(image), tap * LANES : (tap + 1) * LANES] = moved
            total = total + dot_nt(moved, self.weight(CONV, tap))
        parts = [total[:, m * LANES : (m + 1) * LANES] for m in range(self.mp_size)]
        self.deal_sum(X_G_RES, image, parts, r.gres_send, r.gres_land, r.gres_total)

    def back_first(self, image):
        r = self.r
        grads = self.deal_total(X_G_RES, image, r.gres_land, r.gres_total)
        mask = r.half_mask[image]
        pooled = r.pooled[image]
        centre, inv_std = norm_stats(pooled, mask, self.share(image, 2), r.group_spread[...])
        normal = (pooled - centre) * inv_std
        values = normal * self.gain(0) + self.bias(0)
        gate = sigmoid(values)
        grads = grads * mask * (gate * (1.0 + values * (1.0 - gate)))
        grads, gain_grad, bias_grad = norm_backward(
            grads, normal, inv_std, mask, self.gain(0), self.share(image, 2), r.group_spread[...]
        )
        self.add_small(72, image, gain_grad)
        self.add_small(72 + 1, image, bias_grad)
        self.upsample(r.first, image, 0.25 * (r.grad_after[image] + grads))
        low = ((r.merged[image] + r.first[image]) * r.full_mask[image]).astype(jnp.bfloat16)
        self.add_small(0, image, self.tap_rows(dot_nn(r.taps[...].astype(jnp.bfloat16), low), image, 0), True)

    def back_time(self):
        r = self.r
        r.grad_time[self.images :] = jnp.zeros((8 - self.images, LANES), jnp.float32)
        grads = r.grad_time[...].astype(jnp.bfloat16)
        width = r.time_act.shape[2]
        for m in range(self.mp_size):
            r.dw_time[m * width : (m + 1) * width] = dot_tn(r.time_act[m].astype(jnp.bfloat16), grads)
        self.emit_rows(TOUT, r.dw_time[...], 2)
        total = dot_nt(grads, self.weight_rows(TOUT, 2))
        for m in range(self.mp_size):
            r.gt_send[m] = total[:, m * width : (m + 1) * width]
        r.gt_land[self.me] = r.gt_send[self.me]
        self.deal(X_GT, 0, lambda m: r.gt_send.at[pl.ds(m, 1)], lambda m, count: r.gt_land.at[pl.ds(m, count)])
        r.norm_land[self.me] = r.norm_send[self.me]
        self.deal(X_NORM_SUMS, 0, lambda m: r.norm_send.at[pl.ds(m, 1)], lambda m, count: r.norm_land.at[pl.ds(m, count)])

    def back_time_in(self):
        r = self.r
        self.deal_wait(X_GT, 0, lambda m, count: r.gt_land.at[pl.ds(m, count)])
        grads = jnp.sum(r.gt_land[...], axis=0)
        hidden = r.hidden_time[...]
        gate = sigmoid(hidden)
        grads = (grads * (gate * (1.0 + hidden * (1.0 - gate)))).astype(jnp.bfloat16)
        total = 0.0
        for h in range(r.embedded.shape[0]):
            total = total + dot_tn(r.embedded[h], grads[:, h * LANES : (h + 1) * LANES])
        self.emit(TIN, total)
        self.deal_wait(X_NORM_SUMS, 0, lambda m, count: r.norm_land.at[pl.ds(m, count)])
        r.small[72 + 4 : 72 + 8] = jnp.sum(r.norm_land[...], axis=0)[0:4]
        r.small[72 + 10 : 88] = jnp.zeros((6, LANES), jnp.float32)

    def grads_out(self):
        r = self.r
        self.emit(SQ4, dot_tn(r.x_last[...], r.g_proj[:, self.mine()]))

    def grads_ffout(self):
        r = self.r
        share = self.dp_size // self.mp_size
        for m in range(self.mp_size):
            part = dot_tn(r.ff_hidden[...], r.g_ffout[:, m * LANES : (m + 1) * LANES])
            r.dw_ffout[m] = part.reshape(share, 4, self.rows, LANES).astype(jnp.bfloat16)
        low = STARTS[FFOUT]
        r.partials[pl.ds(self.me * share, share), low : low + 4] = r.dw_ffout[self.me]
        self.deal(X_DW_FFOUT, 0, lambda m: r.dw_ffout.at[m], lambda m, count: self.hidden_rows(r.partials, m, count))

    def grads_ffout_wait(self):
        self.deal_wait(X_DW_FFOUT, 0, lambda m, count: self.hidden_rows(self.r.partials, m, count))

    def grads_ffin(self):
        for k in range(8):
            self.emit(FFIN, dot_tn(self.r.ff_in[...], self.r.g_ffin[k]), k)

    def grads_attn(self):
        r = self.r
        self.emit(SQ1, dot_tn(r.x_attn[...], r.g_attn[:, self.mine()]))

    def grads_qkv(self):
        for j in range(3):
            self.emit(QKV, dot_tn(self.r.attn_in[...], self.r.g_qkv[j]), j)

    def grads_in(self):
        r = self.r
        self.emit(SQ0, dot_tn(r.x_norm[...], r.g_in[:, self.mine()]))

    def grads_conv(self, i):
        r = self.r
        for tap in range(3 * i, 3 * i + 3):
            self.emit(CONV, dot_tn(r.x_res[...], r.g_taps[:, tap * LANES : (tap + 1) * LANES]), tap)


SMALL_ROWS = 96
EXCHANGES = 40


def model_scratch(images, dp_size, mp_size, rows, time_local, hidden_local):
    bf16, f32 = jnp.bfloat16, jnp.float32
    tokens = images * TOKENS
    share = TOKENS // mp_size
    wide = lambda kind: pltpu.VMEM((tokens, C), kind)
    per_image = lambda width, kind=f32: pltpu.VMEM((images, TOKENS, width), kind)
    send = lambda: pltpu.VMEM((images, 3, 2, share, C), LINK)
    land = lambda: pltpu.VMEM((images, 3, share, C), LINK)
    own = lambda: pltpu.VMEM((images, share, C), f32)
    tiny = lambda width: pltpu.VMEM((mp_size, 8, width), f32)
    square = lambda: pltpu.VMEM((mp_size, dp_size, rows, LANES), bf16)
    dma = pltpu.SemaphoreType.DMA((EXCHANGES,))
    return dict(
        ex_send=dma, ex_recv=dma, ex_far=dma,
        group_spread=pltpu.VMEM((LANES, LANES), bf16),
        norms_all=pltpu.VMEM((mp_size, 5, 2, LANES), f32),
        context_all=tiny(LANES), time_act=tiny(time_local), cross_val=tiny(LANES), cross_out=tiny(LANES),
        full_mask=pltpu.VMEM((images, PIXELS, LANES), f32), half_mask=per_image(LANES),
        latent8=pltpu.VMEM((8, PIXELS), f32), noise8=pltpu.VMEM((8, PIXELS), f32), lane_mask=pltpu.VMEM((8, PIXELS), f32),
        taps=pltpu.VMEM((72, PIXELS), f32), out_taps=pltpu.VMEM((72, PIXELS), f32),
        first=pltpu.VMEM((images, PIXELS, LANES), f32), merged=pltpu.VMEM((images, PIXELS, LANES), f32),
        last_in=pltpu.VMEM((images, PIXELS, LANES), bf16),
        pooled=per_image(LANES), after_res=per_image(LANES), grad_after=per_image(LANES),
        final_stats=pltpu.VMEM((images, 8, LANES), f32),
        hidden_time=pltpu.VMEM((8, time_local), f32), time_vec=pltpu.VMEM((8, LANES), f32), grad_time=pltpu.VMEM((8, LANES), f32),
        x_res=wide(bf16), x_norm=wide(bf16), x_attn=wide(bf16), x_last=wide(bf16),
        g_proj=wide(bf16), g_ffout=wide(bf16), g_attn=wide(bf16), g_in=wide(bf16),
        attn_in=wide(bf16), ff_in=wide(bf16), ff_hidden=pltpu.VMEM((tokens, hidden_local), bf16),
        stream_in=per_image(C), stream_cross=per_image(C), grad_stream=per_image(C),
        ff_value=per_image(hidden_local), ff_gate=per_image(hidden_local),
        g_hidden=pltpu.VMEM((TOKENS, hidden_local), f32), g_ffin=pltpu.VMEM((8, tokens, LANES), bf16),
        qkv=pltpu.VMEM((3, tokens, LANES), bf16), g_qkv=pltpu.VMEM((3, tokens, LANES), bf16),
        probs=pltpu.VMEM((images, LANES // HD, TOKENS, TOKENS), f32),
        w_in=square(), w_attn=square(), w_out=square(),
        w_ffout=pltpu.VMEM((mp_size, dp_size // mp_size, 4, rows, LANES), bf16),
        dw_ffout=pltpu.VMEM((mp_size, dp_size // mp_size, 4, rows, LANES), bf16),
        ff_send=send(), ff_land=land(), ff_total=own(), gff_send=send(), gff_land=land(), gff_total=own(),
        gat_send=send(), gat_land=land(), gat_total=own(),
        gres_send=pltpu.VMEM((images, 3, 2, TOKENS, LANES), LINK), gres_land=pltpu.VMEM((images, 3, TOKENS, LANES), LINK),
        gres_total=per_image(LANES),
        predicted=pltpu.VMEM((mp_size, 8, PIXELS), f32),
        norm_send=tiny(LANES), norm_land=tiny(LANES),
        gc_part=tiny(C), gv_part=tiny(C), gx_part=tiny(C), gc_full=pltpu.VMEM((8, C), f32),
        dw=pltpu.VMEM((C, LANES), f32), dw_time=pltpu.VMEM((mp_size * time_local, LANES), f32),
        gt_send=tiny(time_local), gt_land=tiny(time_local),
        conv_sum=pltpu.VMEM((images, 3, TOKENS, LANES), f32),
        hot8=pltpu.VMEM((8, LANES), f32), signal8=pltpu.VMEM((8, LANES), f32), level8=pltpu.VMEM((8, LANES), f32),
        labels8=pltpu.VMEM((8, LANES), f32), context=pltpu.VMEM((8, LANES), f32), counts=pltpu.VMEM((1, 8, LANES), f32),
        embedded=pltpu.VMEM((time_local // LANES, 8, TE * time_local // LANES), bf16),
        first_f=pltpu.VMEM((images, 72, LANES), f32), last_f=pltpu.VMEM((images, 72, LANES), f32),
        first_w=pltpu.VMEM((images, 72, LANES), bf16), last_w=pltpu.VMEM((images, 72, LANES), bf16),
        tin_rows=pltpu.VMEM((rows, LANES), f32), shard=pltpu.VMEM((SECTION_COUNT, rows, LANES), bf16),
        full=pltpu.VMEM((dp_size, SECTION_COUNT, rows, LANES), bf16), partials=pltpu.VMEM((dp_size, SECTION_COUNT, rows, LANES), bf16),
        small=pltpu.VMEM((SMALL_ROWS, LANES), f32), table_rows=pltpu.VMEM((1, 8, LANES), f32),
        g_taps=pltpu.VMEM((tokens, 9 * LANES), bf16),
    )


class Reducer:
    def __init__(self, place, refs, dp_size):
        self.place = place
        self.r = refs
        self.dp_size = dp_size
        r = refs
        self.scatter = Scatter(
            place, r.partials, r.total, r.near, r.sums, r.far, (r.sc_a, r.sc_b, r.sc_c, r.sc_d), SCATTER_PIECES
        )
        self.slots = r.gram_low.shape[0]
        self.gather = Gather(
            place, r.gram_low, r.grams, (r.ro_a, r.ro_b, r.ro_c, r.ro_d), tuple((s, 1) for s in range(self.slots))
        )
        self.table = Gather(place, r.table_rows, r.table_all, (r.ta_a, r.ta_b, r.ta_c, r.ta_d), ((0, 1),))
        self.started, self.pumped, self.finished, self.sent = 0, 0, 0, set()
        self.shared, self.passed, self.rooted = [], [], []

    def start(self, count):
        while self.started < count:
            self.scatter.start(self.started)
            self.started += 1

    def pump(self, count):
        while self.pumped < count:
            self.scatter.pump(self.pumped)
            self.pumped += 1

    def finish(self, count):
        while self.finished < count:
            self.scatter.finish(self.finished)
            low, sections = SCATTER_PIECES[self.finished]
            self.r.total_low[pl.ds(low, sections)] = self.r.total[pl.ds(low, sections)].astype(jnp.bfloat16)
            self.finished += 1
            done = {k for start, number in SCATTER_PIECES[: self.finished] for k in range(start, start + number)}
            for position, block in enumerate(ORDER):
                low, sections = BLOCKS[block]
                if position not in self.sent and all(k in done for k in range(low, low + sections)):
                    self.sent.add(position)
                    self.send_block(position)

    def owned_by(self, positions):
        owner = self.place.dp == positions[0] % self.dp_size
        for position in positions[1:]:
            owner = owner | (self.place.dp == position % self.dp_size)
        return owner

    def block_copy(self, position, other, source, count=1):
        r = self.r
        block = ORDER[position]
        slot = position // self.dp_size
        if block in BY_GRAM:
            out, land = r.gram_out.at[BY_GRAM.index(block)], r.gram_land
        else:
            out, land = r.total_low.at[BLOCKS[block][0]], r.rows_land
        land = land.at[slot, source] if count == 1 else land.at[slot, pl.ds(source, count)]
        return remote(
            out if count == 1 else land, land, r.bl_send.at[position], r.bl_recv.at[slot], (other, self.place.mp)
        )

    def send_block(self, position):
        r = self.r
        place = self.place
        block = ORDER[position]
        low, sections = BLOCKS[block]
        owner, slot = position % self.dp_size, position // self.dp_size
        if block in BY_GRAM:
            values = r.total[pl.ds(low, sections)].reshape(-1, LANES)
            r.gram_out[BY_GRAM.index(block)] = gram_of(values).astype(jnp.bfloat16)

        @pl.when(place.dp != owner)
        def _():
            self.block_copy(position, owner, place.dp).start()

        @pl.when(place.dp == owner)
        def _():
            if block in BY_GRAM:
                r.gram_land[slot, place.dp] = r.gram_out[BY_GRAM.index(block)]
            else:
                r.rows_land[slot, place.dp] = r.total_low[low]

    def gram(self, slot):
        r = self.r
        place = self.place
        positions = [p for p in range(len(ORDER)) if p // self.dp_size == slot]
        kinds = (
            [p for p in positions if ORDER[p] in BY_GRAM],
            [p for p in positions if ORDER[p] in TIN_BLOCKS],
            [p for p in positions if ORDER[p] not in BY_GRAM + TIN_BLOCKS],
        )
        for kind, members in enumerate(kinds):
            if not members:
                continue

            @pl.when(self.owned_by(members))
            def _(kind=kind, members=members):
                other = lax.rem(place.dp + 1, self.dp_size)
                self.block_copy(members[0], other, 0, self.dp_size - 1).wait_recv()
                if kind == 0:
                    r.gram_own[slot] = jnp.sum(r.gram_land[slot].astype(jnp.float32), axis=0)
                    return
                values = r.rows_land[slot]
                if values.shape[1] % 16 == 0 and kind == 2:
                    values = values.reshape(-1, LANES)
                else:
                    values = values.astype(jnp.float32).reshape(-1, LANES)
                    if kind == 1:
                        parity = lax.rem(lax.broadcasted_iota(jnp.int32, values.shape, 0), len(TIN_BLOCKS))
                        values = jnp.where(parity == place.dp - members[0] % self.dp_size, values, 0.0)
                    values = values.astype(jnp.bfloat16)
                r.gram_own[slot] = dot_tn(values, values)

    def share(self, slot):
        r = self.r
        self.gram(slot)
        r.gram_low[slot] = r.gram_own[slot].astype(jnp.bfloat16)
        self.gather.start(slot)
        r.grams[self.place.dp, slot] = r.gram_low[slot]

    def root(self, slot):
        r = self.r
        self.gather.ready(slot)
        positions = [p for p in range(len(ORDER)) if p // self.dp_size == slot]
        renewed = [
            shampoo_beta * r.stats[ORDER[p]] + r.grams[p % self.dp_size, slot].astype(jnp.float32) for p in positions
        ]
        for position, root in zip(positions, inverse_roots(renewed)):
            r.roots[ORDER[position]] = root

    def share_ready(self):
        for slot in range(self.slots):
            positions = [p for p in range(len(ORDER)) if p // self.dp_size == slot]
            if slot not in self.shared and all(p in self.sent for p in positions):
                self.shared.append(slot)
                self.share(slot)

    def pass_ready(self):
        for slot in self.shared:
            if slot not in self.passed:
                self.passed.append(slot)
                self.gather.pump(slot)

    def root_ready(self):
        for slot in self.passed:
            if slot not in self.rooted:
                self.rooted.append(slot)
                self.root(slot)

    def small_copy(self):
        r = self.r
        return remote(r.small, r.small_near, r.sm_send.at[0], r.sm_recv.at[0], self.place.partner())

    def far_copy(self, step, count=1):
        r = self.r
        return remote(
            r.small_far.at[pl.ds(0, count)], r.small_far.at[pl.ds(step, count)], r.sm_send.at[1], r.sm_recv.at[1], self.place.across(step)
        )

    def small_start(self):
        self.small_copy().start()
        self.table.start(0)
        self.r.table_all[self.place.dp] = self.r.table_rows[...]

    def small_pump(self):
        r = self.r
        self.small_copy().wait_recv()
        r.small_far[0] = r.small[...] + r.small_near[...]
        steps(1, self.place.outer_size, lambda step: self.far_copy(step).start())
        self.table.pump(0)

    def small_finish(self):
        r = self.r
        self.far_copy(1, self.place.outer_size - 1).wait_recv()
        r.small_sum[...] = jnp.sum(r.small_far[...], axis=0)
        self.table.ready(0)

    def drain(self):
        for piece in range(len(SCATTER_PIECES)):
            self.scatter.drain(piece)
        for slot in range(self.slots):
            self.gather.drain(slot)
        self.table.drain(0)
        self.small_copy().wait_send()
        self.far_copy(1, self.place.outer_size - 1).wait_send()
        for position in range(len(ORDER)):
            @pl.when(self.place.dp != position % self.dp_size)
            def _(position=position):
                self.block_copy(position, position % self.dp_size, self.place.dp).wait_send()


def reducer_scratch(dp_size, rows):
    bf16, f32 = jnp.bfloat16, jnp.float32
    outer = dp_size // 2
    slots = -(-len(ORDER) // dp_size)
    dma = pltpu.SemaphoreType.DMA
    held = lambda: pltpu.VMEM((outer, SECTION_COUNT, rows, LANES), bf16)
    scatter_sem = dma((len(SCATTER_PIECES),))
    gather_sem = dma((len(GATHER_PIECES),))
    root_sem = dma((slots,))
    one_sem = dma((1,))
    return dict(
        near=held(), sums=held(), far=held(),
        total_low=pltpu.VMEM((SECTION_COUNT, rows, LANES), bf16),
        gram_out=pltpu.VMEM((len(BY_GRAM), LANES, LANES), bf16),
        gram_land=pltpu.VMEM((slots, dp_size, LANES, LANES), bf16),
        rows_land=pltpu.VMEM((slots, dp_size, rows, LANES), bf16),
        gram_own=pltpu.VMEM((slots, LANES, LANES), f32),
        gram_low=pltpu.VMEM((slots, LANES, LANES), bf16),
        small_near=pltpu.VMEM((SMALL_ROWS, LANES), f32), small_far=pltpu.VMEM((outer, SMALL_ROWS, LANES), f32),
        sc_a=scatter_sem, sc_b=scatter_sem, sc_c=scatter_sem, sc_d=scatter_sem,
        ga_a=gather_sem, ga_b=gather_sem, ga_c=gather_sem, ga_d=gather_sem,
        ro_a=root_sem, ro_b=root_sem, ro_c=root_sem, ro_d=root_sem,
        ta_a=one_sem, ta_b=one_sem, ta_c=one_sem, ta_d=one_sem,
        co_a=one_sem, co_b=one_sem, co_c=one_sem, co_d=one_sem,
        sm_send=dma((2,)), sm_recv=dma((2,)),
        bl_send=dma((len(ORDER),)), bl_recv=dma((slots,)),
    )


class Refs:
    pass


def step_kernel(images, dp_size, mp_size, names, *refs):
    r = Refs()
    for name, ref in zip(names, refs):
        setattr(r, name, ref)
    place = Place(dp_size, mp_size)
    model = Model(place, r, images, dp_size, mp_size)
    reducer = Reducer(place, r, dp_size)
    weights = Gather(place, r.shard, r.full, (r.ga_a, r.ga_b, r.ga_c, r.ga_d), GATHER_PIECES)
    counts = Gather(place, r.counts, r.counts_all, (r.co_a, r.co_b, r.co_c, r.co_d), ((0, 1),))
    every = range(images)
    slots = list(range(reducer.slots))

    def each(stage, *rest):
        return [functools.partial(stage, image, *rest) for image in every]

    def own():
        r.full[place.dp] = r.shard[...]
        r.counts_all[place.dp] = r.counts[...]

    def do(function, *rest):
        return [functools.partial(function, *rest)]

    def pump(piece):
        weights.pump(piece)
        if piece + WINDOW < len(GATHER_PIECES):
            weights.start(piece + WINDOW)

    model.greet_all(pltpu.get_barrier_semaphore())
    def relay(name):
        return [functools.partial(model.relay, name, image) for image in every]

    schedule = do(model.pack)
    for piece in range(WINDOW):
        schedule += do(weights.start, piece)
    schedule += do(model.prepare) + do(counts.start, 0) + do(own) + do(model.setup)
    schedule += each(model.entry) + do(pump, 0) + do(counts.pump, 0) + do(pump, 1)
    schedule += do(weights.ready, 0) + do(model.time_in) + do(model.share_square, SQ0, r.w_in)
    schedule += do(pump, 2) + do(model.time_out) + do(model.relay, SQ0, 0) + each(model.res_wait)
    for i in range(3):
        schedule += do(weights.ready, 1 + i) + each(model.convolve, i) + do(pump, 3 + i)
    schedule += each(model.convolved) + do(model.spread_wait, X_NORMS, 0, r.norms_all, model.whole_slot)
    schedule += do(model.share_square_wait, SQ0, r.w_in) + do(weights.ready, 4)
    schedule += do(model.attention, 0) + do(pump, 6) + do(weights.ready, 5)
    schedule += do(model.share_square, SQ1, r.w_attn) + do(model.cross_first) + do(model.attention, 1)
    schedule += do(model.relay, SQ1, 0) + do(pump, 7) + do(weights.ready, 6) + do(model.share_ffout) + do(model.cross_second)
    schedule += do(model.share_square_wait, SQ1, r.w_attn) + do(pump, 8) + do(model.cross_last)
    schedule += each(model.feed)
    for k in range(4):
        schedule += do(weights.ready, 7 + k) + each(model.feed_part, k)
        schedule += do(pump, 9 + k) if k < 3 else []
    schedule += do(model.share_ffout_wait) + each(model.feed_out) + relay(X_FF)
    schedule += each(model.leave) + do(weights.ready, 11) + do(model.share_square, SQ4, r.w_out) + do(counts.ready, 0)
    schedule += each(model.finish) + do(model.predict) + do(model.relay, SQ4, 0)
    schedule += do(model.share_square_wait, SQ4, r.w_out) + do(model.loss) + each(model.back_last)
    schedule += do(model.grads_out) + do(reducer.start, 1) + each(model.back_feed) + relay(X_G_FF) + do(model.grads_ffin)
    schedule += do(reducer.start, 3) + each(model.back_cross) + do(model.cross_one)
    schedule += do(model.grads_ffout) + each(model.back_attention) + relay(X_G_AT) + do(reducer.pump, 2)
    schedule += do(model.cross_two) + do(model.grads_attn) + do(model.grads_qkv) + do(model.grads_ffout_wait) + do(reducer.start, 5)
    schedule += each(model.back_in) + do(model.cross_three) + do(reducer.start, 6) + do(reducer.pump, 4)
    schedule += each(model.back_conv) + relay(X_G_RES) + do(model.grads_in) + do(reducer.start, 7)
    schedule += do(model.grads_conv, 0) + do(reducer.start, 8) + do(model.back_time) + do(reducer.finish, 4)
    schedule += do(model.grads_conv, 1) + do(reducer.start, 9) + do(reducer.pump, 7) + do(model.back_time_in) + do(reducer.start, 10)
    schedule += do(model.grads_conv, 2) + do(reducer.start, 11) + do(reducer.share_ready) + do(reducer.pump, 8)
    schedule += do(model.back_first, 0) + do(reducer.pass_ready) + do(reducer.pump, 9) + do(model.back_first, 1)
    schedule += do(reducer.finish, 6) + do(reducer.root_ready) + do(reducer.pump, 11)
    schedule += do(model.cross_four) + do(reducer.small_start) + do(reducer.share_ready)
    schedule += do(reducer.finish, 11) + do(reducer.small_pump) + do(reducer.pass_ready) + do(reducer.share_ready)
    schedule += do(reducer.root_ready) + do(reducer.pass_ready) + do(reducer.small_finish) + do(reducer.root_ready)
    schedule += do(model.drain) + do(reducer.drain)
    for piece in range(len(GATHER_PIECES)):
        schedule += do(weights.drain, piece)
    schedule += do(counts.drain, 0)
    for action in schedule:
        action()


def train_step(images, dp_size, mp_size, scalars, arrays):
    vmem = pl.BlockSpec(memory_space=pltpu.VMEM)
    smem = pl.BlockSpec(memory_space=pltpu.SMEM)
    rows = arrays["w_square"].shape[1]
    f32, bf16 = jnp.float32, jnp.bfloat16
    slots = -(-len(ORDER) // dp_size)
    outs = dict(
        total=jax.ShapeDtypeStruct((SECTION_COUNT, rows, LANES), f32),
        grams=jax.ShapeDtypeStruct((dp_size, slots, LANES, LANES), bf16),
        roots=jax.ShapeDtypeStruct((len(ORDER), LANES, LANES), f32),
        small_sum=jax.ShapeDtypeStruct((SMALL_ROWS, LANES), f32),
        table_all=jax.ShapeDtypeStruct((dp_size, 1, 8, LANES), f32),
        counts_all=jax.ShapeDtypeStruct((dp_size, 1, 8, LANES), f32),
    )
    time_local = arrays["w_tin"].shape[1]
    hidden_local = arrays["w_fi"].shape[2]
    scratch = model_scratch(images, dp_size, mp_size, rows, time_local, hidden_local)
    scratch.update(reducer_scratch(dp_size, rows))
    names = list(scalars) + list(arrays) + list(outs) + list(scratch)
    return pl.pallas_call(
        functools.partial(step_kernel, images, dp_size, mp_size, names),
        out_shape=tuple(outs.values()),
        in_specs=[smem] * len(scalars) + [vmem] * len(arrays),
        out_specs=(vmem,) * len(outs),
        scratch_shapes=list(scratch.values()),
        compiler_params=pltpu.CompilerParams(
            collective_id=1, has_side_effects=True, vmem_limit_bytes=VMEM_LIMIT
        ),
        name="train_step",
    )(*scalars.values(), *arrays.values())


def adam(weight, mean, variance, gradient, rate):
    mean = beta_one * mean + (1 - beta_one) * gradient
    variance = beta_two * variance + (1 - beta_two) * gradient * gradient
    step = mean * (1.0 / (1 - beta_one**STEP)) / (jnp.sqrt(variance * (1.0 / (1 - beta_two**STEP))) + adam_eps)
    return weight - rate * (step + decay * weight), mean, variance


def update_kernel(images, dp_size, names, *refs):
    r = Refs()
    for name, ref in zip(names, refs):
        setattr(r, name, ref)
    rows = r.total.shape[1]
    parity = lax.rem(lax.broadcasted_iota(jnp.int32, (rows, LANES), 0), 2)
    where = {block: (position % dp_size, position // dp_size) for position, block in enumerate(ORDER)}
    for block in range(len(ORDER)):
        owner, slot = where[block]
        r.stats_new[block] = shampoo_beta * r.stats[block] + r.grams[owner, slot].astype(jnp.float32)

    def turned(moment, block):
        return exact(moment, r.roots[block])

    def renew(section, block, old, momentum):
        moment = shampoo_momentum * momentum + r.total[section]
        return old - shampoo_rate * (turned(moment, block) + decay * old), moment

    for k, name in enumerate(SQUARES):
        r.square_new[k], r.square_mom[k] = renew(STARTS[name], k, r.w_square[k], r.m_square[k])
    for k in range(9):
        r.conv_new[k], r.conv_mom[k] = renew(STARTS[CONV] + k, 5, r.w_conv[k], r.m_conv[k])
    for j in range(3):
        r.qkv_new[j], r.qkv_mom[j] = renew(STARTS[QKV] + j, 6 + j, r.w_qkv[j], r.m_qkv[j])
    for k in range(8):
        j, cut = k // 4, slice(k % 4 * LANES, (k % 4 + 1) * LANES)
        new, moment = renew(STARTS[FFIN] + 2 * (k % 4) + j, 9 + k, r.w_fi[:, j, cut], r.m_fi[:, j, cut])
        r.fi_new[:, j, cut] = new
        r.fi_mom[:, j, cut] = moment
    for k in range(4):
        cut = slice(k * rows, (k + 1) * rows)
        r.fo_new[cut], r.fo_mom[cut] = renew(STARTS[FFOUT] + k, 17, r.w_fo[cut], r.m_fo[cut])
    for k in range(2):
        cut = slice(k * rows, (k + 1) * rows)
        r.tout_new[cut], r.tout_mom[cut] = renew(STARTS[TOUT] + k, 20, r.w_tout[cut], r.m_tout[cut])
    halves = r.w_tin.shape[1] // LANES
    r.tin_rows[0] = r.total[STARTS[TIN]]
    for h in range(halves):
        cut = slice(h * LANES, (h + 1) * LANES)
        gradient = r.tin_rows[0, pl.ds(h, rows // halves, stride=halves)]
        moment = shampoo_momentum * r.m_tin[:, cut] + gradient
        r.tin_mom[:, cut] = moment
        old = r.w_tin[:, cut]
        r.tin_new[:, cut] = old - shampoo_rate * (turned(moment, 18 + h) + decay * old)
    for tap in range(9):
        r.first_grad[tap] = r.small_sum[8 * tap : 8 * tap + LAT]
        r.last_grad[tap] = r.small_sum[8 * tap + LAT : 8 * tap + 2 * LAT]
    r.first_new[...], r.first_mean_new[...], r.first_var_new[...] = adam(
        r.conv_first[...], r.first_mean[...], r.first_var[...], r.first_grad[...], rate_first
    )
    r.last_new[...], r.last_mean_new[...], r.last_var_new[...] = adam(
        r.conv_last[...], r.last_mean[...], r.last_var[...], r.last_grad[...], rate_last
    )
    for k in range(5):
        gradient = r.small_sum[72 + 2 * k : 74 + 2 * k]
        r.norm_new[k], r.norm_mean_new[k], r.norm_var_new[k] = adam(
            r.norms[k], r.norm_mean[k], r.norm_var[k], gradient, rate_gain
        )
    count = r.class_table.shape[0]
    row = lax.broadcasted_iota(jnp.int32, (count, LANES), 0).astype(jnp.float32)
    r.table_grad[...] = jnp.zeros((count, LANES), jnp.float32)

    def add(source):
        for image in range(images):
            label = r.table_all[source, 0, images + image : images + image + 1]
            gradient = r.table_all[source, 0, image : image + 1]
            r.table_grad[...] += jnp.where(row == label, gradient, 0.0)

    steps(0, dp_size, add)
    r.table_new[...], r.table_mean_new[...], r.table_var_new[...] = adam(
        r.class_table[...], r.table_mean[...], r.table_var[...], r.table_grad[...], rate_table
    )
    counts = jnp.sum(r.counts_all[...].reshape(dp_size, 8, LANES), axis=0)
    r.loss_terms[0:1] = r.small_sum[88:89, 0:NBANDS]
    r.loss_terms[1:2] = counts[0:1, 0:NBANDS]


def apply_update(images, dp_size, arrays, outs):
    vmem = pl.BlockSpec(memory_space=pltpu.VMEM)
    rows = arrays["total"].shape[1]
    scratch = dict(
        tin_rows=pltpu.VMEM((1, rows, LANES), jnp.float32),
        first_grad=pltpu.VMEM(arrays["conv_first"].shape, jnp.float32),
        last_grad=pltpu.VMEM(arrays["conv_first"].shape, jnp.float32),
        table_grad=pltpu.VMEM(arrays["class_table"].shape, jnp.float32),
    )
    names = list(arrays) + list(outs) + list(scratch)
    return pl.pallas_call(
        functools.partial(update_kernel, images, dp_size, names),
        out_shape=tuple(outs.values()),
        in_specs=[vmem] * len(arrays),
        out_specs=(vmem,) * len(outs),
        scratch_shapes=list(scratch.values()),
        compiler_params=pltpu.CompilerParams(vmem_limit_bytes=VMEM_LIMIT),
        name="apply_update",
    )(*arrays.values())


def local(
    clean_latent,
    noise_latent,
    timesteps,
    labels,
    image_sides,
    w_square,
    mom_square,
    w_conv,
    mom_conv,
    w_qkv,
    mom_qkv,
    w_ffin,
    mom_ffin,
    w_ffout,
    mom_ffout,
    w_time_in,
    mom_time_in,
    w_time_out,
    mom_time_out,
    kron_stats,
    class_table,
    table_mean,
    table_var,
    conv_first,
    first_mean,
    first_var,
    conv_last,
    last_mean,
    last_var,
    norm_params,
    norm_mean,
    norm_var,
):
    dp_size = lax.axis_size(DP)
    mp_size = lax.axis_size(MP)
    images = clean_latent.shape[0]
    weights = dict(
        w_square=w_square, w_conv=w_conv, w_qkv=w_qkv.transpose(1, 0, 2), w_fi=w_ffin, w_fo=w_ffout, w_tin=w_time_in, w_tout=w_time_out
    )
    total, grams, roots, small, table_all, counts_all = train_step(
        images,
        dp_size,
        mp_size,
        dict(timesteps=timesteps, labels=labels, sides=image_sides),
        dict(
            latent=clean_latent.transpose(1, 0, 2),
            noise=noise_latent.transpose(1, 0, 2),
            class_table=class_table,
            norms=norm_params,
            conv_first=conv_first,
            conv_last=conv_last.transpose(0, 2, 1),
            stats=kron_stats,
            **weights,
        ),
    )

    def like(array):
        return jax.ShapeDtypeStruct(array.shape, jnp.float32)

    results = apply_update(
        images,
        dp_size,
        dict(
            total=total, grams=grams, roots=roots, small_sum=small, table_all=table_all, counts_all=counts_all, stats=kron_stats,
            m_square=mom_square, m_conv=mom_conv, m_qkv=mom_qkv.transpose(1, 0, 2), m_fi=mom_ffin, m_fo=mom_ffout, m_tin=mom_time_in, m_tout=mom_time_out,
            class_table=class_table, table_mean=table_mean, table_var=table_var,
            conv_first=conv_first, first_mean=first_mean, first_var=first_var,
            conv_last=conv_last.transpose(0, 2, 1), last_mean=last_mean.transpose(0, 2, 1), last_var=last_var.transpose(0, 2, 1),
            norms=norm_params, norm_mean=norm_mean, norm_var=norm_var,
            **weights,
        ),
        dict(
            square_new=like(w_square), square_mom=like(w_square), conv_new=like(w_conv), conv_mom=like(w_conv),
            qkv_new=like(weights["w_qkv"]), qkv_mom=like(weights["w_qkv"]), fi_new=like(w_ffin), fi_mom=like(w_ffin),
            fo_new=like(w_ffout), fo_mom=like(w_ffout), tin_new=like(w_time_in), tin_mom=like(w_time_in),
            tout_new=like(w_time_out), tout_mom=like(w_time_out), stats_new=like(kron_stats),
            table_new=like(class_table), table_mean_new=like(class_table), table_var_new=like(class_table),
            first_new=like(conv_first), first_mean_new=like(conv_first), first_var_new=like(conv_first),
            last_new=like(conv_first), last_mean_new=like(conv_first), last_var_new=like(conv_first),
            norm_new=like(norm_params), norm_mean_new=like(norm_params), norm_var_new=like(norm_params),
            loss_terms=jax.ShapeDtypeStruct((2, NBANDS), jnp.float32),
        ),
    )
    qkv_out = tuple(array.transpose(1, 0, 2) for array in results[4:6])
    last_out = tuple(array.transpose(0, 2, 1) for array in results[21:24])
    return results[:4] + qkv_out + results[6:21] + last_out + results[24:]


def solution(mesh):
    return jax.shard_map(
        local,
        mesh=mesh,
        in_specs=(
            P(DP, None, None),
            P(DP, None, None),
            P(DP),
            P(DP),
            P(DP),
            P(None, DP, MP),
            P(None, DP, MP),
            P(None, DP, MP),
            P(None, DP, MP),
            P(DP, None, MP),
            P(DP, None, MP),
            P(DP, None, MP),
            P(DP, None, MP),
            P(DP, MP),
            P(DP, MP),
            P(DP, MP),
            P(DP, MP),
            P(DP, MP),
            P(DP, MP),
            P(MP, None, None),
            P(None, MP),
            P(None, MP),
            P(None, MP),
            P(None, None, MP),
            P(None, None, MP),
            P(None, None, MP),
            P(None, MP, None),
            P(None, MP, None),
            P(None, MP, None),
            P(None, None, MP),
            P(None, None, MP),
            P(None, None, MP),
        ),
        out_specs=(
            P(None, DP, MP),
            P(None, DP, MP),
            P(None, DP, MP),
            P(None, DP, MP),
            P(DP, None, MP),
            P(DP, None, MP),
            P(DP, None, MP),
            P(DP, None, MP),
            P(DP, MP),
            P(DP, MP),
            P(DP, MP),
            P(DP, MP),
            P(DP, MP),
            P(DP, MP),
            P(MP, None, None),
            P(None, MP),
            P(None, MP),
            P(None, MP),
            P(None, None, MP),
            P(None, None, MP),
            P(None, None, MP),
            P(None, MP, None),
            P(None, MP, None),
            P(None, MP, None),
            P(None, None, MP),
            P(None, None, MP),
            P(None, None, MP),
            P(),
        ),
        check_vma=False,
    )
```
